32 devices in a mesh: ctx: 8 (over z, y), head: 4 (over x, core).
Axes of the slice: x: 2, y: 2, z: 4, core: 2. Of those that a mesh axis runs over, the one named last changes fastest.
Arguments:
- query: bfloat16 [4096, 1024], P(('ctx', 'head')), may hold values from -7 to 7
- key: bfloat16 [4096, 1024], P(('ctx', 'head')), may hold values from -7 to 7
- value: bfloat16 [4096, 1024], P(('ctx', 'head')), may hold values from -6 to 6
- grad_out: bfloat16 [4096, 1024], P(('ctx', 'head')), may hold values from -6 to 6
- neighbour: int32 [32, 8], replicated, may hold values from 0 to 31, as said below
- counts: int32 [32], replicated, may hold values from 1 to 8, as said below
Outputs:
- attn_out: bfloat16 [4096, 1024], P(('ctx', 'head'))
- grad_query: bfloat16 [4096, 1024], P(('ctx', 'head'))
- grad_key: bfloat16 [4096, 1024], P(('ctx', 'head'))
- grad_value: bfloat16 [4096, 1024], P(('ctx', 'head'))
The draws below stay inside these ranges and needn't reach their ends.
Inputs may be any that keep to these rules, and one draw needn't show every extreme that they name: `neighbour`: row b lists key blocks for query block b: its first entry is b itself, and every entry lies within 8 blocks of b in the periodic block order; some row has an entry exactly 8 blocks ahead, and some row one exactly that far behind. Query block b uses the first counts[b] slots of its row; some block uses all 8 slots and some only one.
All inputs are finite; a program needn't handle non-finite values.
Results may differ from the reference program's by a relative error of at most 0.0083.
Values may be sent and summed in bfloat16 or wider, within the bound.
A program may use at most 64 MiB of HBM per device.

```python
import math
import jax
import jax.numpy as jnp
from jax import lax

H = 16
E = 64
D = 1024
BLK = 128
NNB = 8
REACH = 2
SEQ = 4096
BPS = 4
NB = 32
N_CTX = 8


def paired_fields(key):
    base = jax.random.fold_in(key, 11)
    first_key, second_key = jax.random.split(base, 2)
    first = jax.random.truncated_normal(first_key, -4.0, 4.0, (SEQ, D), jnp.float32)
    second = jax.random.truncated_normal(second_key, -4.0, 4.0, (SEQ, D), jnp.float32)
    return (first, second)


def draw_query(key, part):
    return paired_fields(key)[0].astype(jnp.bfloat16)


def draw_key(key, part):
    return paired_fields(key)[1].astype(jnp.bfloat16)


def draw_neighbour(key, part):
    offset_key, pick_key = jax.random.split(jax.random.fold_in(key, 23), 2)
    span = REACH * BPS
    offsets = jax.random.randint(offset_key, (NB, NNB), -span, span + 1, jnp.int32)
    offsets = offsets.at[:, 0].set(0)
    chosen = jax.random.randint(pick_key, (), 0, NB, jnp.int32)
    offsets = offsets.at[chosen, 1].set(span)
    offsets = offsets.at[(chosen + 1) % NB, 1].set(-span)
    rows = jnp.arange(NB, dtype=jnp.int32)[:, None]
    return jnp.mod(rows + offsets, NB).astype(jnp.int32)


def draw_counts(key, part):
    count_key, pick_key = jax.random.split(jax.random.fold_in(key, 37), 2)
    drawn = jax.random.randint(count_key, (NB,), 1, NNB + 1, jnp.int32)
    chosen = jax.random.randint(pick_key, (), 0, NB, jnp.int32)
    drawn = drawn.at[chosen].set(NNB)
    drawn = drawn.at[(chosen + 1) % NB].set(1)
    return drawn.astype(jnp.int32)


def steps_of(stream_key, extent, pieces, smallest, top_value):
    factor_of = 1.0
    for dim, shards_of in pieces:
        steps = jax.random.uniform(jax.random.fold_in(jax.random.fold_in(stream_key, 6), dim), (shards_of,), jnp.float32, smallest / len(pieces), top_value / len(pieces))
        factor_of = factor_of * jnp.repeat(jnp.exp(steps), extent[dim] // shards_of).reshape((-1,) + (1,) * (len(extent) - 1 - dim))
    return factor_of


def gaussian(rng, shape, spread, most, cuts=(), kind=jnp.bfloat16):
    values = jax.random.normal(rng, shape, jnp.float32) * spread
    if len(cuts) > 0:
        values = steps_of(rng, shape, cuts, -0.22, 0.18) * values
    return jnp.clip(values, min=-most, max=most).astype(kind)


def setup_inputs(seed: int = 0) -> dict:
    streams_of = jax.random.split(jax.random.key(seed), 7)
    return {
        "query": draw_query(jax.random.fold_in(streams_of[6], 71), 0),
        "key": draw_key(jax.random.fold_in(streams_of[6], 71), 0),
        "value": gaussian(streams_of[2], (SEQ, D), 1.0, 6.0, ((0, 32),)),
        "grad_out": gaussian(streams_of[3], (SEQ, D), 1.0, 6.0, ((0, 32),)),
        "neighbour": draw_neighbour(jax.random.fold_in(streams_of[6], 71), 0),
        "counts": draw_counts(jax.random.fold_in(streams_of[6], 71), 0),
    }


def attend_blocks(queries, cotangent, keys_sel, values_sel, usable):
    scale_factor = 1.0 / math.sqrt(queries.shape[-1])
    query_f = queries.astype(jnp.float32)
    grad_f = cotangent.astype(jnp.float32)
    key_f = keys_sel.astype(jnp.float32)
    value_f = values_sel.astype(jnp.float32)
    scores = jnp.einsum('rie,rjte->rijt', query_f, key_f) * scale_factor
    allowed = usable[:, None, :, None]
    masked = jnp.where(allowed, scores, -1e+30)
    highest = lax.optimization_barrier(jnp.max(masked, axis=(2, 3), keepdims=True))
    raised = jnp.where(allowed, jnp.exp(masked - highest), 0.0)
    total = lax.optimization_barrier(jnp.sum(raised, axis=(2, 3), keepdims=True))
    probability = raised / total
    weights = probability.astype(jnp.bfloat16)
    weights_f = weights.astype(jnp.float32)
    out_rows = jnp.einsum('rijt,rjte->rie', weights_f, value_f).astype(jnp.bfloat16)
    dprob = jnp.einsum('rie,rjte->rijt', grad_f, value_f)
    row_delta = lax.optimization_barrier(jnp.sum(probability * dprob, axis=(2, 3), keepdims=True))
    dscore = (probability * (dprob - row_delta) * scale_factor).astype(jnp.bfloat16)
    dscore_f = dscore.astype(jnp.float32)
    dquery = jnp.einsum('rijt,rjte->rie', dscore_f, key_f).astype(jnp.bfloat16)
    dkey_part = jnp.einsum('rijt,rie->rjte', dscore_f, query_f)
    dvalue_part = jnp.einsum('rijt,rie->rjte', weights_f, grad_f)
    return (out_rows, dquery, dkey_part, dvalue_part)

def split_heads(array, seq_len):
    return array.reshape(seq_len, H, E).transpose(1, 0, 2)

def join_heads(array, seq_len):
    return array.transpose(1, 0, 2).reshape(seq_len, H * E)

def reference(query, key, value, grad_out, neighbour, counts):
    seq_len = query.shape[0]

    def per_head(stacked):
        query_h, key_h, value_h, grad_h = stacked
        key_blocks = key_h.reshape(NB, BLK, E)
        value_blocks = value_h.reshape(NB, BLK, E)

        def per_shard(totals, inputs):
            query_g, grad_g, chosen, used = inputs
            usable = jnp.arange(NNB)[None, :] < used[:, None]
            out_g, dq_g, dk_part, dv_part = attend_blocks(query_g, grad_g, key_blocks[chosen], value_blocks[chosen], usable)
            flat = chosen.reshape(-1)
            key_total = totals[0].at[flat].add(dk_part.reshape(-1, BLK, E))
            value_total = totals[1].at[flat].add(dv_part.reshape(-1, BLK, E))
            return ((key_total, value_total), (out_g, dq_g))
        zeros_init = jnp.zeros((NB, BLK, E), jnp.float32)
        inputs = (query_h.reshape(N_CTX, BPS, BLK, E), grad_h.reshape(N_CTX, BPS, BLK, E), neighbour.reshape(N_CTX, BPS, NNB).astype(jnp.int32), counts.reshape(N_CTX, BPS).astype(jnp.int32))
        totals, results = lax.scan(per_shard, (zeros_init, zeros_init), inputs)
        return (results[0].reshape(seq_len, E), results[1].reshape(seq_len, E), totals[0].astype(jnp.bfloat16).reshape(seq_len, E), totals[1].astype(jnp.bfloat16).reshape(seq_len, E))
    results = lax.map(per_head, (split_heads(query, seq_len), split_heads(key, seq_len), split_heads(value, seq_len), split_heads(grad_out, seq_len)))
    return (join_heads(results[0], seq_len), join_heads(results[1], seq_len), join_heads(results[2], seq_len), join_heads(results[3], seq_len))
```

```python
import functools
import math

import jax
import jax.numpy as jnp
from jax import lax
from jax.experimental import pallas as pl
from jax.experimental.pallas import tpu as pltpu
from jax.sharding import PartitionSpec as P

H = 16
E = 64
BLK = 128
NNB = 8
REACH = 2


def passed_along(value, axis, steps):
    count = lax.axis_size(axis)
    pairs = [(source, (source + steps) % count) for source in range(count)]
    return lax.ppermute(value, axis, pairs)


def group_rows(blocks_shard, block_len):
    limit = max(512 // block_len, 1)
    best = 1
    for candidate in range(1, blocks_shard + 1):
        if blocks_shard % candidate == 0 and candidate <= limit:
            best = candidate
    return best


def on_device_windowed(query, key, value, grad_out, neighbour, counts):
    tok_rows = query.shape[0]
    groups = lax.axis_size("head")
    per_dev = H // groups
    head_cols = per_dev * E
    moved = (
        lax.all_to_all(
            query.reshape(tok_rows, groups, head_cols),
            "head",
            split_axis=1,
            concat_axis=0,
            tiled=True,
        ),
        lax.all_to_all(
            key.reshape(tok_rows, groups, head_cols),
            "head",
            split_axis=1,
            concat_axis=0,
            tiled=True,
        ),
        lax.all_to_all(
            value.reshape(tok_rows, groups, head_cols),
            "head",
            split_axis=1,
            concat_axis=0,
            tiled=True,
        ),
        lax.all_to_all(
            grad_out.reshape(tok_rows, groups, head_cols),
            "head",
            split_axis=1,
            concat_axis=0,
            tiled=True,
        ),
    )
    shard_rows = groups * tok_rows
    query_s = moved[0].reshape(shard_rows, head_cols)
    key_s = moved[1].reshape(shard_rows, head_cols)
    value_s = moved[2].reshape(shard_rows, head_cols)
    grad_s = moved[3].reshape(shard_rows, head_cols)
    paired = jnp.concatenate([key_s, value_s], axis=1)
    cycle_len = lax.axis_size("ctx")
    position = lax.axis_index("ctx")
    blocks_shard = shard_rows // BLK
    all_blocks = blocks_shard * cycle_len
    fetched = {}
    offsets_all = list(range(1, REACH + 1)) + [-offset for offset in range(1, REACH + 1)]
    for offset in offsets_all:
        fetched[offset] = passed_along(paired, "ctx", offset)
    ordered = (
        [fetched[REACH - place] for place in range(REACH)]
        + [paired]
        + [fetched[-(place + 1)] for place in range(REACH)]
    )
    span_shards = 2 * REACH + 1
    window = jnp.concatenate(ordered, axis=0).reshape(
        span_shards * blocks_shard, BLK, 2 * head_cols
    )
    rows_nbr = lax.dynamic_slice_in_dim(neighbour, position * blocks_shard, blocks_shard, 0)
    local_idx = jnp.mod(rows_nbr - (position - REACH) * blocks_shard, all_blocks)
    used = lax.dynamic_slice_in_dim(counts, position * blocks_shard, blocks_shard, 0)
    per_group = group_rows(blocks_shard, BLK)
    turns = blocks_shard // per_group
    scale_factor = 1.0 / math.sqrt(E)
    query_g = query_s.reshape(turns, per_group, BLK, per_dev, E)
    grad_g = grad_s.reshape(turns, per_group, BLK, per_dev, E)
    index_g = local_idx.reshape(turns, per_group, NNB)
    used_g = used.reshape(turns, per_group)

    def one_group(totals, inputs):
        queries, cotangent, chosen, used_now = inputs
        selected = window[chosen]
        keys_sel = selected[..., :head_cols].reshape(per_group, NNB, BLK, per_dev, E)
        values_sel = selected[..., head_cols:].reshape(per_group, NNB, BLK, per_dev, E)
        usable = jnp.arange(NNB)[None, :] < used_now[:, None]
        allowed = usable[:, None, None, :, None]
        scores = (
            jnp.einsum("rihe,rjthe->rhijt", queries, keys_sel, preferred_element_type=jnp.float32)
            * scale_factor
        )
        masked = jnp.where(allowed, scores, -1e30)
        highest = jnp.max(masked, axis=(3, 4), keepdims=True)
        raised = jnp.where(allowed, jnp.exp(masked - highest), 0.0)
        total = jnp.sum(raised, axis=(3, 4), keepdims=True)
        probability = raised / total
        weights = probability.astype(jnp.bfloat16)
        out_rows = jnp.einsum(
            "rhijt,rjthe->rihe", weights, values_sel, preferred_element_type=jnp.float32
        ).astype(jnp.bfloat16)
        dprob = jnp.einsum(
            "rihe,rjthe->rhijt", cotangent, values_sel, preferred_element_type=jnp.float32
        )
        row_delta = jnp.sum(probability * dprob, axis=(3, 4), keepdims=True)
        dscore = (probability * (dprob - row_delta) * scale_factor).astype(jnp.bfloat16)
        dquery = jnp.einsum(
            "rhijt,rjthe->rihe", dscore, keys_sel, preferred_element_type=jnp.float32
        ).astype(jnp.bfloat16)
        dkey_part = jnp.einsum(
            "rhijt,rihe->rjthe", dscore, queries, preferred_element_type=jnp.float32
        )
        dvalue_part = jnp.einsum(
            "rhijt,rihe->rjthe", weights, cotangent, preferred_element_type=jnp.float32
        )
        joined = jnp.concatenate(
            [
                dkey_part.reshape(per_group * NNB, BLK, head_cols),
                dvalue_part.reshape(per_group * NNB, BLK, head_cols),
            ],
            axis=-1,
        )
        totals = totals.at[chosen.reshape(-1)].add(joined)
        return (totals, (out_rows, dquery))

    start_grads = jnp.zeros((span_shards * blocks_shard, BLK, 2 * head_cols), jnp.float32)
    grads_window, results = lax.scan(one_group, start_grads, (query_g, grad_g, index_g, used_g))
    grads_window = grads_window.reshape(span_shards, shard_rows, 2 * head_cols)
    combined = grads_window[REACH]
    offsets_back = list(range(1, REACH + 1)) + [-offset for offset in range(1, REACH + 1)]
    for offset in offsets_back:
        combined = combined + passed_along(
            grads_window[REACH - offset].astype(jnp.bfloat16), "ctx", -offset
        ).astype(jnp.float32)
    combined = combined.astype(jnp.bfloat16)
    dkey_s = combined[:, :head_cols]
    dvalue_s = combined[:, head_cols:]
    out_s = results[0].reshape(shard_rows, head_cols)
    dquery_s = results[1].reshape(shard_rows, head_cols)
    back = (
        lax.all_to_all(
            out_s.reshape(shard_rows, 1, head_cols), "head", split_axis=0, concat_axis=1, tiled=True
        ),
        lax.all_to_all(
            dquery_s.reshape(shard_rows, 1, head_cols),
            "head",
            split_axis=0,
            concat_axis=1,
            tiled=True,
        ),
        lax.all_to_all(
            dkey_s.reshape(shard_rows, 1, head_cols),
            "head",
            split_axis=0,
            concat_axis=1,
            tiled=True,
        ),
        lax.all_to_all(
            dvalue_s.reshape(shard_rows, 1, head_cols),
            "head",
            split_axis=0,
            concat_axis=1,
            tiled=True,
        ),
    )
    width = groups * head_cols
    return (
        back[0].reshape(tok_rows, width),
        back[1].reshape(tok_rows, width),
        back[2].reshape(tok_rows, width),
        back[3].reshape(tok_rows, width),
    )


MESH_ID = pl.DeviceIdType.MESH
F32 = jnp.float32
BF16 = jnp.bfloat16
VMEM_BYTES = 40 * 1024 * 1024


def place_of():
    index = lax.axis_index("ctx") * lax.axis_size("head") + lax.axis_index("head")
    return lax.div(index, 2), lax.rem(index, 2)


def device_of(owner, side):
    n_head = lax.axis_size("head")
    index = 2 * owner + side
    return (lax.div(index, n_head), lax.rem(index, n_head))


def greet(pairs):
    owner, side = place_of()
    barrier = pltpu.get_barrier_semaphore()
    pl.semaphore_signal(barrier, inc=1, device_id=device_of(owner, 1 - side), device_id_type=MESH_ID)

    def one(step, carry):
        other = lax.rem(owner + step, pairs)
        pl.semaphore_signal(barrier, inc=1, device_id=device_of(other, side), device_id_type=MESH_ID)
        return carry

    lax.fori_loop(1, pairs, one, 0)
    return barrier


def spread_kernel(
    pairs, query, key, value, grad_out, qd, kv, send_qd, send_kv,
    qd_out, qd_in, kv_out, kv_in, share_out, share_in,
):
    owner, side = place_of()
    barrier = greet(pairs)
    for left, right, pieces in ((key, value, send_kv), (query, grad_out, send_qd)):
        for pair in range(pairs // 2):
            cols = slice(2 * E * pair, 2 * E * (pair + 1))
            a = left[:, cols]
            b = right[:, cols]
            pieces[2 * pair] = jnp.concatenate([a[:, :E], b[:, :E]], axis=1)
            pieces[2 * pair + 1] = jnp.concatenate([a[:, E:], b[:, E:]], axis=1)
    pl.semaphore_wait(barrier, pairs)

    def kv_copy(step, to, source):
        return pltpu.make_async_remote_copy(
            src_ref=send_kv.at[to],
            dst_ref=kv.at[2 * source + side],
            send_sem=kv_out.at[step],
            recv_sem=kv_in.at[step],
            device_id=device_of(to, side),
            device_id_type=MESH_ID,
        )

    def qd_copy(step, to, source):
        return pltpu.make_async_remote_copy(
            src_ref=send_qd.at[to],
            dst_ref=qd.at[source],
            send_sem=qd_out.at[step],
            recv_sem=qd_in.at[step],
            device_id=device_of(to, side),
            device_id_type=MESH_ID,
        )

    def share_copy(step, source, whose):
        return pltpu.make_async_remote_copy(
            src_ref=kv.at[2 * source + side],
            dst_ref=kv.at[2 * source + whose],
            send_sem=share_out.at[step],
            recv_sem=share_in.at[step],
            device_id=device_of(owner, 1 - side),
            device_id_type=MESH_ID,
        )

    def send_keys(step, carry):
        kv_copy(step, lax.rem(owner + step, pairs), owner).start()
        return carry

    def send_queries(step, carry):
        qd_copy(step, lax.rem(owner + step, pairs), owner).start()
        return carry

    lax.fori_loop(1, pairs, send_keys, 0)
    lax.fori_loop(1, pairs, send_queries, 0)
    kv[2 * owner + side] = send_kv[owner]
    qd[owner] = send_qd[owner]
    share_copy(0, owner, side).start()

    def pass_on(step, carry):
        source = lax.rem(owner - step + pairs, pairs)
        kv_copy(step, owner, source).wait_recv()
        share_copy(step, source, side).start()
        return carry

    lax.fori_loop(1, pairs, pass_on, 0)

    def finish(step, carry):
        source = lax.rem(owner - step + pairs, pairs)
        to = lax.rem(owner + step, pairs)
        qd_copy(step, owner, source).wait_recv()
        qd_copy(step, to, owner).wait_send()
        kv_copy(step, to, owner).wait_send()
        return carry

    lax.fori_loop(1, pairs, finish, 0)

    def finish_share(step, carry):
        source = lax.rem(owner - step + pairs, pairs)
        share_copy(step, source, side).wait_send()
        share_copy(step, source, 1 - side).wait_recv()
        return carry

    lax.fori_loop(0, pairs, finish_share, 0)


def attend_kernel(
    blocks, neighbour, counts, qd, kv, od, own, other, kvt, totals, pair_scr, x_scr
):
    _, side = place_of()
    half = blocks // 2
    scale = 1.0 / math.sqrt(E)
    exp_scale = scale * math.log2(math.e)
    low = lax.broadcasted_iota(jnp.int32, (BLK, 2 * E), 1) < E
    top = lax.broadcasted_iota(jnp.int32, (2 * E, BLK), 0) < E

    def prepare(block, carry):
        kvt[block] = kv[block].T
        totals[block] = jnp.zeros((BLK, 2 * E), F32)
        return carry

    lax.fori_loop(0, blocks, prepare, 0)

    def folded(array, op):
        return op(array.reshape(BLK // 8, 8, BLK), axis=0)

    def rows_with(place, block, used):
        both = qd[place]
        zero = jnp.zeros_like(both)
        spread = jnp.concatenate([jnp.where(low, both, zero), jnp.where(low, zero, both)], axis=0)
        names = [neighbour[block, slot] for slot in range(used)]
        highest = None
        for slot in range(used):
            result = lax.dot_general(
                kv[names[slot]], spread, (((1,), (1,)), ((), ())), preferred_element_type=F32
            )
            pair_scr[slot] = result
            part = folded(result[:, :BLK], jnp.max)
            highest = part if highest is None else jnp.maximum(highest, part)
        highest = jnp.max(highest, axis=0, keepdims=True)
        total = jnp.zeros((8, BLK), F32)
        delta = jnp.zeros((8, BLK), F32)
        for slot in range(used):
            raised = jnp.exp2((pair_scr[slot, :, :BLK] - highest) * exp_scale)
            pair_scr[slot, :, :BLK] = raised
            total = total + folded(raised, jnp.sum)
            delta = delta + folded(raised * pair_scr[slot, :, BLK:], jnp.sum)
        inverse = 1.0 / jnp.sum(total, axis=0, keepdims=True)
        delta = jnp.sum(delta, axis=0, keepdims=True) * inverse
        for slot in range(used):
            probability = pair_scr[slot, :, :BLK] * inverse
            dscore = (probability * scale) * (pair_scr[slot, :, BLK:] - delta)
            x_scr[slot] = jnp.concatenate(
                [dscore.astype(BF16), probability.astype(BF16)], axis=1
            )
        rows = jnp.zeros((2 * E, 2 * BLK), F32)
        for slot in range(0, used, 2):
            if slot + 1 < used:
                keys_t = jnp.concatenate([kvt[names[slot]], kvt[names[slot + 1]]], axis=1)
                grads = jnp.concatenate([x_scr[slot], x_scr[slot + 1]], axis=0)
            else:
                keys_t = kvt[names[slot]]
                grads = x_scr[slot]
            rows = rows + jnp.dot(keys_t, grads, preferred_element_type=F32)
        for slot in range(used):
            totals[names[slot]] += jnp.dot(x_scr[slot], spread, preferred_element_type=F32)
        od[place] = jnp.where(top, rows[:, :BLK], rows[:, BLK:]).T.astype(BF16)

    def one_block(place, carry):
        block = 2 * place + side
        used_now = counts[block]
        for used in range(1, NNB + 1):
            pl.when(used_now == used)(functools.partial(rows_with, place, block, used))
        return carry

    lax.fori_loop(0, half, one_block, 0)

    def hand_over(place, carry):
        own[place] = totals[2 * place + side]
        other[place] = totals[2 * place + 1 - side].astype(BF16)
        return carry

    lax.fori_loop(0, half, hand_over, 0)


def collect_kernel(
    pairs, od, own, other, out, dquery, dkey, dvalue, shared, send_kv, got_od, got_kv,
    od_out, od_in, kv_out, kv_in, share_out, share_in,
):
    owner, side = place_of()
    barrier = greet(pairs)
    pl.semaphore_wait(barrier, pairs)

    def share_copy(step, place):
        return pltpu.make_async_remote_copy(
            src_ref=other.at[place],
            dst_ref=shared.at[place],
            send_sem=share_out.at[step],
            recv_sem=share_in.at[step],
            device_id=device_of(owner, 1 - side),
            device_id_type=MESH_ID,
        )

    def od_copy(step, to, source):
        return pltpu.make_async_remote_copy(
            src_ref=od.at[to],
            dst_ref=got_od.at[source],
            send_sem=od_out.at[step],
            recv_sem=od_in.at[step],
            device_id=device_of(to, side),
            device_id_type=MESH_ID,
        )

    def kv_copy(step, to, source):
        return pltpu.make_async_remote_copy(
            src_ref=send_kv.at[to],
            dst_ref=got_kv.at[source],
            send_sem=kv_out.at[step],
            recv_sem=kv_in.at[step],
            device_id=device_of(to, side),
            device_id_type=MESH_ID,
        )

    def start_all(step, carry):
        to = lax.rem(owner + step, pairs)
        share_copy(step, to).start()
        od_copy(step, to, owner).start()
        return carry

    lax.fori_loop(1, pairs, start_all, 0)
    share_copy(0, owner).start()

    def add_and_send(step, carry):
        to = lax.rem(owner + step, pairs)
        share_copy(step, to).wait_recv()
        send_kv[to] = (own[to] + shared[to].astype(F32)).astype(BF16)
        kv_copy(step, to, owner).start()
        return carry

    lax.fori_loop(1, pairs, add_and_send, 0)
    share_copy(0, owner).wait_recv()
    got_kv[owner] = (own[owner] + shared[owner].astype(F32)).astype(BF16)
    got_od[owner] = od[owner]

    def finish(step, carry):
        source = lax.rem(owner - step + pairs, pairs)
        to = lax.rem(owner + step, pairs)
        od_copy(step, owner, source).wait_recv()
        kv_copy(step, owner, source).wait_recv()
        od_copy(step, to, owner).wait_send()
        kv_copy(step, to, owner).wait_send()
        share_copy(step, to).wait_send()
        return carry

    lax.fori_loop(1, pairs, finish, 0)
    share_copy(0, owner).wait_send()
    for first, second, pieces in ((dquery, out, got_od), (dkey, dvalue, got_kv)):
        for pair in range(pairs // 2):
            cols = slice(2 * E * pair, 2 * E * (pair + 1))
            a = pieces[2 * pair]
            b = pieces[2 * pair + 1]
            first[:, cols] = jnp.concatenate([a[:, :E], b[:, :E]], axis=1)
            second[:, cols] = jnp.concatenate([a[:, E:], b[:, E:]], axis=1)


def on_device_whole(query, key, value, grad_out, neighbour, counts):
    pairs = lax.axis_size("ctx") * lax.axis_size("head") // 2
    blocks = 2 * pairs
    width = query.shape[1]
    in_vmem = pl.BlockSpec(memory_space=pltpu.VMEM)
    in_smem = pl.BlockSpec(memory_space=pltpu.SMEM)
    many = pltpu.SemaphoreType.DMA((pairs,))
    piece = (BLK, 2 * E)
    with jax.named_scope("spread_heads"):
        qd, kv = pl.pallas_call(
            functools.partial(spread_kernel, pairs),
            out_shape=(
                jax.ShapeDtypeStruct((pairs, *piece), BF16),
                jax.ShapeDtypeStruct((blocks, *piece), BF16),
            ),
            in_specs=[in_vmem] * 4,
            out_specs=(in_vmem, in_vmem),
            scratch_shapes=[pltpu.VMEM((pairs, *piece), BF16)] * 2 + [many] * 6,
            compiler_params=pltpu.CompilerParams(
                collective_id=0, has_side_effects=True, vmem_limit_bytes=VMEM_BYTES
            ),
        )(query, key, value, grad_out)
    with jax.named_scope("block_attention"):
        od, own, other = pl.pallas_call(
            functools.partial(attend_kernel, blocks),
            out_shape=(
                jax.ShapeDtypeStruct((pairs, *piece), BF16),
                jax.ShapeDtypeStruct((pairs, *piece), F32),
                jax.ShapeDtypeStruct((pairs, *piece), BF16),
            ),
            in_specs=[in_smem] * 2 + [in_vmem] * 2,
            out_specs=(in_vmem,) * 3,
            scratch_shapes=[
                pltpu.VMEM((blocks, 2 * E, BLK), BF16),
                pltpu.VMEM((blocks, *piece), F32),
                pltpu.VMEM((NNB, BLK, 2 * BLK), F32),
                pltpu.VMEM((NNB, BLK, 2 * BLK), BF16),
            ],
            compiler_params=pltpu.CompilerParams(vmem_limit_bytes=VMEM_BYTES),
        )(neighbour, counts, qd, kv)
    with jax.named_scope("collect_heads"):
        whole = jax.ShapeDtypeStruct((BLK, width), BF16)
        return pl.pallas_call(
            functools.partial(collect_kernel, pairs),
            out_shape=(whole,) * 4,
            in_specs=[in_vmem] * 3,
            out_specs=(in_vmem,) * 4,
            scratch_shapes=[pltpu.VMEM((pairs, *piece), BF16)] * 4 + [many] * 6,
            compiler_params=pltpu.CompilerParams(
                collective_id=1, has_side_effects=True, vmem_limit_bytes=VMEM_BYTES
            ),
        )(od, own, other)


def on_device(query, key, value, grad_out, neighbour, counts):
    devices = lax.axis_size("ctx") * lax.axis_size("head")
    if devices == 2 * H and query.shape == (BLK, H * E) and counts.shape[0] == devices:
        return on_device_whole(query, key, value, grad_out, neighbour, counts)
    return on_device_windowed(query, key, value, grad_out, neighbour, counts)


def solution(mesh):
    return jax.shard_map(
        on_device,
        mesh=mesh,
        in_specs=(
            P(("ctx", "head"), None),
            P(("ctx", "head"), None),
            P(("ctx", "head"), None),
            P(("ctx", "head"), None),
            P(),
            P(),
        ),
        out_specs=(
            P(("ctx", "head"), None),
            P(("ctx", "head"), None),
            P(("ctx", "head"), None),
            P(("ctx", "head"), None),
        ),
        check_vma=False,
    )
```

```python
import functools
import math

import jax
import jax.numpy as jnp
from jax import lax
from jax.experimental import pallas as pl
from jax.experimental.pallas import tpu as pltpu
from jax.sharding import PartitionSpec as P

H = 16
E = 64
BLK = 128
NNB = 8
REACH = 2


def passed_along(value, axis, steps):
    count = lax.axis_size(axis)
    pairs = [(source, (source + steps) % count) for source in range(count)]
    return lax.ppermute(value, axis, pairs)


def group_rows(blocks_shard, block_len):
    limit = max(512 // block_len, 1)
    best = 1
    for candidate in range(1, blocks_shard + 1):
        if blocks_shard % candidate == 0 and candidate <= limit:
            best = candidate
    return best


def on_device_windowed(query, key, value, grad_out, neighbour, counts):
    tok_rows = query.shape[0]
    groups = lax.axis_size("head")
    per_dev = H // groups
    head_cols = per_dev * E
    moved = (
        lax.all_to_all(
            query.reshape(tok_rows, groups, head_cols),
            "head",
            split_axis=1,
            concat_axis=0,
            tiled=True,
        ),
        lax.all_to_all(
            key.reshape(tok_rows, groups, head_cols),
            "head",
            split_axis=1,
            concat_axis=0,
            tiled=True,
        ),
        lax.all_to_all(
            value.reshape(tok_rows, groups, head_cols),
            "head",
            split_axis=1,
            concat_axis=0,
            tiled=True,
        ),
        lax.all_to_all(
            grad_out.reshape(tok_rows, groups, head_cols),
            "head",
            split_axis=1,
            concat_axis=0,
            tiled=True,
        ),
    )
    shard_rows = groups * tok_rows
    query_s = moved[0].reshape(shard_rows, head_cols)
    key_s = moved[1].reshape(shard_rows, head_cols)
    value_s = moved[2].reshape(shard_rows, head_cols)
    grad_s = moved[3].reshape(shard_rows, head_cols)
    paired = jnp.concatenate([key_s, value_s], axis=1)
    cycle_len = lax.axis_size("ctx")
    position = lax.axis_index("ctx")
    blocks_shard = shard_rows // BLK
    all_blocks = blocks_shard * cycle_len
    fetched = {}
    offsets_all = list(range(1, REACH + 1)) + [-offset for offset in range(1, REACH + 1)]
    for offset in offsets_all:
        fetched[offset] = passed_along(paired, "ctx", offset)
    ordered = (
        [fetched[REACH - place] for place in range(REACH)]
        + [paired]
        + [fetched[-(place + 1)] for place in range(REACH)]
    )
    span_shards = 2 * REACH + 1
    window = jnp.concatenate(ordered, axis=0).reshape(
        span_shards * blocks_shard, BLK, 2 * head_cols
    )
    rows_nbr = lax.dynamic_slice_in_dim(neighbour, position * blocks_shard, blocks_shard, 0)
    local_idx = jnp.mod(rows_nbr - (position - REACH) * blocks_shard, all_blocks)
    used = lax.dynamic_slice_in_dim(counts, position * blocks_shard, blocks_shard, 0)
    per_group = group_rows(blocks_shard, BLK)
    turns = blocks_shard // per_group
    scale_factor = 1.0 / math.sqrt(E)
    query_g = query_s.reshape(turns, per_group, BLK, per_dev, E)
    grad_g = grad_s.reshape(turns, per_group, BLK, per_dev, E)
    index_g = local_idx.reshape(turns, per_group, NNB)
    used_g = used.reshape(turns, per_group)

    def one_group(totals, inputs):
        queries, cotangent, chosen, used_now = inputs
        selected = window[chosen]
        keys_sel = selected[..., :head_cols].reshape(per_group, NNB, BLK, per_dev, E)
        values_sel = selected[..., head_cols:].reshape(per_group, NNB, BLK, per_dev, E)
        usable = jnp.arange(NNB)[None, :] < used_now[:, None]
        allowed = usable[:, None, None, :, None]
        scores = (
            jnp.einsum("rihe,rjthe->rhijt", queries, keys_sel, preferred_element_type=jnp.float32)
            * scale_factor
        )
        masked = jnp.where(allowed, scores, -1e30)
        highest = jnp.max(masked, axis=(3, 4), keepdims=True)
        raised = jnp.where(allowed, jnp.exp(masked - highest), 0.0)
        total = jnp.sum(raised, axis=(3, 4), keepdims=True)
        probability = raised / total
        weights = probability.astype(jnp.bfloat16)
        out_rows = jnp.einsum(
            "rhijt,rjthe->rihe", weights, values_sel, preferred_element_type=jnp.float32
        ).astype(jnp.bfloat16)
        dprob = jnp.einsum(
            "rihe,rjthe->rhijt", cotangent, values_sel, preferred_element_type=jnp.float32
        )
        row_delta = jnp.sum(probability * dprob, axis=(3, 4), keepdims=True)
        dscore = (probability * (dprob - row_delta) * scale_factor).astype(jnp.bfloat16)
        dquery = jnp.einsum(
            "rhijt,rjthe->rihe", dscore, keys_sel, preferred_element_type=jnp.float32
        ).astype(jnp.bfloat16)
        dkey_part = jnp.einsum(
            "rhijt,rihe->rjthe", dscore, queries, preferred_element_type=jnp.float32
        )
        dvalue_part = jnp.einsum(
            "rhijt,rihe->rjthe", weights, cotangent, preferred_element_type=jnp.float32
        )
        joined = jnp.concatenate(
            [
                dkey_part.reshape(per_group * NNB, BLK, head_cols),
                dvalue_part.reshape(per_group * NNB, BLK, head_cols),
            ],
            axis=-1,
        )
        totals = totals.at[chosen.reshape(-1)].add(joined)
        return (totals, (out_rows, dquery))

    start_grads = jnp.zeros((span_shards * blocks_shard, BLK, 2 * head_cols), jnp.float32)
    grads_window, results = lax.scan(one_group, start_grads, (query_g, grad_g, index_g, used_g))
    grads_window = grads_window.reshape(span_shards, shard_rows, 2 * head_cols)
    combined = grads_window[REACH]
    offsets_back = list(range(1, REACH + 1)) + [-offset for offset in range(1, REACH + 1)]
    for offset in offsets_back:
        combined = combined + passed_along(
            grads_window[REACH - offset].astype(jnp.bfloat16), "ctx", -offset
        ).astype(jnp.float32)
    combined = combined.astype(jnp.bfloat16)
    dkey_s = combined[:, :head_cols]
    dvalue_s = combined[:, head_cols:]
    out_s = results[0].reshape(shard_rows, head_cols)
    dquery_s = results[1].reshape(shard_rows, head_cols)
    back = (
        lax.all_to_all(
            out_s.reshape(shard_rows, 1, head_cols), "head", split_axis=0, concat_axis=1, tiled=True
        ),
        lax.all_to_all(
            dquery_s.reshape(shard_rows, 1, head_cols),
            "head",
            split_axis=0,
            concat_axis=1,
            tiled=True,
        ),
        lax.all_to_all(
            dkey_s.reshape(shard_rows, 1, head_cols),
            "head",
            split_axis=0,
            concat_axis=1,
            tiled=True,
        ),
        lax.all_to_all(
            dvalue_s.reshape(shard_rows, 1, head_cols),
            "head",
            split_axis=0,
            concat_axis=1,
            tiled=True,
        ),
    )
    width = groups * head_cols
    return (
        back[0].reshape(tok_rows, width),
        back[1].reshape(tok_rows, width),
        back[2].reshape(tok_rows, width),
        back[3].reshape(tok_rows, width),
    )


MESH_ID = pl.DeviceIdType.MESH
F32 = jnp.float32
BF16 = jnp.bfloat16
VMEM_BYTES = 20 * 1024 * 1024


def place_of():
    index = lax.axis_index("ctx") * lax.axis_size("head") + lax.axis_index("head")
    return lax.div(index, 2), lax.rem(index, 2)


def device_of(owner, side):
    n_head = lax.axis_size("head")
    index = 2 * owner + side
    return (lax.div(index, n_head), lax.rem(index, n_head))


def partners(pairs, owner, step):
    half = pairs // 2
    far = 1 - lax.div(step, half)
    base = lax.rem(lax.div(owner, half) + far, 2) * half
    low, turn = lax.rem(owner, half), lax.rem(step, half)
    return base + lax.rem(low + turn, half), base + lax.rem(low - turn + half, half)


def each_step(pairs, body):
    def one(step, carry):
        body(step)
        return carry

    lax.fori_loop(0, pairs // 2, one, 0)
    lax.fori_loop(pairs // 2 + 1, pairs, one, 0)


def greet(pairs):
    owner, side = place_of()
    barrier = pltpu.get_barrier_semaphore()
    pl.semaphore_signal(barrier, inc=1, device_id=device_of(owner, 1 - side), device_id_type=MESH_ID)

    def one(step):
        to, _ = partners(pairs, owner, step)
        pl.semaphore_signal(barrier, inc=1, device_id=device_of(to, side), device_id_type=MESH_ID)

    each_step(pairs, one)
    return barrier


def spread_kernel(
    pairs, query, key, value, grad_out, qd, kv, kvt, own_rows, send_qd, send_kv,
    load, qd_out, qd_in, kv_out, kv_in, share_out, share_in,
):
    owner, side = place_of()
    loads = [
        pltpu.make_async_copy(array, own_rows.at[place], load.at[place])
        for place, array in enumerate((key, value, query, grad_out))
    ]
    for copy in loads:
        copy.start()
    barrier = greet(pairs)

    def pack(first, pieces):
        loads[first].wait()
        loads[first + 1].wait()
        for pair in range(pairs // 2):
            cols = slice(2 * E * pair, 2 * E * (pair + 1))
            a = own_rows[first, :, cols]
            b = own_rows[first + 1, :, cols]
            pieces[2 * pair] = jnp.concatenate([a[:, :E], b[:, :E]], axis=1)
            pieces[2 * pair + 1] = jnp.concatenate([a[:, E:], b[:, E:]], axis=1)

    def kv_copy(step, to, source):
        return pltpu.make_async_remote_copy(
            src_ref=send_kv.at[to],
            dst_ref=kv.at[2 * source + side],
            send_sem=kv_out.at[step],
            recv_sem=kv_in.at[step],
            device_id=device_of(to, side),
            device_id_type=MESH_ID,
        )

    def qd_copy(step, to, source):
        return pltpu.make_async_remote_copy(
            src_ref=send_qd.at[to],
            dst_ref=qd.at[source],
            send_sem=qd_out.at[step],
            recv_sem=qd_in.at[step],
            device_id=device_of(to, side),
            device_id_type=MESH_ID,
        )

    def share_copy(step, source, whose):
        return pltpu.make_async_remote_copy(
            src_ref=kv.at[2 * source + side],
            dst_ref=kv.at[2 * source + whose],
            send_sem=share_out.at[step],
            recv_sem=share_in.at[step],
            device_id=device_of(owner, 1 - side),
            device_id_type=MESH_ID,
        )

    def send_keys(step):
        to, _ = partners(pairs, owner, step)
        kv_copy(step, to, owner).start()

    def send_queries(step):
        to, _ = partners(pairs, owner, step)
        qd_copy(step, to, owner).start()

    pack(0, send_kv)
    pl.semaphore_wait(barrier, pairs)
    each_step(pairs, send_keys)
    pack(2, send_qd)
    each_step(pairs, send_queries)
    mine = 2 * owner + side
    kv[mine] = send_kv[owner]
    qd[owner] = send_qd[owner]
    share_copy(pairs // 2, owner, side).start()
    kvt[mine] = kv[mine].T

    def pass_on(step):
        _, source = partners(pairs, owner, step)
        kv_copy(step, owner, source).wait_recv()
        share_copy(step, source, side).start()
        kvt[2 * source + side] = kv[2 * source + side].T

    def take_share(step):
        _, source = partners(pairs, owner, step)
        share_copy(step, source, side).wait_send()
        share_copy(step, source, 1 - side).wait_recv()
        kvt[2 * source + 1 - side] = kv[2 * source + 1 - side].T

    def finish(step):
        to, source = partners(pairs, owner, step)
        qd_copy(step, owner, source).wait_recv()
        qd_copy(step, to, owner).wait_send()
        kv_copy(step, to, owner).wait_send()

    each_step(pairs, pass_on)
    take_share(jnp.int32(pairs // 2))
    each_step(pairs, take_share)
    each_step(pairs, finish)


def attend_kernel(
    blocks, neighbour_hbm, counts, qd, kv, kvt, od, totals, neighbour, pair_scr, x_scr, load
):
    _, side = place_of()
    half = blocks // 2
    scale = 1.0 / math.sqrt(E)
    exp_scale = scale * math.log2(math.e)
    low = lax.broadcasted_iota(jnp.int32, (BLK, 2 * E), 1) < E
    top = lax.broadcasted_iota(jnp.int32, (2 * E, BLK), 0) < E
    names_copy = pltpu.make_async_copy(neighbour_hbm, neighbour, load)
    names_copy.start()

    def clear(block, carry):
        totals[block] = jnp.zeros((BLK, 2 * E), F32)
        return carry

    lax.fori_loop(0, blocks, clear, 0)
    names_copy.wait()

    def folded(array, op):
        return op(array.reshape(BLK // 8, 8, BLK), axis=0)

    def rows_with(place, block, used):
        both = qd[place]
        zero = jnp.zeros_like(both)
        spread = jnp.concatenate([jnp.where(low, both, zero), jnp.where(low, zero, both)], axis=0)
        names = [neighbour[block, slot] for slot in range(used)]
        highest = None
        for slot in range(used):
            result = lax.dot_general(
                kv[names[slot]], spread, (((1,), (1,)), ((), ())), preferred_element_type=F32
            )
            pair_scr[slot] = result
            part = folded(result[:, :BLK], jnp.max)
            highest = part if highest is None else jnp.maximum(highest, part)
        highest = jnp.max(highest, axis=0, keepdims=True)
        total = jnp.zeros((8, BLK), F32)
        delta = jnp.zeros((8, BLK), F32)
        for slot in range(used):
            raised = jnp.exp2((pair_scr[slot, :, :BLK] - highest) * exp_scale)
            pair_scr[slot, :, :BLK] = raised
            total = total + folded(raised, jnp.sum)
            delta = delta + folded(raised * pair_scr[slot, :, BLK:], jnp.sum)
        inverse = 1.0 / jnp.sum(total, axis=0, keepdims=True)
        delta = jnp.sum(delta, axis=0, keepdims=True) * inverse
        for slot in range(used):
            probability = pair_scr[slot, :, :BLK] * inverse
            dscore = (probability * scale) * (pair_scr[slot, :, BLK:] - delta)
            x_scr[slot] = jnp.concatenate(
                [dscore.astype(BF16), probability.astype(BF16)], axis=1
            )
        rows = jnp.zeros((2 * E, 2 * BLK), F32)
        for slot in range(0, used, 2):
            if slot + 1 < used:
                keys_t = jnp.concatenate([kvt[names[slot]], kvt[names[slot + 1]]], axis=1)
                grads = jnp.concatenate([x_scr[slot], x_scr[slot + 1]], axis=0)
            else:
                keys_t = kvt[names[slot]]
                grads = x_scr[slot]
            rows = rows + jnp.dot(keys_t, grads, preferred_element_type=F32)
        for slot in range(used):
            totals[names[slot]] += jnp.dot(x_scr[slot], spread, preferred_element_type=F32)
        od[place] = jnp.where(top, rows[:, :BLK], rows[:, BLK:]).T.astype(BF16)

    def one_block(place, carry):
        block = 2 * place + side
        used_now = counts[block]
        for used in range(1, NNB + 1):
            pl.when(used_now == used)(functools.partial(rows_with, place, block, used))
        return carry

    lax.fori_loop(0, half, one_block, 0)


def collect_kernel(
    pairs, od, totals, got_od, got_kv, other, shared, send_kv,
    od_out, od_in, kv_out, kv_in, share_out, share_in,
):
    owner, side = place_of()
    barrier = greet(pairs)

    def share_copy(step, place):
        return pltpu.make_async_remote_copy(
            src_ref=other.at[place],
            dst_ref=shared.at[place],
            send_sem=share_out.at[step],
            recv_sem=share_in.at[step],
            device_id=device_of(owner, 1 - side),
            device_id_type=MESH_ID,
        )

    def od_copy(step, to, source):
        return pltpu.make_async_remote_copy(
            src_ref=od.at[to],
            dst_ref=got_od.at[source],
            send_sem=od_out.at[step],
            recv_sem=od_in.at[step],
            device_id=device_of(to, side),
            device_id_type=MESH_ID,
        )

    def kv_copy(step, to, source):
        return pltpu.make_async_remote_copy(
            src_ref=send_kv.at[to],
            dst_ref=got_kv.at[source],
            send_sem=kv_out.at[step],
            recv_sem=kv_in.at[step],
            device_id=device_of(to, side),
            device_id_type=MESH_ID,
        )

    def narrow(place, carry):
        other[place] = totals[2 * place + 1 - side].astype(BF16)
        return carry

    lax.fori_loop(0, pairs, narrow, 0)
    pl.semaphore_wait(barrier, pairs)

    def start_all(step):
        to, _ = partners(pairs, owner, step)
        od_copy(step, to, owner).start()
        share_copy(step, to).start()

    def summed(place):
        return (totals[2 * place + side] + shared[place].astype(F32)).astype(BF16)

    def add_and_send(step):
        to, _ = partners(pairs, owner, step)
        share_copy(step, to).wait_recv()
        send_kv[to] = summed(to)
        kv_copy(step, to, owner).start()

    def finish(step):
        to, source = partners(pairs, owner, step)
        od_copy(step, owner, source).wait_recv()
        kv_copy(step, owner, source).wait_recv()
        od_copy(step, to, owner).wait_send()
        kv_copy(step, to, owner).wait_send()
        share_copy(step, to).wait_send()

    each_step(pairs, start_all)
    share_copy(pairs // 2, owner).start()
    each_step(pairs, add_and_send)
    share_copy(pairs // 2, owner).wait_recv()
    got_kv[owner] = summed(owner)
    got_od[owner] = od[owner]
    each_step(pairs, finish)
    share_copy(pairs // 2, owner).wait_send()


def join_kernel(pairs, got_od, got_kv, out, dquery, dkey, dvalue, rows, store):
    copies = []
    for place, (pieces, part, array) in enumerate(
        ((got_od, 1, out), (got_od, 0, dquery), (got_kv, 0, dkey), (got_kv, 1, dvalue))
    ):
        cut = slice(part * E, (part + 1) * E)
        for pair in range(pairs // 2):
            cols = slice(2 * E * pair, 2 * E * (pair + 1))
            rows[place, :, cols] = jnp.concatenate(
                [pieces[2 * pair][:, cut], pieces[2 * pair + 1][:, cut]], axis=1
            )
        copies.append(pltpu.make_async_copy(rows.at[place], array, store.at[place]))
        copies[-1].start()
    for copy in copies:
        copy.wait()


def on_device_whole(query, key, value, grad_out, neighbour, counts):
    pairs = lax.axis_size("ctx") * lax.axis_size("head") // 2
    blocks = 2 * pairs
    width = query.shape[1]
    in_vmem = pl.BlockSpec(memory_space=pltpu.VMEM)
    in_smem = pl.BlockSpec(memory_space=pltpu.SMEM)
    in_hbm = pl.BlockSpec(memory_space=pltpu.HBM)
    many = pltpu.SemaphoreType.DMA((pairs,))
    piece = (BLK, 2 * E)
    own_pieces = jax.ShapeDtypeStruct((pairs, *piece), BF16)
    all_pieces = jax.ShapeDtypeStruct((blocks, *piece), BF16)
    with jax.named_scope("spread_heads"):
        qd, kv, kvt = pl.pallas_call(
            functools.partial(spread_kernel, pairs),
            out_shape=(own_pieces, all_pieces, all_pieces),
            in_specs=[in_hbm] * 4,
            out_specs=(in_vmem,) * 3,
            scratch_shapes=[pltpu.VMEM((4, BLK, width), BF16)]
            + [pltpu.VMEM((pairs, *piece), BF16)] * 2
            + [pltpu.SemaphoreType.DMA((4,))]
            + [many] * 6,
            compiler_params=pltpu.CompilerParams(
                collective_id=0, has_side_effects=True, vmem_limit_bytes=VMEM_BYTES
            ),
        )(query, key, value, grad_out)
    with jax.named_scope("block_attention"):
        od, totals = pl.pallas_call(
            functools.partial(attend_kernel, blocks),
            out_shape=(own_pieces, jax.ShapeDtypeStruct((blocks, *piece), F32)),
            in_specs=[in_hbm, in_smem] + [in_vmem] * 3,
            out_specs=(in_vmem,) * 2,
            scratch_shapes=[
                pltpu.SMEM(neighbour.shape, jnp.int32),
                pltpu.VMEM((NNB, BLK, 2 * BLK), F32),
                pltpu.VMEM((NNB, BLK, 2 * BLK), BF16),
                pltpu.SemaphoreType.DMA(()),
            ],
            compiler_params=pltpu.CompilerParams(vmem_limit_bytes=VMEM_BYTES),
        )(neighbour, counts, qd, kv, kvt)
    with jax.named_scope("collect_heads"):
        got_od, got_kv = pl.pallas_call(
            functools.partial(collect_kernel, pairs),
            out_shape=(own_pieces,) * 2,
            in_specs=[in_vmem] * 2,
            out_specs=(in_vmem,) * 2,
            scratch_shapes=[pltpu.VMEM((pairs, *piece), BF16)] * 3 + [many] * 6,
            compiler_params=pltpu.CompilerParams(
                collective_id=1, has_side_effects=True, vmem_limit_bytes=VMEM_BYTES
            ),
        )(od, totals)
    with jax.named_scope("join_heads"):
        return pl.pallas_call(
            functools.partial(join_kernel, pairs),
            out_shape=(jax.ShapeDtypeStruct((BLK, width), BF16),) * 4,
            in_specs=[in_vmem] * 2,
            out_specs=(in_hbm,) * 4,
            scratch_shapes=[
                pltpu.VMEM((4, BLK, width), BF16),
                pltpu.SemaphoreType.DMA((4,)),
            ],
            compiler_params=pltpu.CompilerParams(vmem_limit_bytes=VMEM_BYTES),
        )(got_od, got_kv)


def on_device(query, key, value, grad_out, neighbour, counts):
    devices = lax.axis_size("ctx") * lax.axis_size("head")
    if devices == 2 * H and query.shape == (BLK, H * E) and counts.shape[0] == devices:
        return on_device_whole(query, key, value, grad_out, neighbour, counts)
    return on_device_windowed(query, key, value, grad_out, neighbour, counts)


def solution(mesh):
    return jax.shard_map(
        on_device,
        mesh=mesh,
        in_specs=(
            P(("ctx", "head"), None),
            P(("ctx", "head"), None),
            P(("ctx", "head"), None),
            P(("ctx", "head"), None),
            P(),
            P(),
        ),
        out_specs=(
            P(("ctx", "head"), None),
            P(("ctx", "head"), None),
            P(("ctx", "head"), None),
            P(("ctx", "head"), None),
        ),
        check_vma=False,
    )
```

```python
import functools
import math

import jax
import jax.numpy as jnp
from jax import lax
from jax.experimental import pallas as pl
from jax.experimental.pallas import tpu as pltpu
from jax.sharding import PartitionSpec as P

H = 16
E = 64
BLK = 128
NNB = 8
REACH = 2


def passed_along(value, axis, steps):
    count = lax.axis_size(axis)
    pairs = [(source, (source + steps) % count) for source in range(count)]
    return lax.ppermute(value, axis, pairs)


def group_rows(blocks_shard, block_len):
    limit = max(512 // block_len, 1)
    best = 1
    for candidate in range(1, blocks_shard + 1):
        if blocks_shard % candidate == 0 and candidate <= limit:
            best = candidate
    return best


def on_device_windowed(query, key, value, grad_out, neighbour, counts):
    tok_rows = query.shape[0]
    groups = lax.axis_size("head")
    per_dev = H // groups
    head_cols = per_dev * E
    moved = (
        lax.all_to_all(
            query.reshape(tok_rows, groups, head_cols),
            "head",
            split_axis=1,
            concat_axis=0,
            tiled=True,
        ),
        lax.all_to_all(
            key.reshape(tok_rows, groups, head_cols),
            "head",
            split_axis=1,
            concat_axis=0,
            tiled=True,
        ),
        lax.all_to_all(
            value.reshape(tok_rows, groups, head_cols),
            "head",
            split_axis=1,
            concat_axis=0,
            tiled=True,
        ),
        lax.all_to_all(
            grad_out.reshape(tok_rows, groups, head_cols),
            "head",
            split_axis=1,
            concat_axis=0,
            tiled=True,
        ),
    )
    shard_rows = groups * tok_rows
    query_s = moved[0].reshape(shard_rows, head_cols)
    key_s = moved[1].reshape(shard_rows, head_cols)
    value_s = moved[2].reshape(shard_rows, head_cols)
    grad_s = moved[3].reshape(shard_rows, head_cols)
    paired = jnp.concatenate([key_s, value_s], axis=1)
    cycle_len = lax.axis_size("ctx")
    position = lax.axis_index("ctx")
    blocks_shard = shard_rows // BLK
    all_blocks = blocks_shard * cycle_len
    fetched = {}
    offsets_all = list(range(1, REACH + 1)) + [-offset for offset in range(1, REACH + 1)]
    for offset in offsets_all:
        fetched[offset] = passed_along(paired, "ctx", offset)
    ordered = (
        [fetched[REACH - place] for place in range(REACH)]
        + [paired]
        + [fetched[-(place + 1)] for place in range(REACH)]
    )
    span_shards = 2 * REACH + 1
    window = jnp.concatenate(ordered, axis=0).reshape(
        span_shards * blocks_shard, BLK, 2 * head_cols
    )
    rows_nbr = lax.dynamic_slice_in_dim(neighbour, position * blocks_shard, blocks_shard, 0)
    local_idx = jnp.mod(rows_nbr - (position - REACH) * blocks_shard, all_blocks)
    used = lax.dynamic_slice_in_dim(counts, position * blocks_shard, blocks_shard, 0)
    per_group = group_rows(blocks_shard, BLK)
    turns = blocks_shard // per_group
    scale_factor = 1.0 / math.sqrt(E)
    query_g = query_s.reshape(turns, per_group, BLK, per_dev, E)
    grad_g = grad_s.reshape(turns, per_group, BLK, per_dev, E)
    index_g = local_idx.reshape(turns, per_group, NNB)
    used_g = used.reshape(turns, per_group)

    def one_group(totals, inputs):
        queries, cotangent, chosen, used_now = inputs
        selected = window[chosen]
        keys_sel = selected[..., :head_cols].reshape(per_group, NNB, BLK, per_dev, E)
        values_sel = selected[..., head_cols:].reshape(per_group, NNB, BLK, per_dev, E)
        usable = jnp.arange(NNB)[None, :] < used_now[:, None]
        allowed = usable[:, None, None, :, None]
        scores = (
            jnp.einsum("rihe,rjthe->rhijt", queries, keys_sel, preferred_element_type=jnp.float32)
            * scale_factor
        )
        masked = jnp.where(allowed, scores, -1e30)
        highest = jnp.max(masked, axis=(3, 4), keepdims=True)
        raised = jnp.where(allowed, jnp.exp(masked - highest), 0.0)
        total = jnp.sum(raised, axis=(3, 4), keepdims=True)
        probability = raised / total
        weights = probability.astype(jnp.bfloat16)
        out_rows = jnp.einsum(
            "rhijt,rjthe->rihe", weights, values_sel, preferred_element_type=jnp.float32
        ).astype(jnp.bfloat16)
        dprob = jnp.einsum(
            "rihe,rjthe->rhijt", cotangent, values_sel, preferred_element_type=jnp.float32
        )
        row_delta = jnp.sum(probability * dprob, axis=(3, 4), keepdims=True)
        dscore = (probability * (dprob - row_delta) * scale_factor).astype(jnp.bfloat16)
        dquery = jnp.einsum(
            "rhijt,rjthe->rihe", dscore, keys_sel, preferred_element_type=jnp.float32
        ).astype(jnp.bfloat16)
        dkey_part = jnp.einsum(
            "rhijt,rihe->rjthe", dscore, queries, preferred_element_type=jnp.float32
        )
        dvalue_part = jnp.einsum(
            "rhijt,rihe->rjthe", weights, cotangent, preferred_element_type=jnp.float32
        )
        joined = jnp.concatenate(
            [
                dkey_part.reshape(per_group * NNB, BLK, head_cols),
                dvalue_part.reshape(per_group * NNB, BLK, head_cols),
            ],
            axis=-1,
        )
        totals = totals.at[chosen.reshape(-1)].add(joined)
        return (totals, (out_rows, dquery))

    start_grads = jnp.zeros((span_shards * blocks_shard, BLK, 2 * head_cols), jnp.float32)
    grads_window, results = lax.scan(one_group, start_grads, (query_g, grad_g, index_g, used_g))
    grads_window = grads_window.reshape(span_shards, shard_rows, 2 * head_cols)
    combined = grads_window[REACH]
    offsets_back = list(range(1, REACH + 1)) + [-offset for offset in range(1, REACH + 1)]
    for offset in offsets_back:
        combined = combined + passed_along(
            grads_window[REACH - offset].astype(jnp.bfloat16), "ctx", -offset
        ).astype(jnp.float32)
    combined = combined.astype(jnp.bfloat16)
    dkey_s = combined[:, :head_cols]
    dvalue_s = combined[:, head_cols:]
    out_s = results[0].reshape(shard_rows, head_cols)
    dquery_s = results[1].reshape(shard_rows, head_cols)
    back = (
        lax.all_to_all(
            out_s.reshape(shard_rows, 1, head_cols), "head", split_axis=0, concat_axis=1, tiled=True
        ),
        lax.all_to_all(
            dquery_s.reshape(shard_rows, 1, head_cols),
            "head",
            split_axis=0,
            concat_axis=1,
            tiled=True,
        ),
        lax.all_to_all(
            dkey_s.reshape(shard_rows, 1, head_cols),
            "head",
            split_axis=0,
            concat_axis=1,
            tiled=True,
        ),
        lax.all_to_all(
            dvalue_s.reshape(shard_rows, 1, head_cols),
            "head",
            split_axis=0,
            concat_axis=1,
            tiled=True,
        ),
    )
    width = groups * head_cols
    return (
        back[0].reshape(tok_rows, width),
        back[1].reshape(tok_rows, width),
        back[2].reshape(tok_rows, width),
        back[3].reshape(tok_rows, width),
    )


MESH_ID = pl.DeviceIdType.MESH
F32 = jnp.float32
BF16 = jnp.bfloat16
VMEM_BYTES = 20 * 1024 * 1024


def left_in_hbm(array):
    return pltpu.with_memory_space_constraint(array, pltpu.HBM)


def place_of():
    index = lax.axis_index("ctx") * lax.axis_size("head") + lax.axis_index("head")
    return lax.div(index, 2), lax.rem(index, 2)


def device_of(owner, side):
    n_head = lax.axis_size("head")
    index = 2 * owner + side
    return (lax.div(index, n_head), lax.rem(index, n_head))


def partners(pairs, owner, step):
    half = pairs // 2
    far = 1 - lax.div(step, half)
    base = lax.rem(lax.div(owner, half) + far, 2) * half
    low, turn = lax.rem(owner, half), lax.rem(step, half)
    return base + lax.rem(low + turn, half), base + lax.rem(low - turn + half, half)


def each_step(pairs, body):
    def one(step, carry):
        body(step)
        return carry

    lax.fori_loop(0, pairs // 2, one, 0)
    lax.fori_loop(pairs // 2 + 1, pairs, one, 0)


def greet(pairs):
    owner, side = place_of()
    barrier = pltpu.get_barrier_semaphore()
    pl.semaphore_signal(barrier, inc=1, device_id=device_of(owner, 1 - side), device_id_type=MESH_ID)

    def one(step):
        to, _ = partners(pairs, owner, step)
        pl.semaphore_signal(barrier, inc=1, device_id=device_of(to, side), device_id_type=MESH_ID)

    each_step(pairs, one)
    return barrier


def spread_kernel(
    pairs, query, key, value, grad_out, qd, kv, kvt, own_rows, send_qd, send_kv,
    load, qd_out, qd_in, kv_out, kv_in, share_out, share_in,
):
    owner, side = place_of()
    loads = [
        pltpu.make_async_copy(array, own_rows.at[place], load.at[place])
        for place, array in enumerate((key, value, query, grad_out))
    ]
    for copy in loads:
        copy.start()
    barrier = greet(pairs)

    def pack(first, pieces):
        loads[first].wait()
        loads[first + 1].wait()
        for pair in range(pairs // 2):
            cols = slice(2 * E * pair, 2 * E * (pair + 1))
            a = own_rows[first, :, cols]
            b = own_rows[first + 1, :, cols]
            pieces[2 * pair] = jnp.concatenate([a[:, :E], b[:, :E]], axis=1)
            pieces[2 * pair + 1] = jnp.concatenate([a[:, E:], b[:, E:]], axis=1)

    def kv_copy(step, to, source):
        return pltpu.make_async_remote_copy(
            src_ref=send_kv.at[to],
            dst_ref=kv.at[2 * source + side],
            send_sem=kv_out.at[step],
            recv_sem=kv_in.at[step],
            device_id=device_of(to, side),
            device_id_type=MESH_ID,
        )

    def qd_copy(step, to, source):
        return pltpu.make_async_remote_copy(
            src_ref=send_qd.at[to],
            dst_ref=qd.at[source],
            send_sem=qd_out.at[step],
            recv_sem=qd_in.at[step],
            device_id=device_of(to, side),
            device_id_type=MESH_ID,
        )

    def share_copy(step, source, whose):
        return pltpu.make_async_remote_copy(
            src_ref=kv.at[2 * source + side],
            dst_ref=kv.at[2 * source + whose],
            send_sem=share_out.at[step],
            recv_sem=share_in.at[step],
            device_id=device_of(owner, 1 - side),
            device_id_type=MESH_ID,
        )

    def send_keys(step):
        to, _ = partners(pairs, owner, step)
        kv_copy(step, to, owner).start()

    def send_queries(step):
        to, _ = partners(pairs, owner, step)
        qd_copy(step, to, owner).start()

    pack(0, send_kv)
    pl.semaphore_wait(barrier, pairs)
    each_step(pairs, send_keys)
    pack(2, send_qd)
    each_step(pairs, send_queries)
    mine = 2 * owner + side
    kv[mine] = send_kv[owner]
    qd[owner] = send_qd[owner]
    share_copy(pairs // 2, owner, side).start()
    kvt[mine] = kv[mine].T

    def pass_on(step):
        _, source = partners(pairs, owner, step)
        kv_copy(step, owner, source).wait_recv()
        share_copy(step, source, side).start()
        kvt[2 * source + side] = kv[2 * source + side].T

    def take_share(step):
        _, source = partners(pairs, owner, step)
        share_copy(step, source, side).wait_send()
        share_copy(step, source, 1 - side).wait_recv()
        kvt[2 * source + 1 - side] = kv[2 * source + 1 - side].T

    def finish(step):
        to, source = partners(pairs, owner, step)
        qd_copy(step, owner, source).wait_recv()
        qd_copy(step, to, owner).wait_send()
        kv_copy(step, to, owner).wait_send()

    each_step(pairs, pass_on)
    take_share(jnp.int32(pairs // 2))
    each_step(pairs, take_share)
    each_step(pairs, finish)


def attend_kernel(
    blocks, neighbour_hbm, counts_hbm, qd, kv, kvt, od, totals,
    neighbour, counts, pair_scr, x_scr, load
):
    _, side = place_of()
    half = blocks // 2
    scale = 1.0 / math.sqrt(E)
    exp_scale = scale * math.log2(math.e)
    low = lax.broadcasted_iota(jnp.int32, (BLK, 2 * E), 1) < E
    top = lax.broadcasted_iota(jnp.int32, (2 * E, BLK), 0) < E
    names_copy = pltpu.make_async_copy(neighbour_hbm, neighbour, load.at[0])
    names_copy.start()
    counts_copy = pltpu.make_async_copy(counts_hbm, counts, load.at[1])
    counts_copy.start()

    def clear(block, carry):
        totals[block] = jnp.zeros((BLK, 2 * E), F32)
        return carry

    lax.fori_loop(0, blocks, clear, 0)
    names_copy.wait()
    counts_copy.wait()

    def folded(array, op):
        return op(array.reshape(BLK // 8, 8, BLK), axis=0)

    def rows_with(place, block, used):
        both = qd[place]
        zero = jnp.zeros_like(both)
        spread = jnp.concatenate([jnp.where(low, both, zero), jnp.where(low, zero, both)], axis=0)
        names = [neighbour[slot, block] for slot in range(used)]
        highest = None
        for slot in range(used):
            result = lax.dot_general(
                kv[names[slot]], spread, (((1,), (1,)), ((), ())), preferred_element_type=F32
            )
            pair_scr[slot] = result
            part = folded(result[:, :BLK], jnp.max)
            highest = part if highest is None else jnp.maximum(highest, part)
        highest = jnp.max(highest, axis=0, keepdims=True)
        total = jnp.zeros((8, BLK), F32)
        delta = jnp.zeros((8, BLK), F32)
        for slot in range(used):
            raised = jnp.exp2((pair_scr[slot, :, :BLK] - highest) * exp_scale)
            pair_scr[slot, :, :BLK] = raised
            total = total + folded(raised, jnp.sum)
            delta = delta + folded(raised * pair_scr[slot, :, BLK:], jnp.sum)
        inverse = 1.0 / jnp.sum(total, axis=0, keepdims=True)
        delta = jnp.sum(delta, axis=0, keepdims=True) * inverse
        for slot in range(used):
            probability = pair_scr[slot, :, :BLK] * inverse
            dscore = (probability * scale) * (pair_scr[slot, :, BLK:] - delta)
            x_scr[slot] = jnp.concatenate(
                [dscore.astype(BF16), probability.astype(BF16)], axis=1
            )
        rows = jnp.zeros((2 * E, 2 * BLK), F32)
        for slot in range(0, used, 2):
            if slot + 1 < used:
                keys_t = jnp.concatenate([kvt[names[slot]], kvt[names[slot + 1]]], axis=1)
                grads = jnp.concatenate([x_scr[slot], x_scr[slot + 1]], axis=0)
            else:
                keys_t = kvt[names[slot]]
                grads = x_scr[slot]
            rows = rows + jnp.dot(keys_t, grads, preferred_element_type=F32)
        for slot in range(used):
            totals[names[slot]] += jnp.dot(x_scr[slot], spread, preferred_element_type=F32)
        od[place] = jnp.where(top, rows[:, :BLK], rows[:, BLK:]).T.astype(BF16)

    def one_block(place, carry):
        block = 2 * place + side
        used_now = counts[block]
        for used in range(1, NNB + 1):
            pl.when(used_now == used)(functools.partial(rows_with, place, block, used))
        return carry

    lax.fori_loop(0, half, one_block, 0)


def collect_kernel(
    pairs, od, totals, got_od, got_kv, other, shared, send_kv,
    od_out, od_in, kv_out, kv_in, share_out, share_in,
):
    owner, side = place_of()
    barrier = greet(pairs)

    def share_copy(step, place):
        return pltpu.make_async_remote_copy(
            src_ref=other.at[place],
            dst_ref=shared.at[place],
            send_sem=share_out.at[step],
            recv_sem=share_in.at[step],
            device_id=device_of(owner, 1 - side),
            device_id_type=MESH_ID,
        )

    def od_copy(step, to, source):
        return pltpu.make_async_remote_copy(
            src_ref=od.at[to],
            dst_ref=got_od.at[source],
            send_sem=od_out.at[step],
            recv_sem=od_in.at[step],
            device_id=device_of(to, side),
            device_id_type=MESH_ID,
        )

    def kv_copy(step, to, source):
        return pltpu.make_async_remote_copy(
            src_ref=send_kv.at[to],
            dst_ref=got_kv.at[source],
            send_sem=kv_out.at[step],
            recv_sem=kv_in.at[step],
            device_id=device_of(to, side),
            device_id_type=MESH_ID,
        )

    def narrow(place, carry):
        other[place] = totals[2 * place + 1 - side].astype(BF16)
        return carry

    lax.fori_loop(0, pairs, narrow, 0)
    pl.semaphore_wait(barrier, pairs)

    def start_all(step):
        to, _ = partners(pairs, owner, step)
        od_copy(step, to, owner).start()
        share_copy(step, to).start()

    def summed(place):
        return (totals[2 * place + side] + shared[place].astype(F32)).astype(BF16)

    def add_and_send(step):
        to, _ = partners(pairs, owner, step)
        share_copy(step, to).wait_recv()
        send_kv[to] = summed(to)
        kv_copy(step, to, owner).start()

    def finish(step):
        to, source = partners(pairs, owner, step)
        od_copy(step, owner, source).wait_recv()
        kv_copy(step, owner, source).wait_recv()
        od_copy(step, to, owner).wait_send()
        kv_copy(step, to, owner).wait_send()
        share_copy(step, to).wait_send()

    each_step(pairs, start_all)
    share_copy(pairs // 2, owner).start()
    each_step(pairs, add_and_send)
    share_copy(pairs // 2, owner).wait_recv()
    got_kv[owner] = summed(owner)
    got_od[owner] = od[owner]
    each_step(pairs, finish)
    share_copy(pairs // 2, owner).wait_send()


def join_kernel(pairs, got_od, got_kv, out, dquery, dkey, dvalue, rows, store):
    copies = []
    for place, (pieces, part, array) in enumerate(
        ((got_od, 1, out), (got_od, 0, dquery), (got_kv, 0, dkey), (got_kv, 1, dvalue))
    ):
        cut = slice(part * E, (part + 1) * E)
        for pair in range(pairs // 2):
            cols = slice(2 * E * pair, 2 * E * (pair + 1))
            rows[place, :, cols] = jnp.concatenate(
                [pieces[2 * pair][:, cut], pieces[2 * pair + 1][:, cut]], axis=1
            )
        copies.append(pltpu.make_async_copy(rows.at[place], array, store.at[place]))
        copies[-1].start()
    for copy in copies:
        copy.wait()


def on_device_whole(query, key, value, grad_out, neighbour, counts):
    pairs = lax.axis_size("ctx") * lax.axis_size("head") // 2
    blocks = 2 * pairs
    width = query.shape[1]
    in_vmem = pl.BlockSpec(memory_space=pltpu.VMEM)
    in_hbm = pl.BlockSpec(memory_space=pltpu.HBM)
    many = pltpu.SemaphoreType.DMA((pairs,))
    piece = (BLK, 2 * E)
    own_pieces = jax.ShapeDtypeStruct((pairs, *piece), BF16)
    all_pieces = jax.ShapeDtypeStruct((blocks, *piece), BF16)
    with jax.named_scope("spread_heads"):
        qd, kv, kvt = pl.pallas_call(
            functools.partial(spread_kernel, pairs),
            out_shape=tuple(pltpu.VMEM((count, *piece), BF16) for count in (pairs, blocks, blocks)),
            in_specs=[in_hbm] * 4,
            out_specs=(in_vmem,) * 3,
            scratch_shapes=[pltpu.VMEM((4, BLK, width), BF16)]
            + [pltpu.VMEM((pairs, *piece), BF16)] * 2
            + [pltpu.SemaphoreType.DMA((4,))]
            + [many] * 6,
            compiler_params=pltpu.CompilerParams(
                collective_id=0, has_side_effects=True, vmem_limit_bytes=VMEM_BYTES
            ),
        )(*map(left_in_hbm, (query, key, value, grad_out)))
    with jax.named_scope("block_attention"):
        od, totals = pl.pallas_call(
            functools.partial(attend_kernel, blocks),
            out_shape=(own_pieces, jax.ShapeDtypeStruct((blocks, *piece), F32)),
            in_specs=[in_hbm] * 2 + [in_vmem] * 3,
            out_specs=(in_vmem,) * 2,
            scratch_shapes=[
                pltpu.SMEM(neighbour.shape[::-1], jnp.int32),
                pltpu.SMEM(counts.shape, jnp.int32),
                pltpu.VMEM((NNB, BLK, 2 * BLK), F32),
                pltpu.VMEM((NNB, BLK, 2 * BLK), BF16),
                pltpu.SemaphoreType.DMA((2,)),
            ],
            compiler_params=pltpu.CompilerParams(vmem_limit_bytes=VMEM_BYTES),
        )(left_in_hbm(neighbour.T), left_in_hbm(counts), qd, kv, kvt)
    with jax.named_scope("collect_heads"):
        got_od, got_kv = pl.pallas_call(
            functools.partial(collect_kernel, pairs),
            out_shape=(own_pieces,) * 2,
            in_specs=[in_vmem] * 2,
            out_specs=(in_vmem,) * 2,
            scratch_shapes=[pltpu.VMEM((pairs, *piece), BF16)] * 3 + [many] * 6,
            compiler_params=pltpu.CompilerParams(
                collective_id=1, has_side_effects=True, vmem_limit_bytes=VMEM_BYTES
            ),
        )(od, totals)
    with jax.named_scope("join_heads"):
        return pl.pallas_call(
            functools.partial(join_kernel, pairs),
            out_shape=(jax.ShapeDtypeStruct((BLK, width), BF16),) * 4,
            in_specs=[in_vmem] * 2,
            out_specs=(in_hbm,) * 4,
            scratch_shapes=[
                pltpu.VMEM((4, BLK, width), BF16),
                pltpu.SemaphoreType.DMA((4,)),
            ],
            compiler_params=pltpu.CompilerParams(vmem_limit_bytes=VMEM_BYTES),
        )(got_od, got_kv)


def on_device(query, key, value, grad_out, neighbour, counts):
    devices = lax.axis_size("ctx") * lax.axis_size("head")
    if devices == 2 * H and query.shape == (BLK, H * E) and counts.shape[0] == devices:
        return on_device_whole(query, key, value, grad_out, neighbour, counts)
    return on_device_windowed(query, key, value, grad_out, neighbour, counts)


def solution(mesh):
    return jax.shard_map(
        on_device,
        mesh=mesh,
        in_specs=(
            P(("ctx", "head"), None),
            P(("ctx", "head"), None),
            P(("ctx", "head"), None),
            P(("ctx", "head"), None),
            P(),
            P(),
        ),
        out_specs=(
            P(("ctx", "head"), None),
            P(("ctx", "head"), None),
            P(("ctx", "head"), None),
            P(("ctx", "head"), None),
        ),
        check_vma=False,
    )
```

```python
import functools
import math

import jax
import jax.numpy as jnp
from jax import lax
from jax.experimental import pallas as pl
from jax.experimental.pallas import tpu as pltpu
from jax.sharding import PartitionSpec as P

H = 16
E = 64
BLK = 128
NNB = 8
REACH = 2


def passed_along(value, axis, steps):
    count = lax.axis_size(axis)
    pairs = [(source, (source + steps) % count) for source in range(count)]
    return lax.ppermute(value, axis, pairs)


def group_rows(blocks_shard, block_len):
    limit = max(512 // block_len, 1)
    best = 1
    for candidate in range(1, blocks_shard + 1):
        if blocks_shard % candidate == 0 and candidate <= limit:
            best = candidate
    return best


def on_device_windowed(query, key, value, grad_out, neighbour, counts):
    tok_rows = query.shape[0]
    groups = lax.axis_size("head")
    per_dev = H // groups
    head_cols = per_dev * E
    moved = (
        lax.all_to_all(
            query.reshape(tok_rows, groups, head_cols),
            "head",
            split_axis=1,
            concat_axis=0,
            tiled=True,
        ),
        lax.all_to_all(
            key.reshape(tok_rows, groups, head_cols),
            "head",
            split_axis=1,
            concat_axis=0,
            tiled=True,
        ),
        lax.all_to_all(
            value.reshape(tok_rows, groups, head_cols),
            "head",
            split_axis=1,
            concat_axis=0,
            tiled=True,
        ),
        lax.all_to_all(
            grad_out.reshape(tok_rows, groups, head_cols),
            "head",
            split_axis=1,
            concat_axis=0,
            tiled=True,
        ),
    )
    shard_rows = groups * tok_rows
    query_s = moved[0].reshape(shard_rows, head_cols)
    key_s = moved[1].reshape(shard_rows, head_cols)
    value_s = moved[2].reshape(shard_rows, head_cols)
    grad_s = moved[3].reshape(shard_rows, head_cols)
    paired = jnp.concatenate([key_s, value_s], axis=1)
    cycle_len = lax.axis_size("ctx")
    position = lax.axis_index("ctx")
    blocks_shard = shard_rows // BLK
    all_blocks = blocks_shard * cycle_len
    fetched = {}
    offsets_all = list(range(1, REACH + 1)) + [-offset for offset in range(1, REACH + 1)]
    for offset in offsets_all:
        fetched[offset] = passed_along(paired, "ctx", offset)
    ordered = (
        [fetched[REACH - place] for place in range(REACH)]
        + [paired]
        + [fetched[-(place + 1)] for place in range(REACH)]
    )
    span_shards = 2 * REACH + 1
    window = jnp.concatenate(ordered, axis=0).reshape(
        span_shards * blocks_shard, BLK, 2 * head_cols
    )
    rows_nbr = lax.dynamic_slice_in_dim(neighbour, position * blocks_shard, blocks_shard, 0)
    local_idx = jnp.mod(rows_nbr - (position - REACH) * blocks_shard, all_blocks)
    used = lax.dynamic_slice_in_dim(counts, position * blocks_shard, blocks_shard, 0)
    per_group = group_rows(blocks_shard, BLK)
    turns = blocks_shard // per_group
    scale_factor = 1.0 / math.sqrt(E)
    query_g = query_s.reshape(turns, per_group, BLK, per_dev, E)
    grad_g = grad_s.reshape(turns, per_group, BLK, per_dev, E)
    index_g = local_idx.reshape(turns, per_group, NNB)
    used_g = used.reshape(turns, per_group)

    def one_group(totals, inputs):
        queries, cotangent, chosen, used_now = inputs
        selected = window[chosen]
        keys_sel = selected[..., :head_cols].reshape(per_group, NNB, BLK, per_dev, E)
        values_sel = selected[..., head_cols:].reshape(per_group, NNB, BLK, per_dev, E)
        usable = jnp.arange(NNB)[None, :] < used_now[:, None]
        allowed = usable[:, None, None, :, None]
        scores = (
            jnp.einsum("rihe,rjthe->rhijt", queries, keys_sel, preferred_element_type=jnp.float32)
            * scale_factor
        )
        masked = jnp.where(allowed, scores, -1e30)
        highest = jnp.max(masked, axis=(3, 4), keepdims=True)
        raised = jnp.where(allowed, jnp.exp(masked - highest), 0.0)
        total = jnp.sum(raised, axis=(3, 4), keepdims=True)
        probability = raised / total
        weights = probability.astype(jnp.bfloat16)
        out_rows = jnp.einsum(
            "rhijt,rjthe->rihe", weights, values_sel, preferred_element_type=jnp.float32
        ).astype(jnp.bfloat16)
        dprob = jnp.einsum(
            "rihe,rjthe->rhijt", cotangent, values_sel, preferred_element_type=jnp.float32
        )
        row_delta = jnp.sum(probability * dprob, axis=(3, 4), keepdims=True)
        dscore = (probability * (dprob - row_delta) * scale_factor).astype(jnp.bfloat16)
        dquery = jnp.einsum(
            "rhijt,rjthe->rihe", dscore, keys_sel, preferred_element_type=jnp.float32
        ).astype(jnp.bfloat16)
        dkey_part = jnp.einsum(
            "rhijt,rihe->rjthe", dscore, queries, preferred_element_type=jnp.float32
        )
        dvalue_part = jnp.einsum(
            "rhijt,rihe->rjthe", weights, cotangent, preferred_element_type=jnp.float32
        )
        joined = jnp.concatenate(
            [
                dkey_part.reshape(per_group * NNB, BLK, head_cols),
                dvalue_part.reshape(per_group * NNB, BLK, head_cols),
            ],
            axis=-1,
        )
        totals = totals.at[chosen.reshape(-1)].add(joined)
        return (totals, (out_rows, dquery))

    start_grads = jnp.zeros((span_shards * blocks_shard, BLK, 2 * head_cols), jnp.float32)
    grads_window, results = lax.scan(one_group, start_grads, (query_g, grad_g, index_g, used_g))
    grads_window = grads_window.reshape(span_shards, shard_rows, 2 * head_cols)
    combined = grads_window[REACH]
    offsets_back = list(range(1, REACH + 1)) + [-offset for offset in range(1, REACH + 1)]
    for offset in offsets_back:
        combined = combined + passed_along(
            grads_window[REACH - offset].astype(jnp.bfloat16), "ctx", -offset
        ).astype(jnp.float32)
    combined = combined.astype(jnp.bfloat16)
    dkey_s = combined[:, :head_cols]
    dvalue_s = combined[:, head_cols:]
    out_s = results[0].reshape(shard_rows, head_cols)
    dquery_s = results[1].reshape(shard_rows, head_cols)
    back = (
        lax.all_to_all(
            out_s.reshape(shard_rows, 1, head_cols), "head", split_axis=0, concat_axis=1, tiled=True
        ),
        lax.all_to_all(
            dquery_s.reshape(shard_rows, 1, head_cols),
            "head",
            split_axis=0,
            concat_axis=1,
            tiled=True,
        ),
        lax.all_to_all(
            dkey_s.reshape(shard_rows, 1, head_cols),
            "head",
            split_axis=0,
            concat_axis=1,
            tiled=True,
        ),
        lax.all_to_all(
            dvalue_s.reshape(shard_rows, 1, head_cols),
            "head",
            split_axis=0,
            concat_axis=1,
            tiled=True,
        ),
    )
    width = groups * head_cols
    return (
        back[0].reshape(tok_rows, width),
        back[1].reshape(tok_rows, width),
        back[2].reshape(tok_rows, width),
        back[3].reshape(tok_rows, width),
    )


MESH_ID = pl.DeviceIdType.MESH
F32 = jnp.float32
BF16 = jnp.bfloat16
GROUP = 2
VMEM_BYTES = 20 * 1024 * 1024


def left_in_hbm(array):
    return pltpu.with_memory_space_constraint(array, pltpu.HBM)


def place_of():
    index = lax.axis_index("ctx") * lax.axis_size("head") + lax.axis_index("head")
    return lax.div(index, 2), lax.rem(index, 2)


def device_of(owner, side):
    n_head = lax.axis_size("head")
    index = 2 * owner + side
    return (lax.div(index, n_head), lax.rem(index, n_head))


def partners(pairs, owner, step):
    half = pairs // 2
    far = 1 - lax.div(step, half)
    base = lax.rem(lax.div(owner, half) + far, 2) * half
    low, turn = lax.rem(owner, half), lax.rem(step, half)
    return base + lax.rem(low + turn, half), base + lax.rem(low - turn + half, half)


def each_step(pairs, body):
    def one(step, carry):
        body(step)
        return carry

    lax.fori_loop(0, pairs // 2, one, 0)
    lax.fori_loop(pairs // 2 + 1, pairs, one, 0)


def greet(pairs):
    owner, side = place_of()
    barrier = pltpu.get_barrier_semaphore()
    pl.semaphore_signal(barrier, inc=1, device_id=device_of(owner, 1 - side), device_id_type=MESH_ID)

    def one(step):
        to, _ = partners(pairs, owner, step)
        pl.semaphore_signal(barrier, inc=1, device_id=device_of(to, side), device_id_type=MESH_ID)

    each_step(pairs, one)
    return barrier


def spread_kernel(
    pairs, query, key, value, grad_out, qd, kv, kvt, own_rows, send_qd, send_kv,
    load, qd_out, qd_in, kv_out, kv_in, share_out, share_in,
):
    owner, side = place_of()
    loads = [
        pltpu.make_async_copy(array, own_rows.at[place], load.at[place])
        for place, array in enumerate((key, value, query, grad_out))
    ]
    for copy in loads:
        copy.start()
    barrier = greet(pairs)

    def pack(first, pieces):
        loads[first].wait()
        loads[first + 1].wait()
        for pair in range(pairs // 2):
            cols = slice(2 * E * pair, 2 * E * (pair + 1))
            a = own_rows[first, :, cols]
            b = own_rows[first + 1, :, cols]
            pieces[2 * pair] = jnp.concatenate([a[:, :E], b[:, :E]], axis=1)
            pieces[2 * pair + 1] = jnp.concatenate([a[:, E:], b[:, E:]], axis=1)

    def kv_copy(step, to, source):
        return pltpu.make_async_remote_copy(
            src_ref=send_kv.at[to],
            dst_ref=kv.at[2 * source + side],
            send_sem=kv_out.at[step],
            recv_sem=kv_in.at[step],
            device_id=device_of(to, side),
            device_id_type=MESH_ID,
        )

    def qd_copy(step, to, source):
        return pltpu.make_async_remote_copy(
            src_ref=send_qd.at[to],
            dst_ref=qd.at[source],
            send_sem=qd_out.at[step],
            recv_sem=qd_in.at[step],
            device_id=device_of(to, side),
            device_id_type=MESH_ID,
        )

    def share_copy(step, source, whose):
        return pltpu.make_async_remote_copy(
            src_ref=kv.at[2 * source + side],
            dst_ref=kv.at[2 * source + whose],
            send_sem=share_out.at[step],
            recv_sem=share_in.at[step],
            device_id=device_of(owner, 1 - side),
            device_id_type=MESH_ID,
        )

    def send_keys(step):
        to, _ = partners(pairs, owner, step)
        kv_copy(step, to, owner).start()

    def send_queries(step):
        to, _ = partners(pairs, owner, step)
        qd_copy(step, to, owner).start()

    pack(0, send_kv)
    pl.semaphore_wait(barrier, pairs)
    each_step(pairs, send_keys)
    pack(2, send_qd)
    each_step(pairs, send_queries)
    mine = 2 * owner + side
    kv[mine] = send_kv[owner]
    qd[owner] = send_qd[owner]
    share_copy(pairs // 2, owner, side).start()
    kvt[mine] = kv[mine].T

    def pass_on(step):
        _, source = partners(pairs, owner, step)
        kv_copy(step, owner, source).wait_recv()
        share_copy(step, source, side).start()
        kvt[2 * source + side] = kv[2 * source + side].T

    def take_share(step):
        _, source = partners(pairs, owner, step)
        share_copy(step, source, side).wait_send()
        share_copy(step, source, 1 - side).wait_recv()
        kvt[2 * source + 1 - side] = kv[2 * source + 1 - side].T

    def finish(step):
        to, source = partners(pairs, owner, step)
        qd_copy(step, owner, source).wait_recv()
        qd_copy(step, to, owner).wait_send()
        kv_copy(step, to, owner).wait_send()

    each_step(pairs, pass_on)
    take_share(jnp.int32(pairs // 2))
    each_step(pairs, take_share)
    each_step(pairs, finish)


def attend_kernel(
    blocks, neighbour_hbm, counts_hbm, qd, kv, kvt, od, totals,
    neighbour, counts, starts, order, pair_scr, x_scr, load
):
    _, side = place_of()
    half = blocks // 2
    scale = 1.0 / math.sqrt(E)
    exp_scale = scale * math.log2(math.e)
    low = lax.broadcasted_iota(jnp.int32, (BLK, 2 * E), 1) < E
    top = lax.broadcasted_iota(jnp.int32, (2 * E, BLK), 0) < E
    names_copy = pltpu.make_async_copy(neighbour_hbm, neighbour, load.at[0])
    names_copy.start()
    counts_copy = pltpu.make_async_copy(counts_hbm, counts, load.at[1])
    counts_copy.start()

    def clear(block, carry):
        totals[block] = jnp.zeros((BLK, 2 * E), F32)
        return carry

    lax.fori_loop(0, blocks, clear, 0)
    names_copy.wait()
    counts_copy.wait()

    def folded(array, op):
        return op(array.reshape(BLK // 8, 8, BLK), axis=0)

    def sort_by_used():
        for used in range(NNB + 1):
            starts[used] = 0
        for place in range(half):
            used = counts[2 * place + side]
            starts[used - 1] = starts[used - 1] + 1
        for used in range(NNB - 1, -1, -1):
            starts[used] = starts[used] + starts[used + 1]
        for place in range(half):
            used = counts[2 * place + side]
            at = starts[used]
            order[at] = place
            starts[used] = at + 1

    def rows_with(places, used):
        group = range(len(places))
        blocks_now = [2 * place + side for place in places]
        names = [[neighbour[slot, block] for slot in range(used)] for block in blocks_now]
        valid = [[slot < counts[block] for slot in range(used)] for block in blocks_now]
        spread, ahead = [], []
        for place in places:
            both = qd[place]
            zero = jnp.zeros_like(both)
            upper = jnp.where(low, both, zero)
            lower = jnp.where(low, zero, both)
            spread.append(jnp.concatenate([upper, lower], axis=0))
            ahead.append(jnp.concatenate([upper, lower * jnp.asarray(scale, BF16)], axis=0))
        highest = [None for _ in group]
        for slot in range(used):
            for one in group:
                result = lax.dot_general(
                    kv[names[one][slot]],
                    ahead[one],
                    (((1,), (1,)), ((), ())),
                    preferred_element_type=F32,
                )
                pair_scr[one, slot] = result
                part = folded(result[:, :BLK], jnp.max)
                if one > 0 and slot > 0:
                    part = jnp.where(valid[one][slot], part, -jnp.inf)
                highest[one] = part if slot == 0 else jnp.maximum(highest[one], part)
        highest = [jnp.max(part, axis=0, keepdims=True) for part in highest]
        total = [jnp.zeros((8, BLK), F32) for _ in group]
        delta = [jnp.zeros((8, BLK), F32) for _ in group]
        for slot in range(used):
            for one in group:
                raised = jnp.exp2((pair_scr[one, slot, :, :BLK] - highest[one]) * exp_scale)
                if one > 0 and slot > 0:
                    raised = jnp.where(valid[one][slot], raised, 0.0)
                pair_scr[one, slot, :, :BLK] = raised
                total[one] = total[one] + folded(raised, jnp.sum)
                delta[one] = delta[one] + folded(raised * pair_scr[one, slot, :, BLK:], jnp.sum)
        inverse = [1.0 / jnp.sum(part, axis=0, keepdims=True) for part in total]
        delta = [jnp.sum(delta[one], axis=0, keepdims=True) * inverse[one] for one in group]
        for slot in range(used):
            for one in group:
                probability = pair_scr[one, slot, :, :BLK] * inverse[one]
                dscore = probability * (pair_scr[one, slot, :, BLK:] - delta[one])
                x_scr[one, slot] = jnp.concatenate(
                    [dscore.astype(BF16), probability.astype(BF16)], axis=1
                )
        for one in group:
            rows = jnp.zeros((2 * E, 2 * BLK), F32)
            for slot in range(0, used, 2):
                if slot + 1 < used:
                    keys_t = jnp.concatenate(
                        [kvt[names[one][slot]], kvt[names[one][slot + 1]]], axis=1
                    )
                    grads = jnp.concatenate([x_scr[one, slot], x_scr[one, slot + 1]], axis=0)
                else:
                    keys_t = kvt[names[one][slot]]
                    grads = x_scr[one, slot]
                rows = rows + jnp.dot(keys_t, grads, preferred_element_type=F32)
            od[places[one]] = jnp.where(top, rows[:, :BLK], rows[:, BLK:]).T.astype(BF16)
        for slot in range(used):
            for one in group:
                totals[names[one][slot]] += jnp.dot(
                    x_scr[one, slot], spread[one], preferred_element_type=F32
                )

    def one_group(turn, carry):
        places = [order[GROUP * turn + one] for one in range(GROUP)]
        used_now = counts[2 * places[0] + side]
        for used in range(1, NNB + 1):
            pl.when(used_now == used)(functools.partial(rows_with, places, used))
        return carry

    sort_by_used()
    lax.fori_loop(0, half // GROUP, one_group, 0)


def collect_kernel(
    pairs, od, totals, got_od, got_kv, other, shared, send_kv,
    od_out, od_in, kv_out, kv_in, share_out, share_in,
):
    owner, side = place_of()
    barrier = greet(pairs)

    def share_copy(step, place):
        return pltpu.make_async_remote_copy(
            src_ref=other.at[place],
            dst_ref=shared.at[place],
            send_sem=share_out.at[step],
            recv_sem=share_in.at[step],
            device_id=device_of(owner, 1 - side),
            device_id_type=MESH_ID,
        )

    def od_copy(step, to, source):
        return pltpu.make_async_remote_copy(
            src_ref=od.at[to],
            dst_ref=got_od.at[source],
            send_sem=od_out.at[step],
            recv_sem=od_in.at[step],
            device_id=device_of(to, side),
            device_id_type=MESH_ID,
        )

    def kv_copy(step, to, source):
        return pltpu.make_async_remote_copy(
            src_ref=send_kv.at[to],
            dst_ref=got_kv.at[source],
            send_sem=kv_out.at[step],
            recv_sem=kv_in.at[step],
            device_id=device_of(to, side),
            device_id_type=MESH_ID,
        )

    def narrow(place, carry):
        other[place] = totals[2 * place + 1 - side].astype(BF16)
        return carry

    lax.fori_loop(0, pairs, narrow, 0)
    pl.semaphore_wait(barrier, pairs)

    def start_all(step):
        to, _ = partners(pairs, owner, step)
        od_copy(step, to, owner).start()
        share_copy(step, to).start()

    def summed(place):
        return (totals[2 * place + side] + shared[place].astype(F32)).astype(BF16)

    def add_and_send(step):
        to, _ = partners(pairs, owner, step)
        share_copy(step, to).wait_recv()
        send_kv[to] = summed(to)
        kv_copy(step, to, owner).start()

    def finish(step):
        to, source = partners(pairs, owner, step)
        od_copy(step, owner, source).wait_recv()
        kv_copy(step, owner, source).wait_recv()
        od_copy(step, to, owner).wait_send()
        kv_copy(step, to, owner).wait_send()
        share_copy(step, to).wait_send()

    each_step(pairs, start_all)
    share_copy(pairs // 2, owner).start()
    each_step(pairs, add_and_send)
    share_copy(pairs // 2, owner).wait_recv()
    got_kv[owner] = summed(owner)
    got_od[owner] = od[owner]
    each_step(pairs, finish)
    share_copy(pairs // 2, owner).wait_send()


def join_kernel(pairs, got_od, got_kv, out, dquery, dkey, dvalue, rows, store):
    copies = []
    for place, (pieces, part, array) in enumerate(
        ((got_od, 1, out), (got_od, 0, dquery), (got_kv, 0, dkey), (got_kv, 1, dvalue))
    ):
        cut = slice(part * E, (part + 1) * E)
        for pair in range(pairs // 2):
            cols = slice(2 * E * pair, 2 * E * (pair + 1))
            rows[place, :, cols] = jnp.concatenate(
                [pieces[2 * pair][:, cut], pieces[2 * pair + 1][:, cut]], axis=1
            )
        copies.append(pltpu.make_async_copy(rows.at[place], array, store.at[place]))
        copies[-1].start()
    for copy in copies:
        copy.wait()


def on_device_whole(query, key, value, grad_out, neighbour, counts):
    pairs = lax.axis_size("ctx") * lax.axis_size("head") // 2
    blocks = 2 * pairs
    width = query.shape[1]
    in_vmem = pl.BlockSpec(memory_space=pltpu.VMEM)
    in_hbm = pl.BlockSpec(memory_space=pltpu.HBM)
    many = pltpu.SemaphoreType.DMA((pairs,))
    piece = (BLK, 2 * E)
    own_pieces = jax.ShapeDtypeStruct((pairs, *piece), BF16)
    all_pieces = jax.ShapeDtypeStruct((blocks, *piece), BF16)
    with jax.named_scope("spread_heads"):
        qd, kv, kvt = pl.pallas_call(
            functools.partial(spread_kernel, pairs),
            out_shape=tuple(pltpu.VMEM((count, *piece), BF16) for count in (pairs, blocks, blocks)),
            in_specs=[in_hbm] * 4,
            out_specs=(in_vmem,) * 3,
            scratch_shapes=[pltpu.VMEM((4, BLK, width), BF16)]
            + [pltpu.VMEM((pairs, *piece), BF16)] * 2
            + [pltpu.SemaphoreType.DMA((4,))]
            + [many] * 6,
            compiler_params=pltpu.CompilerParams(
                collective_id=0, has_side_effects=True, vmem_limit_bytes=VMEM_BYTES
            ),
        )(*map(left_in_hbm, (query, key, value, grad_out)))
    with jax.named_scope("block_attention"):
        od, totals = pl.pallas_call(
            functools.partial(attend_kernel, blocks),
            out_shape=(own_pieces, jax.ShapeDtypeStruct((blocks, *piece), F32)),
            in_specs=[in_hbm] * 2 + [in_vmem] * 3,
            out_specs=(in_vmem,) * 2,
            scratch_shapes=[
                pltpu.SMEM(neighbour.shape[::-1], jnp.int32),
                pltpu.SMEM(counts.shape, jnp.int32),
                pltpu.SMEM((NNB + 1,), jnp.int32),
                pltpu.SMEM((pairs,), jnp.int32),
                pltpu.VMEM((GROUP, NNB, BLK, 2 * BLK), F32),
                pltpu.VMEM((GROUP, NNB, BLK, 2 * BLK), BF16),
                pltpu.SemaphoreType.DMA((2,)),
            ],
            compiler_params=pltpu.CompilerParams(vmem_limit_bytes=VMEM_BYTES),
        )(left_in_hbm(neighbour.T), left_in_hbm(counts), qd, kv, kvt)
    with jax.named_scope("collect_heads"):
        got_od, got_kv = pl.pallas_call(
            functools.partial(collect_kernel, pairs),
            out_shape=(own_pieces,) * 2,
            in_specs=[in_vmem] * 2,
            out_specs=(in_vmem,) * 2,
            scratch_shapes=[pltpu.VMEM((pairs, *piece), BF16)] * 3 + [many] * 6,
            compiler_params=pltpu.CompilerParams(
                collective_id=1, has_side_effects=True, vmem_limit_bytes=VMEM_BYTES
            ),
        )(od, totals)
    with jax.named_scope("join_heads"):
        return pl.pallas_call(
            functools.partial(join_kernel, pairs),
            out_shape=(jax.ShapeDtypeStruct((BLK, width), BF16),) * 4,
            in_specs=[in_vmem] * 2,
            out_specs=(in_hbm,) * 4,
            scratch_shapes=[
                pltpu.VMEM((4, BLK, width), BF16),
                pltpu.SemaphoreType.DMA((4,)),
            ],
            compiler_params=pltpu.CompilerParams(vmem_limit_bytes=VMEM_BYTES),
        )(got_od, got_kv)


def on_device(query, key, value, grad_out, neighbour, counts):
    devices = lax.axis_size("ctx") * lax.axis_size("head")
    if devices == 2 * H and H % GROUP == 0 and query.shape == (BLK, H * E) and counts.shape[0] == devices:
        return on_device_whole(query, key, value, grad_out, neighbour, counts)
    return on_device_windowed(query, key, value, grad_out, neighbour, counts)


def solution(mesh):
    return jax.shard_map(
        on_device,
        mesh=mesh,
        in_specs=(
            P(("ctx", "head"), None),
            P(("ctx", "head"), None),
            P(("ctx", "head"), None),
            P(("ctx", "head"), None),
            P(),
            P(),
        ),
        out_specs=(
            P(("ctx", "head"), None),
            P(("ctx", "head"), None),
            P(("ctx", "head"), None),
            P(("ctx", "head"), None),
        ),
        check_vma=False,
    )
```

```python
import functools
import math

import jax
import jax.numpy as jnp
from jax import lax
from jax.experimental import pallas as pl
from jax.experimental.pallas import tpu as pltpu
from jax.sharding import PartitionSpec as P

H = 16
E = 64
BLK = 128
NNB = 8
REACH = 2


def passed_along(value, axis, steps):
    count = lax.axis_size(axis)
    pairs = [(source, (source + steps) % count) for source in range(count)]
    return lax.ppermute(value, axis, pairs)


def group_rows(blocks_shard, block_len):
    limit = max(512 // block_len, 1)
    best = 1
    for candidate in range(1, blocks_shard + 1):
        if blocks_shard % candidate == 0 and candidate <= limit:
            best = candidate
    return best


def on_device_windowed(query, key, value, grad_out, neighbour, counts):
    tok_rows = query.shape[0]
    groups = lax.axis_size("head")
    per_dev = H // groups
    head_cols = per_dev * E
    moved = (
        lax.all_to_all(
            query.reshape(tok_rows, groups, head_cols),
            "head",
            split_axis=1,
            concat_axis=0,
            tiled=True,
        ),
        lax.all_to_all(
            key.reshape(tok_rows, groups, head_cols),
            "head",
            split_axis=1,
            concat_axis=0,
            tiled=True,
        ),
        lax.all_to_all(
            value.reshape(tok_rows, groups, head_cols),
            "head",
            split_axis=1,
            concat_axis=0,
            tiled=True,
        ),
        lax.all_to_all(
            grad_out.reshape(tok_rows, groups, head_cols),
            "head",
            split_axis=1,
            concat_axis=0,
            tiled=True,
        ),
    )
    shard_rows = groups * tok_rows
    query_s = moved[0].reshape(shard_rows, head_cols)
    key_s = moved[1].reshape(shard_rows, head_cols)
    value_s = moved[2].reshape(shard_rows, head_cols)
    grad_s = moved[3].reshape(shard_rows, head_cols)
    paired = jnp.concatenate([key_s, value_s], axis=1)
    cycle_len = lax.axis_size("ctx")
    position = lax.axis_index("ctx")
    blocks_shard = shard_rows // BLK
    all_blocks = blocks_shard * cycle_len
    fetched = {}
    offsets_all = list(range(1, REACH + 1)) + [-offset for offset in range(1, REACH + 1)]
    for offset in offsets_all:
        fetched[offset] = passed_along(paired, "ctx", offset)
    ordered = (
        [fetched[REACH - place] for place in range(REACH)]
        + [paired]
        + [fetched[-(place + 1)] for place in range(REACH)]
    )
    span_shards = 2 * REACH + 1
    window = jnp.concatenate(ordered, axis=0).reshape(
        span_shards * blocks_shard, BLK, 2 * head_cols
    )
    rows_nbr = lax.dynamic_slice_in_dim(neighbour, position * blocks_shard, blocks_shard, 0)
    local_idx = jnp.mod(rows_nbr - (position - REACH) * blocks_shard, all_blocks)
    used = lax.dynamic_slice_in_dim(counts, position * blocks_shard, blocks_shard, 0)
    per_group = group_rows(blocks_shard, BLK)
    turns = blocks_shard // per_group
    scale_factor = 1.0 / math.sqrt(E)
    query_g = query_s.reshape(turns, per_group, BLK, per_dev, E)
    grad_g = grad_s.reshape(turns, per_group, BLK, per_dev, E)
    index_g = local_idx.reshape(turns, per_group, NNB)
    used_g = used.reshape(turns, per_group)

    def one_group(totals, inputs):
        queries, cotangent, chosen, used_now = inputs
        selected = window[chosen]
        keys_sel = selected[..., :head_cols].reshape(per_group, NNB, BLK, per_dev, E)
        values_sel = selected[..., head_cols:].reshape(per_group, NNB, BLK, per_dev, E)
        usable = jnp.arange(NNB)[None, :] < used_now[:, None]
        allowed = usable[:, None, None, :, None]
        scores = (
            jnp.einsum("rihe,rjthe->rhijt", queries, keys_sel, preferred_element_type=jnp.float32)
            * scale_factor
        )
        masked = jnp.where(allowed, scores, -1e30)
        highest = jnp.max(masked, axis=(3, 4), keepdims=True)
        raised = jnp.where(allowed, jnp.exp(masked - highest), 0.0)
        total = jnp.sum(raised, axis=(3, 4), keepdims=True)
        probability = raised / total
        weights = probability.astype(jnp.bfloat16)
        out_rows = jnp.einsum(
            "rhijt,rjthe->rihe", weights, values_sel, preferred_element_type=jnp.float32
        ).astype(jnp.bfloat16)
        dprob = jnp.einsum(
            "rihe,rjthe->rhijt", cotangent, values_sel, preferred_element_type=jnp.float32
        )
        row_delta = jnp.sum(probability * dprob, axis=(3, 4), keepdims=True)
        dscore = (probability * (dprob - row_delta) * scale_factor).astype(jnp.bfloat16)
        dquery = jnp.einsum(
            "rhijt,rjthe->rihe", dscore, keys_sel, preferred_element_type=jnp.float32
        ).astype(jnp.bfloat16)
        dkey_part = jnp.einsum(
            "rhijt,rihe->rjthe", dscore, queries, preferred_element_type=jnp.float32
        )
        dvalue_part = jnp.einsum(
            "rhijt,rihe->rjthe", weights, cotangent, preferred_element_type=jnp.float32
        )
        joined = jnp.concatenate(
            [
                dkey_part.reshape(per_group * NNB, BLK, head_cols),
                dvalue_part.reshape(per_group * NNB, BLK, head_cols),
            ],
            axis=-1,
        )
        totals = totals.at[chosen.reshape(-1)].add(joined)
        return (totals, (out_rows, dquery))

    start_grads = jnp.zeros((span_shards * blocks_shard, BLK, 2 * head_cols), jnp.float32)
    grads_window, results = lax.scan(one_group, start_grads, (query_g, grad_g, index_g, used_g))
    grads_window = grads_window.reshape(span_shards, shard_rows, 2 * head_cols)
    combined = grads_window[REACH]
    offsets_back = list(range(1, REACH + 1)) + [-offset for offset in range(1, REACH + 1)]
    for offset in offsets_back:
        combined = combined + passed_along(
            grads_window[REACH - offset].astype(jnp.bfloat16), "ctx", -offset
        ).astype(jnp.float32)
    combined = combined.astype(jnp.bfloat16)
    dkey_s = combined[:, :head_cols]
    dvalue_s = combined[:, head_cols:]
    out_s = results[0].reshape(shard_rows, head_cols)
    dquery_s = results[1].reshape(shard_rows, head_cols)
    back = (
        lax.all_to_all(
            out_s.reshape(shard_rows, 1, head_cols), "head", split_axis=0, concat_axis=1, tiled=True
        ),
        lax.all_to_all(
            dquery_s.reshape(shard_rows, 1, head_cols),
            "head",
            split_axis=0,
            concat_axis=1,
            tiled=True,
        ),
        lax.all_to_all(
            dkey_s.reshape(shard_rows, 1, head_cols),
            "head",
            split_axis=0,
            concat_axis=1,
            tiled=True,
        ),
        lax.all_to_all(
            dvalue_s.reshape(shard_rows, 1, head_cols),
            "head",
            split_axis=0,
            concat_axis=1,
            tiled=True,
        ),
    )
    width = groups * head_cols
    return (
        back[0].reshape(tok_rows, width),
        back[1].reshape(tok_rows, width),
        back[2].reshape(tok_rows, width),
        back[3].reshape(tok_rows, width),
    )


MESH_ID = pl.DeviceIdType.MESH
F32 = jnp.float32
BF16 = jnp.bfloat16
GROUP = 4
VMEM_BYTES = 20 * 1024 * 1024


def left_in_hbm(array):
    return pltpu.with_memory_space_constraint(array, pltpu.HBM)


def place_of():
    index = lax.axis_index("ctx") * lax.axis_size("head") + lax.axis_index("head")
    return lax.div(index, 2), lax.rem(index, 2)


def device_of(owner, side):
    n_head = lax.axis_size("head")
    index = 2 * owner + side
    return (lax.div(index, n_head), lax.rem(index, n_head))


def partners(pairs, owner, step):
    half = pairs // 2
    far = 1 - lax.div(step, half)
    base = lax.rem(lax.div(owner, half) + far, 2) * half
    low, turn = lax.rem(owner, half), lax.rem(step, half)
    return base + lax.rem(low + turn, half), base + lax.rem(low - turn + half, half)


def each_step(pairs, body):
    def one(step, carry):
        body(step)
        return carry

    lax.fori_loop(0, pairs // 2, one, 0)
    lax.fori_loop(pairs // 2 + 1, pairs, one, 0)


def greet(pairs):
    owner, side = place_of()
    barrier = pltpu.get_barrier_semaphore()
    pl.semaphore_signal(barrier, inc=1, device_id=device_of(owner, 1 - side), device_id_type=MESH_ID)

    def one(step):
        to, _ = partners(pairs, owner, step)
        pl.semaphore_signal(barrier, inc=1, device_id=device_of(to, side), device_id_type=MESH_ID)

    each_step(pairs, one)
    return barrier


def spread_kernel(
    pairs, query, key, value, grad_out, qd, kv, kvt, own_rows, send_qd, send_kv,
    load, qd_out, qd_in, kv_out, kv_in, share_out, share_in,
):
    owner, side = place_of()
    loads = [
        pltpu.make_async_copy(array, own_rows.at[place], load.at[place])
        for place, array in enumerate((key, value, query, grad_out))
    ]
    for copy in loads:
        copy.start()
    barrier = greet(pairs)

    def pack(first, pieces):
        loads[first].wait()
        loads[first + 1].wait()
        for pair in range(pairs // 2):
            cols = slice(2 * E * pair, 2 * E * (pair + 1))
            a = own_rows[first, :, cols]
            b = own_rows[first + 1, :, cols]
            pieces[2 * pair] = jnp.concatenate([a[:, :E], b[:, :E]], axis=1)
            pieces[2 * pair + 1] = jnp.concatenate([a[:, E:], b[:, E:]], axis=1)

    def kv_copy(step, to, source):
        return pltpu.make_async_remote_copy(
            src_ref=send_kv.at[to],
            dst_ref=kv.at[2 * source + side],
            send_sem=kv_out.at[step],
            recv_sem=kv_in.at[step],
            device_id=device_of(to, side),
            device_id_type=MESH_ID,
        )

    def qd_copy(step, to, source):
        return pltpu.make_async_remote_copy(
            src_ref=send_qd.at[to],
            dst_ref=qd.at[source],
            send_sem=qd_out.at[step],
            recv_sem=qd_in.at[step],
            device_id=device_of(to, side),
            device_id_type=MESH_ID,
        )

    def share_copy(step, source, whose):
        return pltpu.make_async_remote_copy(
            src_ref=kv.at[2 * source + side],
            dst_ref=kv.at[2 * source + whose],
            send_sem=share_out.at[step],
            recv_sem=share_in.at[step],
            device_id=device_of(owner, 1 - side),
            device_id_type=MESH_ID,
        )

    def send_keys(step):
        to, _ = partners(pairs, owner, step)
        kv_copy(step, to, owner).start()

    def send_queries(step):
        to, _ = partners(pairs, owner, step)
        qd_copy(step, to, owner).start()

    pack(0, send_kv)
    pl.semaphore_wait(barrier, pairs)
    each_step(pairs, send_keys)
    pack(2, send_qd)
    each_step(pairs, send_queries)
    mine = 2 * owner + side
    kv[mine] = send_kv[owner]
    qd[owner] = send_qd[owner]
    share_copy(pairs // 2, owner, side).start()
    kvt[mine] = kv[mine].T

    def pass_on(step):
        _, source = partners(pairs, owner, step)
        kv_copy(step, owner, source).wait_recv()
        share_copy(step, source, side).start()
        kvt[2 * source + side] = kv[2 * source + side].T

    def take_share(step):
        _, source = partners(pairs, owner, step)
        share_copy(step, source, side).wait_send()
        share_copy(step, source, 1 - side).wait_recv()
        kvt[2 * source + 1 - side] = kv[2 * source + 1 - side].T

    def finish(step):
        to, source = partners(pairs, owner, step)
        qd_copy(step, owner, source).wait_recv()
        qd_copy(step, to, owner).wait_send()
        kv_copy(step, to, owner).wait_send()

    each_step(pairs, pass_on)
    take_share(jnp.int32(pairs // 2))
    each_step(pairs, take_share)
    each_step(pairs, finish)


def attend_kernel(
    blocks, neighbour_hbm, counts_hbm, qd, kv, kvt, od, totals,
    neighbour, counts, starts, order, pair_scr, x_scr, load
):
    _, side = place_of()
    half = blocks // 2
    scale = 1.0 / math.sqrt(E)
    exp_scale = scale * math.log2(math.e)
    low = lax.broadcasted_iota(jnp.int32, (BLK, 2 * E), 1) < E
    top = lax.broadcasted_iota(jnp.int32, (2 * E, BLK), 0) < E
    names_copy = pltpu.make_async_copy(neighbour_hbm, neighbour, load.at[0])
    names_copy.start()
    counts_copy = pltpu.make_async_copy(counts_hbm, counts, load.at[1])
    counts_copy.start()

    def clear(block, carry):
        totals[block] = jnp.zeros((BLK, 2 * E), F32)
        return carry

    lax.fori_loop(0, blocks, clear, 0)
    names_copy.wait()
    counts_copy.wait()

    def folded(array, op):
        return op(array.reshape(BLK // 8, 8, BLK), axis=0)

    def sort_by_used():
        for used in range(NNB + 1):
            starts[used] = 0
        for place in range(half):
            used = counts[2 * place + side]
            starts[used - 1] = starts[used - 1] + 1
        for used in range(NNB - 1, -1, -1):
            starts[used] = starts[used] + starts[used + 1]
        for place in range(half):
            used = counts[2 * place + side]
            at = starts[used]
            order[at] = place
            starts[used] = at + 1

    def rows_with(places, used):
        group = range(len(places))
        blocks_now = [2 * place + side for place in places]
        names = [[neighbour[slot, block] for slot in range(used)] for block in blocks_now]
        valid = [[slot < counts[block] for slot in range(used)] for block in blocks_now]
        spread, ahead = [], []
        for place in places:
            both = qd[place]
            zero = jnp.zeros_like(both)
            upper = jnp.where(low, both, zero)
            lower = jnp.where(low, zero, both)
            spread.append(jnp.concatenate([upper, lower], axis=0))
            ahead.append(jnp.concatenate([upper, lower * jnp.asarray(scale, BF16)], axis=0))
        highest = [None for _ in group]
        for slot in range(used):
            for one in group:
                result = lax.dot_general(
                    kv[names[one][slot]],
                    ahead[one],
                    (((1,), (1,)), ((), ())),
                    preferred_element_type=F32,
                )
                pair_scr[one, slot] = result
                part = folded(result[:, :BLK], jnp.max)
                if one > 0 and slot > 0:
                    part = jnp.where(valid[one][slot], part, -jnp.inf)
                highest[one] = part if slot == 0 else jnp.maximum(highest[one], part)
        highest = [jnp.max(part, axis=0, keepdims=True) for part in highest]
        total = [jnp.zeros((8, BLK), F32) for _ in group]
        delta = [jnp.zeros((8, BLK), F32) for _ in group]
        for slot in range(used):
            for one in group:
                raised = jnp.exp2((pair_scr[one, slot, :, :BLK] - highest[one]) * exp_scale)
                if one > 0 and slot > 0:
                    raised = jnp.where(valid[one][slot], raised, 0.0)
                pair_scr[one, slot, :, :BLK] = raised
                total[one] = total[one] + folded(raised, jnp.sum)
                delta[one] = delta[one] + folded(raised * pair_scr[one, slot, :, BLK:], jnp.sum)
        inverse = [1.0 / jnp.sum(part, axis=0, keepdims=True) for part in total]
        delta = [jnp.sum(delta[one], axis=0, keepdims=True) * inverse[one] for one in group]
        for slot in range(used):
            for one in group:
                probability = pair_scr[one, slot, :, :BLK] * inverse[one]
                dscore = probability * (pair_scr[one, slot, :, BLK:] - delta[one])
                x_scr[one, slot] = jnp.concatenate(
                    [dscore.astype(BF16), probability.astype(BF16)], axis=1
                )
        for one in group:
            rows = jnp.zeros((2 * E, 2 * BLK), F32)
            for slot in range(0, used, 2):
                if slot + 1 < used:
                    keys_t = jnp.concatenate(
                        [kvt[names[one][slot]], kvt[names[one][slot + 1]]], axis=1
                    )
                    grads = jnp.concatenate([x_scr[one, slot], x_scr[one, slot + 1]], axis=0)
                else:
                    keys_t = kvt[names[one][slot]]
                    grads = x_scr[one, slot]
                rows = rows + jnp.dot(keys_t, grads, preferred_element_type=F32)
            od[places[one]] = jnp.where(top, rows[:, :BLK], rows[:, BLK:]).T.astype(BF16)
        for slot in range(used):
            for one in group:
                totals[names[one][slot]] += jnp.dot(
                    x_scr[one, slot], spread[one], preferred_element_type=F32
                )

    def one_group(turn, carry):
        places = [order[GROUP * turn + one] for one in range(GROUP)]
        used_now = counts[2 * places[0] + side]
        for used in range(1, NNB + 1):
            pl.when(used_now == used)(functools.partial(rows_with, places, used))
        return carry

    sort_by_used()
    lax.fori_loop(0, half // GROUP, one_group, 0)


def collect_kernel(
    pairs, od, totals, got_od, got_kv, other, shared, send_kv,
    od_out, od_in, kv_out, kv_in, share_out, share_in,
):
    owner, side = place_of()
    barrier = greet(pairs)

    def share_copy(step, place):
        return pltpu.make_async_remote_copy(
            src_ref=other.at[place],
            dst_ref=shared.at[place],
            send_sem=share_out.at[step],
            recv_sem=share_in.at[step],
            device_id=device_of(owner, 1 - side),
            device_id_type=MESH_ID,
        )

    def od_copy(step, to, source):
        return pltpu.make_async_remote_copy(
            src_ref=od.at[to],
            dst_ref=got_od.at[source],
            send_sem=od_out.at[step],
            recv_sem=od_in.at[step],
            device_id=device_of(to, side),
            device_id_type=MESH_ID,
        )

    def kv_copy(step, to, source):
        return pltpu.make_async_remote_copy(
            src_ref=send_kv.at[to],
            dst_ref=got_kv.at[source],
            send_sem=kv_out.at[step],
            recv_sem=kv_in.at[step],
            device_id=device_of(to, side),
            device_id_type=MESH_ID,
        )

    def narrow(place, carry):
        other[place] = totals[2 * place + 1 - side].astype(BF16)
        return carry

    lax.fori_loop(0, pairs, narrow, 0)
    pl.semaphore_wait(barrier, pairs)

    def start_all(step):
        to, _ = partners(pairs, owner, step)
        od_copy(step, to, owner).start()
        share_copy(step, to).start()

    def summed(place):
        return (totals[2 * place + side] + shared[place].astype(F32)).astype(BF16)

    def add_and_send(step):
        to, _ = partners(pairs, owner, step)
        share_copy(step, to).wait_recv()
        send_kv[to] = summed(to)
        kv_copy(step, to, owner).start()

    def finish(step):
        to, source = partners(pairs, owner, step)
        od_copy(step, owner, source).wait_recv()
        kv_copy(step, owner, source).wait_recv()
        od_copy(step, to, owner).wait_send()
        kv_copy(step, to, owner).wait_send()
        share_copy(step, to).wait_send()

    each_step(pairs, start_all)
    share_copy(pairs // 2, owner).start()
    each_step(pairs, add_and_send)
    share_copy(pairs // 2, owner).wait_recv()
    got_kv[owner] = summed(owner)
    got_od[owner] = od[owner]
    each_step(pairs, finish)
    share_copy(pairs // 2, owner).wait_send()


def join_kernel(pairs, got_od, got_kv, out, dquery, dkey, dvalue, rows, store):
    copies = []
    for place, (pieces, part, array) in enumerate(
        ((got_od, 1, out), (got_od, 0, dquery), (got_kv, 0, dkey), (got_kv, 1, dvalue))
    ):
        cut = slice(part * E, (part + 1) * E)
        for pair in range(pairs // 2):
            cols = slice(2 * E * pair, 2 * E * (pair + 1))
            rows[place, :, cols] = jnp.concatenate(
                [pieces[2 * pair][:, cut], pieces[2 * pair + 1][:, cut]], axis=1
            )
        copies.append(pltpu.make_async_copy(rows.at[place], array, store.at[place]))
        copies[-1].start()
    for copy in copies:
        copy.wait()


def on_device_whole(query, key, value, grad_out, neighbour, counts):
    pairs = lax.axis_size("ctx") * lax.axis_size("head") // 2
    blocks = 2 * pairs
    width = query.shape[1]
    in_vmem = pl.BlockSpec(memory_space=pltpu.VMEM)
    in_hbm = pl.BlockSpec(memory_space=pltpu.HBM)
    many = pltpu.SemaphoreType.DMA((pairs,))
    piece = (BLK, 2 * E)
    own_pieces = jax.ShapeDtypeStruct((pairs, *piece), BF16)
    all_pieces = jax.ShapeDtypeStruct((blocks, *piece), BF16)
    with jax.named_scope("spread_heads"):
        qd, kv, kvt = pl.pallas_call(
            functools.partial(spread_kernel, pairs),
            out_shape=tuple(pltpu.VMEM((count, *piece), BF16) for count in (pairs, blocks, blocks)),
            in_specs=[in_hbm] * 4,
            out_specs=(in_vmem,) * 3,
            scratch_shapes=[pltpu.VMEM((4, BLK, width), BF16)]
            + [pltpu.VMEM((pairs, *piece), BF16)] * 2
            + [pltpu.SemaphoreType.DMA((4,))]
            + [many] * 6,
            compiler_params=pltpu.CompilerParams(
                collective_id=0, has_side_effects=True, vmem_limit_bytes=VMEM_BYTES
            ),
        )(*map(left_in_hbm, (query, key, value, grad_out)))
    with jax.named_scope("block_attention"):
        od, totals = pl.pallas_call(
            functools.partial(attend_kernel, blocks),
            out_shape=(own_pieces, jax.ShapeDtypeStruct((blocks, *piece), F32)),
            in_specs=[in_hbm] * 2 + [in_vmem] * 3,
            out_specs=(in_vmem,) * 2,
            scratch_shapes=[
                pltpu.SMEM(neighbour.shape[::-1], jnp.int32),
                pltpu.SMEM(counts.shape, jnp.int32),
                pltpu.SMEM((NNB + 1,), jnp.int32),
                pltpu.SMEM((pairs,), jnp.int32),
                pltpu.VMEM((GROUP, NNB, BLK, 2 * BLK), F32),
                pltpu.VMEM((GROUP, NNB, BLK, 2 * BLK), BF16),
                pltpu.SemaphoreType.DMA((2,)),
            ],
            compiler_params=pltpu.CompilerParams(vmem_limit_bytes=VMEM_BYTES),
        )(left_in_hbm(neighbour.T), left_in_hbm(counts), qd, kv, kvt)
    with jax.named_scope("collect_heads"):
        got_od, got_kv = pl.pallas_call(
            functools.partial(collect_kernel, pairs),
            out_shape=(own_pieces,) * 2,
            in_specs=[in_vmem] * 2,
            out_specs=(in_vmem,) * 2,
            scratch_shapes=[pltpu.VMEM((pairs, *piece), BF16)] * 3 + [many] * 6,
            compiler_params=pltpu.CompilerParams(
                collective_id=1, has_side_effects=True, vmem_limit_bytes=VMEM_BYTES
            ),
        )(od, totals)
    with jax.named_scope("join_heads"):
        return pl.pallas_call(
            functools.partial(join_kernel, pairs),
            out_shape=(jax.ShapeDtypeStruct((BLK, width), BF16),) * 4,
            in_specs=[in_vmem] * 2,
            out_specs=(in_hbm,) * 4,
            scratch_shapes=[
                pltpu.VMEM((4, BLK, width), BF16),
                pltpu.SemaphoreType.DMA((4,)),
            ],
            compiler_params=pltpu.CompilerParams(vmem_limit_bytes=VMEM_BYTES),
        )(got_od, got_kv)


def on_device(query, key, value, grad_out, neighbour, counts):
    devices = lax.axis_size("ctx") * lax.axis_size("head")
    if devices == 2 * H and H % GROUP == 0 and query.shape == (BLK, H * E) and counts.shape[0] == devices:
        return on_device_whole(query, key, value, grad_out, neighbour, counts)
    return on_device_windowed(query, key, value, grad_out, neighbour, counts)


def solution(mesh):
    return jax.shard_map(
        on_device,
        mesh=mesh,
        in_specs=(
            P(("ctx", "head"), None),
            P(("ctx", "head"), None),
            P(("ctx", "head"), None),
            P(("ctx", "head"), None),
            P(),
            P(),
        ),
        out_specs=(
            P(("ctx", "head"), None),
            P(("ctx", "head"), None),
            P(("ctx", "head"), None),
            P(("ctx", "head"), None),
        ),
        check_vma=False,
    )
```

```python
import functools
import math

import jax
import jax.numpy as jnp
from jax import lax
from jax.experimental import pallas as pl
from jax.experimental.pallas import tpu as pltpu
from jax.sharding import PartitionSpec as P

H = 16
E = 64
BLK = 128
NNB = 8
REACH = 2


def passed_along(value, axis, steps):
    count = lax.axis_size(axis)
    pairs = [(source, (source + steps) % count) for source in range(count)]
    return lax.ppermute(value, axis, pairs)


def group_rows(blocks_shard, block_len):
    limit = max(512 // block_len, 1)
    best = 1
    for candidate in range(1, blocks_shard + 1):
        if blocks_shard % candidate == 0 and candidate <= limit:
            best = candidate
    return best


def on_device_windowed(query, key, value, grad_out, neighbour, counts):
    tok_rows = query.shape[0]
    groups = lax.axis_size("head")
    per_dev = H // groups
    head_cols = per_dev * E
    moved = (
        lax.all_to_all(
            query.reshape(tok_rows, groups, head_cols),
            "head",
            split_axis=1,
            concat_axis=0,
            tiled=True,
        ),
        lax.all_to_all(
            key.reshape(tok_rows, groups, head_cols),
            "head",
            split_axis=1,
            concat_axis=0,
            tiled=True,
        ),
        lax.all_to_all(
            value.reshape(tok_rows, groups, head_cols),
            "head",
            split_axis=1,
            concat_axis=0,
            tiled=True,
        ),
        lax.all_to_all(
            grad_out.reshape(tok_rows, groups, head_cols),
            "head",
            split_axis=1,
            concat_axis=0,
            tiled=True,
        ),
    )
    shard_rows = groups * tok_rows
    query_s = moved[0].reshape(shard_rows, head_cols)
    key_s = moved[1].reshape(shard_rows, head_cols)
    value_s = moved[2].reshape(shard_rows, head_cols)
    grad_s = moved[3].reshape(shard_rows, head_cols)
    paired = jnp.concatenate([key_s, value_s], axis=1)
    cycle_len = lax.axis_size("ctx")
    position = lax.axis_index("ctx")
    blocks_shard = shard_rows // BLK
    all_blocks = blocks_shard * cycle_len
    fetched = {}
    offsets_all = list(range(1, REACH + 1)) + [-offset for offset in range(1, REACH + 1)]
    for offset in offsets_all:
        fetched[offset] = passed_along(paired, "ctx", offset)
    ordered = (
        [fetched[REACH - place] for place in range(REACH)]
        + [paired]
        + [fetched[-(place + 1)] for place in range(REACH)]
    )
    span_shards = 2 * REACH + 1
    window = jnp.concatenate(ordered, axis=0).reshape(
        span_shards * blocks_shard, BLK, 2 * head_cols
    )
    rows_nbr = lax.dynamic_slice_in_dim(neighbour, position * blocks_shard, blocks_shard, 0)
    local_idx = jnp.mod(rows_nbr - (position - REACH) * blocks_shard, all_blocks)
    used = lax.dynamic_slice_in_dim(counts, position * blocks_shard, blocks_shard, 0)
    per_group = group_rows(blocks_shard, BLK)
    turns = blocks_shard // per_group
    scale_factor = 1.0 / math.sqrt(E)
    query_g = query_s.reshape(turns, per_group, BLK, per_dev, E)
    grad_g = grad_s.reshape(turns, per_group, BLK, per_dev, E)
    index_g = local_idx.reshape(turns, per_group, NNB)
    used_g = used.reshape(turns, per_group)

    def one_group(totals, inputs):
        queries, cotangent, chosen, used_now = inputs
        selected = window[chosen]
        keys_sel = selected[..., :head_cols].reshape(per_group, NNB, BLK, per_dev, E)
        values_sel = selected[..., head_cols:].reshape(per_group, NNB, BLK, per_dev, E)
        usable = jnp.arange(NNB)[None, :] < used_now[:, None]
        allowed = usable[:, None, None, :, None]
        scores = (
            jnp.einsum("rihe,rjthe->rhijt", queries, keys_sel, preferred_element_type=jnp.float32)
            * scale_factor
        )
        masked = jnp.where(allowed, scores, -1e30)
        highest = jnp.max(masked, axis=(3, 4), keepdims=True)
        raised = jnp.where(allowed, jnp.exp(masked - highest), 0.0)
        total = jnp.sum(raised, axis=(3, 4), keepdims=True)
        probability = raised / total
        weights = probability.astype(jnp.bfloat16)
        out_rows = jnp.einsum(
            "rhijt,rjthe->rihe", weights, values_sel, preferred_element_type=jnp.float32
        ).astype(jnp.bfloat16)
        dprob = jnp.einsum(
            "rihe,rjthe->rhijt", cotangent, values_sel, preferred_element_type=jnp.float32
        )
        row_delta = jnp.sum(probability * dprob, axis=(3, 4), keepdims=True)
        dscore = (probability * (dprob - row_delta) * scale_factor).astype(jnp.bfloat16)
        dquery = jnp.einsum(
            "rhijt,rjthe->rihe", dscore, keys_sel, preferred_element_type=jnp.float32
        ).astype(jnp.bfloat16)
        dkey_part = jnp.einsum(
            "rhijt,rihe->rjthe", dscore, queries, preferred_element_type=jnp.float32
        )
        dvalue_part = jnp.einsum(
            "rhijt,rihe->rjthe", weights, cotangent, preferred_element_type=jnp.float32
        )
        joined = jnp.concatenate(
            [
                dkey_part.reshape(per_group * NNB, BLK, head_cols),
                dvalue_part.reshape(per_group * NNB, BLK, head_cols),
            ],
            axis=-1,
        )
        totals = totals.at[chosen.reshape(-1)].add(joined)
        return (totals, (out_rows, dquery))

    start_grads = jnp.zeros((span_shards * blocks_shard, BLK, 2 * head_cols), jnp.float32)
    grads_window, results = lax.scan(one_group, start_grads, (query_g, grad_g, index_g, used_g))
    grads_window = grads_window.reshape(span_shards, shard_rows, 2 * head_cols)
    combined = grads_window[REACH]
    offsets_back = list(range(1, REACH + 1)) + [-offset for offset in range(1, REACH + 1)]
    for offset in offsets_back:
        combined = combined + passed_along(
            grads_window[REACH - offset].astype(jnp.bfloat16), "ctx", -offset
        ).astype(jnp.float32)
    combined = combined.astype(jnp.bfloat16)
    dkey_s = combined[:, :head_cols]
    dvalue_s = combined[:, head_cols:]
    out_s = results[0].reshape(shard_rows, head_cols)
    dquery_s = results[1].reshape(shard_rows, head_cols)
    back = (
        lax.all_to_all(
            out_s.reshape(shard_rows, 1, head_cols), "head", split_axis=0, concat_axis=1, tiled=True
        ),
        lax.all_to_all(
            dquery_s.reshape(shard_rows, 1, head_cols),
            "head",
            split_axis=0,
            concat_axis=1,
            tiled=True,
        ),
        lax.all_to_all(
            dkey_s.reshape(shard_rows, 1, head_cols),
            "head",
            split_axis=0,
            concat_axis=1,
            tiled=True,
        ),
        lax.all_to_all(
            dvalue_s.reshape(shard_rows, 1, head_cols),
            "head",
            split_axis=0,
            concat_axis=1,
            tiled=True,
        ),
    )
    width = groups * head_cols
    return (
        back[0].reshape(tok_rows, width),
        back[1].reshape(tok_rows, width),
        back[2].reshape(tok_rows, width),
        back[3].reshape(tok_rows, width),
    )


MESH_ID = pl.DeviceIdType.MESH
F32 = jnp.float32
BF16 = jnp.bfloat16
GROUP = 2
VMEM_BYTES = 20 * 1024 * 1024


def left_in_hbm(array):
    return pltpu.with_memory_space_constraint(array, pltpu.HBM)


def place_of():
    index = lax.axis_index("ctx") * lax.axis_size("head") + lax.axis_index("head")
    return lax.div(index, 2), lax.rem(index, 2)


def device_of(owner, side):
    n_head = lax.axis_size("head")
    index = 2 * owner + side
    return (lax.div(index, n_head), lax.rem(index, n_head))


def partners(pairs, owner, step):
    half = pairs // 2
    far = 1 - lax.div(step, half)
    base = lax.rem(lax.div(owner, half) + far, 2) * half
    low, turn = lax.rem(owner, half), lax.rem(step, half)
    return base + lax.rem(low + turn, half), base + lax.rem(low - turn + half, half)


def each_step(pairs, body):
    def one(step, carry):
        body(step)
        return carry

    lax.fori_loop(0, pairs // 2, one, 0)
    lax.fori_loop(pairs // 2 + 1, pairs, one, 0)


def greet(pairs):
    owner, side = place_of()
    barrier = pltpu.get_barrier_semaphore()
    pl.semaphore_signal(barrier, inc=1, device_id=device_of(owner, 1 - side), device_id_type=MESH_ID)

    def one(step):
        to, _ = partners(pairs, owner, step)
        pl.semaphore_signal(barrier, inc=1, device_id=device_of(to, side), device_id_type=MESH_ID)

    each_step(pairs, one)
    return barrier


def spread_kernel(
    pairs, query, key, value, grad_out, qd, kv, kvt, own_rows, send_qd, send_kv,
    load, qd_out, qd_in, kv_out, kv_in, share_out, share_in,
):
    owner, side = place_of()
    loads = [
        pltpu.make_async_copy(array, own_rows.at[place], load.at[place])
        for place, array in enumerate((key, value, query, grad_out))
    ]
    for copy in loads:
        copy.start()
    barrier = greet(pairs)

    def pack(first, pieces):
        loads[first].wait()
        loads[first + 1].wait()
        for pair in range(pairs // 2):
            cols = slice(2 * E * pair, 2 * E * (pair + 1))
            a = own_rows[first, :, cols]
            b = own_rows[first + 1, :, cols]
            pieces[2 * pair] = jnp.concatenate([a[:, :E], b[:, :E]], axis=1)
            pieces[2 * pair + 1] = jnp.concatenate([a[:, E:], b[:, E:]], axis=1)

    def kv_copy(step, to, source):
        return pltpu.make_async_remote_copy(
            src_ref=send_kv.at[to],
            dst_ref=kv.at[2 * source + side],
            send_sem=kv_out.at[step],
            recv_sem=kv_in.at[step],
            device_id=device_of(to, side),
            device_id_type=MESH_ID,
        )

    def qd_copy(step, to, source):
        return pltpu.make_async_remote_copy(
            src_ref=send_qd.at[to],
            dst_ref=qd.at[source],
            send_sem=qd_out.at[step],
            recv_sem=qd_in.at[step],
            device_id=device_of(to, side),
            device_id_type=MESH_ID,
        )

    def share_copy(step, source, whose):
        return pltpu.make_async_remote_copy(
            src_ref=kv.at[2 * source + side],
            dst_ref=kv.at[2 * source + whose],
            send_sem=share_out.at[step],
            recv_sem=share_in.at[step],
            device_id=device_of(owner, 1 - side),
            device_id_type=MESH_ID,
        )

    def send_keys(step):
        to, _ = partners(pairs, owner, step)
        kv_copy(step, to, owner).start()

    def send_queries(step):
        to, _ = partners(pairs, owner, step)
        qd_copy(step, to, owner).start()

    pack(0, send_kv)
    pl.semaphore_wait(barrier, pairs)
    each_step(pairs, send_keys)
    pack(2, send_qd)
    each_step(pairs, send_queries)
    mine = 2 * owner + side
    kv[mine] = send_kv[owner]
    qd[owner] = send_qd[owner]
    share_copy(pairs // 2, owner, side).start()
    kvt[mine] = kv[mine].T

    def pass_on(step):
        _, source = partners(pairs, owner, step)
        kv_copy(step, owner, source).wait_recv()
        share_copy(step, source, side).start()
        kvt[2 * source + side] = kv[2 * source + side].T

    def take_share(step):
        _, source = partners(pairs, owner, step)
        share_copy(step, source, side).wait_send()
        share_copy(step, source, 1 - side).wait_recv()
        kvt[2 * source + 1 - side] = kv[2 * source + 1 - side].T

    def finish(step):
        to, source = partners(pairs, owner, step)
        qd_copy(step, owner, source).wait_recv()
        qd_copy(step, to, owner).wait_send()
        kv_copy(step, to, owner).wait_send()

    each_step(pairs, pass_on)
    take_share(jnp.int32(pairs // 2))
    each_step(pairs, take_share)
    each_step(pairs, finish)


def attend_kernel(
    blocks, neighbour_hbm, counts_hbm, qd, kv, kvt, od, totals,
    neighbour, counts, starts, order, pair_scr, x_scr, load
):
    _, side = place_of()
    half = blocks // 2
    scale = 1.0 / math.sqrt(E)
    exp_scale = scale * math.log2(math.e)
    low = lax.broadcasted_iota(jnp.int32, (BLK, 2 * E), 1) < E
    top = lax.broadcasted_iota(jnp.int32, (2 * E, BLK), 0) < E
    names_copy = pltpu.make_async_copy(neighbour_hbm, neighbour, load.at[0])
    names_copy.start()
    counts_copy = pltpu.make_async_copy(counts_hbm, counts, load.at[1])
    counts_copy.start()

    def clear(block, carry):
        totals[block] = jnp.zeros((BLK, 2 * E), F32)
        return carry

    lax.fori_loop(0, blocks, clear, 0)
    names_copy.wait()
    counts_copy.wait()

    def folded(array, op):
        return op(array.reshape(BLK // 8, 8, BLK), axis=0)

    def sort_by_used():
        for used in range(NNB + 1):
            starts[used] = 0
        for place in range(half):
            used = counts[2 * place + side]
            starts[used - 1] = starts[used - 1] + 1
        for used in range(NNB - 1, -1, -1):
            starts[used] = starts[used] + starts[used + 1]
        for place in range(half):
            used = counts[2 * place + side]
            at = starts[used]
            order[at] = place
            starts[used] = at + 1

    def rows_with(places, used):
        group = range(len(places))
        blocks_now = [2 * place + side for place in places]
        names = [[neighbour[slot, block] for slot in range(used)] for block in blocks_now]
        valid = [[slot < counts[block] for slot in range(used)] for block in blocks_now]
        spread, ahead = [], []
        for place in places:
            both = qd[place]
            zero = jnp.zeros_like(both)
            upper = jnp.where(low, both, zero)
            lower = jnp.where(low, zero, both)
            spread.append(jnp.concatenate([upper, lower], axis=0))
            ahead.append(jnp.concatenate([upper, lower * jnp.asarray(scale, BF16)], axis=0))
        highest = [None for _ in group]
        for one in group:
            keys = jnp.concatenate([kv[name] for name in names[one]], axis=0)
            result = lax.dot_general(
                keys, ahead[one], (((1,), (1,)), ((), ())), preferred_element_type=F32
            ).reshape(used, BLK, 2 * BLK)
            for slot in range(used):
                pair_scr[one, slot] = result[slot]
                part = folded(result[slot, :, :BLK], jnp.max)
                if one > 0 and slot > 0:
                    part = jnp.where(valid[one][slot], part, -jnp.inf)
                highest[one] = part if slot == 0 else jnp.maximum(highest[one], part)
        highest = [jnp.max(part, axis=0, keepdims=True) for part in highest]
        total = [jnp.zeros((8, BLK), F32) for _ in group]
        delta = [jnp.zeros((8, BLK), F32) for _ in group]
        for slot in range(used):
            for one in group:
                raised = jnp.exp2((pair_scr[one, slot, :, :BLK] - highest[one]) * exp_scale)
                if one > 0 and slot > 0:
                    raised = jnp.where(valid[one][slot], raised, 0.0)
                pair_scr[one, slot, :, :BLK] = raised
                total[one] = total[one] + folded(raised, jnp.sum)
                delta[one] = delta[one] + folded(raised * pair_scr[one, slot, :, BLK:], jnp.sum)
        inverse = [1.0 / jnp.sum(part, axis=0, keepdims=True) for part in total]
        delta = [jnp.sum(delta[one], axis=0, keepdims=True) * inverse[one] for one in group]
        for slot in range(used):
            for one in group:
                probability = pair_scr[one, slot, :, :BLK] * inverse[one]
                dscore = probability * (pair_scr[one, slot, :, BLK:] - delta[one])
                x_scr[one, slot] = jnp.concatenate(
                    [dscore.astype(BF16), probability.astype(BF16)], axis=1
                )
        for one in group:
            rows = jnp.zeros((2 * E, 2 * BLK), F32)
            for slot in range(0, used, 2):
                if slot + 1 < used:
                    keys_t = jnp.concatenate(
                        [kvt[names[one][slot]], kvt[names[one][slot + 1]]], axis=1
                    )
                    grads = jnp.concatenate([x_scr[one, slot], x_scr[one, slot + 1]], axis=0)
                else:
                    keys_t = kvt[names[one][slot]]
                    grads = x_scr[one, slot]
                rows = rows + jnp.dot(keys_t, grads, preferred_element_type=F32)
            od[places[one]] = jnp.where(top, rows[:, :BLK], rows[:, BLK:]).T.astype(BF16)
        for one in group:
            grads = x_scr[one, :used].reshape(used * BLK, 2 * BLK)
            added = jnp.dot(grads, spread[one], preferred_element_type=F32)
            for slot in range(used):
                totals[names[one][slot]] += added[slot * BLK : (slot + 1) * BLK]

    def one_group(totals, inputs):
        queries, cotangent, chosen, used_now = inputs
        selected = window[chosen]
        keys_sel = selected[..., :head_cols].reshape(per_group, NNB, BLK, per_dev, E)
        values_sel = selected[..., head_cols:].reshape(per_group, NNB, BLK, per_dev, E)
        usable = jnp.arange(NNB)[None, :] < used_now[:, None]
        allowed = usable[:, None, None, :, None]
        scores = (
            jnp.einsum("rihe,rjthe->rhijt", queries, keys_sel, preferred_element_type=jnp.float32)
            * scale_factor
        )
        masked = jnp.where(allowed, scores, -1e30)
        highest = jnp.max(masked, axis=(3, 4), keepdims=True)
        raised = jnp.where(allowed, jnp.exp(masked - highest), 0.0)
        total = jnp.sum(raised, axis=(3, 4), keepdims=True)
        probability = raised / total
        weights = probability.astype(jnp.bfloat16)
        out_rows = jnp.einsum(
            "rhijt,rjthe->rihe", weights, values_sel, preferred_element_type=jnp.float32
        ).astype(jnp.bfloat16)
        dprob = jnp.einsum(
            "rihe,rjthe->rhijt", cotangent, values_sel, preferred_element_type=jnp.float32
        )
        row_delta = jnp.sum(probability * dprob, axis=(3, 4), keepdims=True)
        dscore = (probability * (dprob - row_delta) * scale_factor).astype(jnp.bfloat16)
        dquery = jnp.einsum(
            "rhijt,rjthe->rihe", dscore, keys_sel, preferred_element_type=jnp.float32
        ).astype(jnp.bfloat16)
        dkey_part = jnp.einsum(
            "rhijt,rihe->rjthe", dscore, queries, preferred_element_type=jnp.float32
        )
        dvalue_part = jnp.einsum(
            "rhijt,rihe->rjthe", weights, cotangent, preferred_element_type=jnp.float32
        )
        joined = jnp.concatenate(
            [
                dkey_part.reshape(per_group * NNB, BLK, head_cols),
                dvalue_part.reshape(per_group * NNB, BLK, head_cols),
            ],
            axis=-1,
        )
        totals = totals.at[chosen.reshape(-1)].add(joined)
        return (totals, (out_rows, dquery))

    start_grads = jnp.zeros((span_shards * blocks_shard, BLK, 2 * head_cols), jnp.float32)
    grads_window, results = lax.scan(one_group, start_grads, (query_g, grad_g, index_g, used_g))
    grads_window = grads_window.reshape(span_shards, shard_rows, 2 * head_cols)
    combined = grads_window[REACH]
    offsets_back = list(range(1, REACH + 1)) + [-offset for offset in range(1, REACH + 1)]
    for offset in offsets_back:
        combined = combined + passed_along(
            grads_window[REACH - offset].astype(jnp.bfloat16), "ctx", -offset
        ).astype(jnp.float32)
    combined = combined.astype(jnp.bfloat16)
    dkey_s = combined[:, :head_cols]
    dvalue_s = combined[:, head_cols:]
    out_s = results[0].reshape(shard_rows, head_cols)
    dquery_s = results[1].reshape(shard_rows, head_cols)
    back = (
        lax.all_to_all(
            out_s.reshape(shard_rows, 1, head_cols), "head", split_axis=0, concat_axis=1, tiled=True
        ),
        lax.all_to_all(
            dquery_s.reshape(shard_rows, 1, head_cols),
            "head",
            split_axis=0,
            concat_axis=1,
            tiled=True,
        ),
        lax.all_to_all(
            dkey_s.reshape(shard_rows, 1, head_cols),
            "head",
            split_axis=0,
            concat_axis=1,
            tiled=True,
        ),
        lax.all_to_all(
            dvalue_s.reshape(shard_rows, 1, head_cols),
            "head",
            split_axis=0,
            concat_axis=1,
            tiled=True,
        ),
    )
    width = groups * head_cols
    return (
        back[0].reshape(tok_rows, width),
        back[1].reshape(tok_rows, width),
        back[2].reshape(tok_rows, width),
        back[3].reshape(tok_rows, width),
    )


MESH_ID = pl.DeviceIdType.MESH
F32 = jnp.float32
BF16 = jnp.bfloat16
GROUP = 2
VMEM_BYTES = 20 * 1024 * 1024


def left_in_hbm(array):
    return pltpu.with_memory_space_constraint(array, pltpu.HBM)


def place_of():
    index = lax.axis_index("ctx") * lax.axis_size("head") + lax.axis_index("head")
    return lax.div(index, 2), lax.rem(index, 2)


def device_of(owner, side):
    n_head = lax.axis_size("head")
    index = 2 * owner + side
    return (lax.div(index, n_head), lax.rem(index, n_head))


def partners(pairs, owner, step):
    half = pairs // 2
    far = 1 - lax.div(step, half)
    base = lax.rem(lax.div(owner, half) + far, 2) * half
    low, turn = lax.rem(owner, half), lax.rem(step, half)
    return base + lax.rem(low + turn, half), base + lax.rem(low - turn + half, half)


def each_step(pairs, body):
    def one(step, carry):
        body(step)
        return carry

    lax.fori_loop(0, pairs // 2, one, 0)
    lax.fori_loop(pairs // 2 + 1, pairs, one, 0)


def greet(pairs):
    owner, side = place_of()
    barrier = pltpu.get_barrier_semaphore()
    pl.semaphore_signal(barrier, inc=1, device_id=device_of(owner, 1 - side), device_id_type=MESH_ID)

    def one(step):
        to, _ = partners(pairs, owner, step)
        pl.semaphore_signal(barrier, inc=1, device_id=device_of(to, side), device_id_type=MESH_ID)

    each_step(pairs, one)
    return barrier


def spread_kernel(
    pairs, query, key, value, grad_out, qd, kv, kvt, own_rows, send_qd, send_kv,
    load, qd_out, qd_in, kv_out, kv_in, share_out, share_in,
):
    owner, side = place_of()
    loads = [
        pltpu.make_async_copy(array, own_rows.at[place], load.at[place])
        for place, array in enumerate((key, value, query, grad_out))
    ]
    for copy in loads:
        copy.start()
    barrier = greet(pairs)

    def pack(first, pieces):
        loads[first].wait()
        loads[first + 1].wait()
        for pair in range(pairs // 2):
            cols = slice(2 * E * pair, 2 * E * (pair + 1))
            a = own_rows[first, :, cols]
            b = own_rows[first + 1, :, cols]
            pieces[2 * pair] = jnp.concatenate([a[:, :E], b[:, :E]], axis=1)
            pieces[2 * pair + 1] = jnp.concatenate([a[:, E:], b[:, E:]], axis=1)

    def kv_copy(step, to, source):
        return pltpu.make_async_remote_copy(
            src_ref=send_kv.at[to],
            dst_ref=kv.at[2 * source + side],
            send_sem=kv_out.at[step],
            recv_sem=kv_in.at[step],
            device_id=device_of(to, side),
            device_id_type=MESH_ID,
        )

    def qd_copy(step, to, source):
        return pltpu.make_async_remote_copy(
            src_ref=send_qd.at[to],
            dst_ref=qd.at[source],
            send_sem=qd_out.at[step],
            recv_sem=qd_in.at[step],
            device_id=device_of(to, side),
            device_id_type=MESH_ID,
        )

    def share_copy(step, source, whose):
        return pltpu.make_async_remote_copy(
            src_ref=kv.at[2 * source + side],
            dst_ref=kv.at[2 * source + whose],
            send_sem=share_out.at[step],
            recv_sem=share_in.at[step],
            device_id=device_of(owner, 1 - side),
            device_id_type=MESH_ID,
        )

    def send_keys(step):
        to, _ = partners(pairs, owner, step)
        kv_copy(step, to, owner).start()

    def send_queries(step):
        to, _ = partners(pairs, owner, step)
        qd_copy(step, to, owner).start()

    pack(0, send_kv)
    pl.semaphore_wait(barrier, pairs)
    each_step(pairs, send_keys)
    pack(2, send_qd)
    each_step(pairs, send_queries)
    mine = 2 * owner + side
    kv[mine] = send_kv[owner]
    qd[owner] = send_qd[owner]
    share_copy(pairs // 2, owner, side).start()
    kvt[mine] = kv[mine].T

    def pass_on(step):
        _, source = partners(pairs, owner, step)
        kv_copy(step, owner, source).wait_recv()
        share_copy(step, source, side).start()
        kvt[2 * source + side] = kv[2 * source + side].T

    def take_share(step):
        _, source = partners(pairs, owner, step)
        share_copy(step, source, side).wait_send()
        share_copy(step, source, 1 - side).wait_recv()
        kvt[2 * source + 1 - side] = kv[2 * source + 1 - side].T

    def finish(step):
        to, source = partners(pairs, owner, step)
        qd_copy(step, owner, source).wait_recv()
        qd_copy(step, to, owner).wait_send()
        kv_copy(step, to, owner).wait_send()

    each_step(pairs, pass_on)
    take_share(jnp.int32(pairs // 2))
    each_step(pairs, take_share)
    each_step(pairs, finish)


def attend_kernel(
    blocks, neighbour_hbm, counts_hbm, qd, kv, kvt, od, totals,
    neighbour, counts, starts, order, pair_scr, x_scr, load
):
    _, side = place_of()
    half = blocks // 2
    scale = 1.0 / math.sqrt(E)
    exp_scale = scale * math.log2(math.e)
    low = lax.broadcasted_iota(jnp.int32, (BLK, 2 * E), 1) < E
    top = lax.broadcasted_iota(jnp.int32, (2 * E, BLK), 0) < E
    names_copy = pltpu.make_async_copy(neighbour_hbm, neighbour, load.at[0])
    names_copy.start()
    counts_copy = pltpu.make_async_copy(counts_hbm, counts, load.at[1])
    counts_copy.start()

    def clear(block, carry):
        totals[block] = jnp.zeros((BLK, 2 * E), F32)
        return carry

    lax.fori_loop(0, blocks, clear, 0)
    names_copy.wait()
    counts_copy.wait()

    def folded(array, op):
        return op(array.reshape(BLK // 8, 8, BLK), axis=0)

    def sort_by_used():
        for used in range(NNB + 1):
            starts[used] = 0
        for place in range(half):
            used = counts[2 * place + side]
            starts[used - 1] = starts[used - 1] + 1
        for used in range(NNB - 1, -1, -1):
            starts[used] = starts[used] + starts[used + 1]
        for place in range(half):
            used = counts[2 * place + side]
            at = starts[used]
            order[at] = place
            starts[used] = at + 1

    def rows_with(places, used):
        group = range(len(places))
        blocks_now = [2 * place + side for place in places]
        names = [[neighbour[slot, block] for slot in range(used)] for block in blocks_now]
        valid = [[slot < counts[block] for slot in range(used)] for block in blocks_now]
        spread, ahead = [], []
        for place in places:
            both = qd[place]
            zero = jnp.zeros_like(both)
            upper = jnp.where(low, both, zero)
            lower = jnp.where(low, zero, both)
            spread.append(jnp.concatenate([upper, lower], axis=0))
            ahead.append(jnp.concatenate([upper, lower * jnp.asarray(scale, BF16)], axis=0))
        highest = [None for _ in group]
        for one in group:
            keys = jnp.concatenate([kv[name] for name in names[one]], axis=0)
            result = lax.dot_general(
                keys, ahead[one], (((1,), (1,)), ((), ())), preferred_element_type=F32
            ).reshape(used, BLK, 2 * BLK)
            for slot in range(used):
                pair_scr[one, slot] = result[slot]
                part = folded(result[slot, :, :BLK], jnp.max)
                if one > 0 and slot > 0:
                    part = jnp.where(valid[one][slot], part, -jnp.inf)
                highest[one] = part if slot == 0 else jnp.maximum(highest[one], part)
        highest = [jnp.max(part, axis=0, keepdims=True) for part in highest]
        total = [jnp.zeros((8, BLK), F32) for _ in group]
        delta = [jnp.zeros((8, BLK), F32) for _ in group]
        for slot in range(used):
            for one in group:
                raised = jnp.exp2((pair_scr[one, slot, :, :BLK] - highest[one]) * exp_scale)
                if one > 0 and slot > 0:
                    raised = jnp.where(valid[one][slot], raised, 0.0)
                pair_scr[one, slot, :, :BLK] = raised
                total[one] = total[one] + folded(raised, jnp.sum)
                delta[one] = delta[one] + folded(raised * pair_scr[one, slot, :, BLK:], jnp.sum)
        inverse = [1.0 / jnp.sum(part, axis=0, keepdims=True) for part in total]
        delta = [jnp.sum(delta[one], axis=0, keepdims=True) * inverse[one] for one in group]
        for slot in range(used):
            for one in group:
                probability = pair_scr[one, slot, :, :BLK] * inverse[one]
                dscore = probability * (pair_scr[one, slot, :, BLK:] - delta[one])
                x_scr[one, slot] = jnp.concatenate(
                    [dscore.astype(BF16), probability.astype(BF16)], axis=1
                )
        for one in group:
            rows = jnp.zeros((2 * E, 2 * BLK), F32)
            for slot in range(0, used, 2):
                if slot + 1 < used:
                    keys_t = jnp.concatenate(
                        [kvt[names[one][slot]], kvt[names[one][slot + 1]]], axis=1
                    )
                    grads = jnp.concatenate([x_scr[one, slot], x_scr[one, slot + 1]], axis=0)
                else:
                    keys_t = kvt[names[one][slot]]
                    grads = x_scr[one, slot]
                rows = rows + jnp.dot(keys_t, grads, preferred_element_type=F32)
            od[places[one]] = jnp.where(top, rows[:, :BLK], rows[:, BLK:]).T.astype(BF16)
        for slot in range(used):
            for one in group:
                totals[names[one][slot]] += jnp.dot(
                    x_scr[one, slot], spread[one], preferred_element_type=F32
                )

    def one_group(turn, carry):
        places = [order[GROUP * turn + one] for one in range(GROUP)]
        used_now = counts[2 * places[0] + side]
        for used in range(1, NNB + 1):
            pl.when(used_now == used)(functools.partial(rows_with, places, used))
        return carry

    sort_by_used()
    lax.fori_loop(0, half // GROUP, one_group, 0)


def collect_kernel(
    pairs, od, totals, got_od, got_kv, other, shared, send_kv,
    od_out, od_in, kv_out, kv_in, share_out, share_in,
):
    owner, side = place_of()
    barrier = greet(pairs)

    def share_copy(step, place):
        return pltpu.make_async_remote_copy(
            src_ref=other.at[place],
            dst_ref=shared.at[place],
            send_sem=share_out.at[step],
            recv_sem=share_in.at[step],
            device_id=device_of(owner, 1 - side),
            device_id_type=MESH_ID,
        )

    def od_copy(step, to, source):
        return pltpu.make_async_remote_copy(
            src_ref=od.at[to],
            dst_ref=got_od.at[source],
            send_sem=od_out.at[step],
            recv_sem=od_in.at[step],
            device_id=device_of(to, side),
            device_id_type=MESH_ID,
        )

    def kv_copy(step, to, source):
        return pltpu.make_async_remote_copy(
            src_ref=send_kv.at[to],
            dst_ref=got_kv.at[source],
            send_sem=kv_out.at[step],
            recv_sem=kv_in.at[step],
            device_id=device_of(to, side),
            device_id_type=MESH_ID,
        )

    def narrow(place, carry):
        other[place] = totals[2 * place + 1 - side].astype(BF16)
        return carry

    lax.fori_loop(0, pairs, narrow, 0)
    pl.semaphore_wait(barrier, pairs)

    def start_all(step):
        to, _ = partners(pairs, owner, step)
        od_copy(step, to, owner).start()
        share_copy(step, to).start()

    def summed(place):
        return (totals[2 * place + side] + shared[place].astype(F32)).astype(BF16)

    def add_and_send(step):
        to, _ = partners(pairs, owner, step)
        share_copy(step, to).wait_recv()
        send_kv[to] = summed(to)
        kv_copy(step, to, owner).start()

    def finish(step):
        to, source = partners(pairs, owner, step)
        od_copy(step, owner, source).wait_recv()
        kv_copy(step, owner, source).wait_recv()
        od_copy(step, to, owner).wait_send()
        kv_copy(step, to, owner).wait_send()
        share_copy(step, to).wait_send()

    each_step(pairs, start_all)
    share_copy(pairs // 2, owner).start()
    each_step(pairs, add_and_send)
    share_copy(pairs // 2, owner).wait_recv()
    got_kv[owner] = summed(owner)
    got_od[owner] = od[owner]
    each_step(pairs, finish)
    share_copy(pairs // 2, owner).wait_send()


def join_kernel(pairs, got_od, got_kv, out, dquery, dkey, dvalue, rows, store):
    copies = []
    for place, (pieces, part, array) in enumerate(
        ((got_od, 1, out), (got_od, 0, dquery), (got_kv, 0, dkey), (got_kv, 1, dvalue))
    ):
        cut = slice(part * E, (part + 1) * E)
        for pair in range(pairs // 2):
            cols = slice(2 * E * pair, 2 * E * (pair + 1))
            rows[place, :, cols] = jnp.concatenate(
                [pieces[2 * pair][:, cut], pieces[2 * pair + 1][:, cut]], axis=1
            )
        copies.append(pltpu.make_async_copy(rows.at[place], array, store.at[place]))
        copies[-1].start()
    for copy in copies:
        copy.wait()


def on_device_whole(query, key, value, grad_out, neighbour, counts):
    pairs = lax.axis_size("ctx") * lax.axis_size("head") // 2
    blocks = 2 * pairs
    width = query.shape[1]
    in_vmem = pl.BlockSpec(memory_space=pltpu.VMEM)
    in_hbm = pl.BlockSpec(memory_space=pltpu.HBM)
    many = pltpu.SemaphoreType.DMA((pairs,))
    piece = (BLK, 2 * E)
    own_pieces = jax.ShapeDtypeStruct((pairs, *piece), BF16)
    all_pieces = jax.ShapeDtypeStruct((blocks, *piece), BF16)
    with jax.named_scope("spread_heads"):
        qd, kv, kvt = pl.pallas_call(
            functools.partial(spread_kernel, pairs),
            out_shape=tuple(pltpu.VMEM((count, *piece), BF16) for count in (pairs, blocks, blocks)),
            in_specs=[in_hbm] * 4,
            out_specs=(in_vmem,) * 3,
            scratch_shapes=[pltpu.VMEM((4, BLK, width), BF16)]
            + [pltpu.VMEM((pairs, *piece), BF16)] * 2
            + [pltpu.SemaphoreType.DMA((4,))]
            + [many] * 6,
            compiler_params=pltpu.CompilerParams(
                collective_id=0, has_side_effects=True, vmem_limit_bytes=VMEM_BYTES
            ),
        )(*map(left_in_hbm, (query, key, value, grad_out)))
    with jax.named_scope("block_attention"):
        od, totals = pl.pallas_call(
            functools.partial(attend_kernel, blocks),
            out_shape=(own_pieces, jax.ShapeDtypeStruct((blocks, *piece), F32)),
            in_specs=[in_hbm] * 2 + [in_vmem] * 3,
            out_specs=(in_vmem,) * 2,
            scratch_shapes=[
                pltpu.SMEM(neighbour.shape[::-1], jnp.int32),
                pltpu.SMEM(counts.shape, jnp.int32),
                pltpu.SMEM((NNB + 1,), jnp.int32),
                pltpu.SMEM((pairs,), jnp.int32),
                pltpu.VMEM((GROUP, NNB, BLK, 2 * BLK), F32),
                pltpu.VMEM((GROUP, NNB, BLK, 2 * BLK), BF16),
                pltpu.SemaphoreType.DMA((2,)),
            ],
            compiler_params=pltpu.CompilerParams(vmem_limit_bytes=VMEM_BYTES),
        )(left_in_hbm(neighbour.T), left_in_hbm(counts), qd, kv, kvt)
    with jax.named_scope("collect_heads"):
        got_od, got_kv = pl.pallas_call(
            functools.partial(collect_kernel, pairs),
            out_shape=(own_pieces,) * 2,
            in_specs=[in_vmem] * 2,
            out_specs=(in_vmem,) * 2,
            scratch_shapes=[pltpu.VMEM((pairs, *piece), BF16)] * 3 + [many] * 6,
            compiler_params=pltpu.CompilerParams(
                collective_id=1, has_side_effects=True, vmem_limit_bytes=VMEM_BYTES
            ),
        )(od, totals)
    with jax.named_scope("join_heads"):
        return pl.pallas_call(
            functools.partial(join_kernel, pairs),
            out_shape=(jax.ShapeDtypeStruct((BLK, width), BF16),) * 4,
            in_specs=[in_vmem] * 2,
            out_specs=(in_hbm,) * 4,
            scratch_shapes=[
                pltpu.VMEM((4, BLK, width), BF16),
                pltpu.SemaphoreType.DMA((4,)),
            ],
            compiler_params=pltpu.CompilerParams(vmem_limit_bytes=VMEM_BYTES),
        )(got_od, got_kv)


def on_device(query, key, value, grad_out, neighbour, counts):
    devices = lax.axis_size("ctx") * lax.axis_size("head")
    if devices == 2 * H and H % GROUP == 0 and query.shape == (BLK, H * E) and counts.shape[0] == devices:
        return on_device_whole(query, key, value, grad_out, neighbour, counts)
    return on_device_windowed(query, key, value, grad_out, neighbour, counts)


def solution(mesh):
    return jax.shard_map(
        on_device,
        mesh=mesh,
        in_specs=(
            P(("ctx", "head"), None),
            P(("ctx", "head"), None),
            P(("ctx", "head"), None),
            P(("ctx", "head"), None),
            P(),
            P(),
        ),
        out_specs=(
            P(("ctx", "head"), None),
            P(("ctx", "head"), None),
            P(("ctx", "head"), None),
            P(("ctx", "head"), None),
        ),
        check_vma=False,
    )
```

```python
import functools
import math

import jax
import jax.numpy as jnp
from jax import lax
from jax.experimental import pallas as pl
from jax.experimental.pallas import tpu as pltpu
from jax.sharding import PartitionSpec as P

H = 16
E = 64
BLK = 128
NNB = 8
REACH = 2


def passed_along(value, axis, steps):
    count = lax.axis_size(axis)
    pairs = [(source, (source + steps) % count) for source in range(count)]
    return lax.ppermute(value, axis, pairs)


def group_rows(blocks_shard, block_len):
    limit = max(512 // block_len, 1)
    best = 1
    for candidate in range(1, blocks_shard + 1):
        if blocks_shard % candidate == 0 and candidate <= limit:
            best = candidate
    return best


def on_device_windowed(query, key, value, grad_out, neighbour, counts):
    tok_rows = query.shape[0]
    groups = lax.axis_size("head")
    per_dev = H // groups
    head_cols = per_dev * E
    moved = (
        lax.all_to_all(
            query.reshape(tok_rows, groups, head_cols),
            "head",
            split_axis=1,
            concat_axis=0,
            tiled=True,
        ),
        lax.all_to_all(
            key.reshape(tok_rows, groups, head_cols),
            "head",
            split_axis=1,
            concat_axis=0,
            tiled=True,
        ),
        lax.all_to_all(
            value.reshape(tok_rows, groups, head_cols),
            "head",
            split_axis=1,
            concat_axis=0,
            tiled=True,
        ),
        lax.all_to_all(
            grad_out.reshape(tok_rows, groups, head_cols),
            "head",
            split_axis=1,
            concat_axis=0,
            tiled=True,
        ),
    )
    shard_rows = groups * tok_rows
    query_s = moved[0].reshape(shard_rows, head_cols)
    key_s = moved[1].reshape(shard_rows, head_cols)
    value_s = moved[2].reshape(shard_rows, head_cols)
    grad_s = moved[3].reshape(shard_rows, head_cols)
    paired = jnp.concatenate([key_s, value_s], axis=1)
    cycle_len = lax.axis_size("ctx")
    position = lax.axis_index("ctx")
    blocks_shard = shard_rows // BLK
    all_blocks = blocks_shard * cycle_len
    fetched = {}
    offsets_all = list(range(1, REACH + 1)) + [-offset for offset in range(1, REACH + 1)]
    for offset in offsets_all:
        fetched[offset] = passed_along(paired, "ctx", offset)
    ordered = (
        [fetched[REACH - place] for place in range(REACH)]
        + [paired]
        + [fetched[-(place + 1)] for place in range(REACH)]
    )
    span_shards = 2 * REACH + 1
    window = jnp.concatenate(ordered, axis=0).reshape(
        span_shards * blocks_shard, BLK, 2 * head_cols
    )
    rows_nbr = lax.dynamic_slice_in_dim(neighbour, position * blocks_shard, blocks_shard, 0)
    local_idx = jnp.mod(rows_nbr - (position - REACH) * blocks_shard, all_blocks)
    used = lax.dynamic_slice_in_dim(counts, position * blocks_shard, blocks_shard, 0)
    per_group = group_rows(blocks_shard, BLK)
    turns = blocks_shard // per_group
    scale_factor = 1.0 / math.sqrt(E)
    query_g = query_s.reshape(turns, per_group, BLK, per_dev, E)
    grad_g = grad_s.reshape(turns, per_group, BLK, per_dev, E)
    index_g = local_idx.reshape(turns, per_group, NNB)
    used_g = used.reshape(turns, per_group)

    def one_group(totals, inputs):
        queries, cotangent, chosen, used_now = inputs
        selected = window[chosen]
        keys_sel = selected[..., :head_cols].reshape(per_group, NNB, BLK, per_dev, E)
        values_sel = selected[..., head_cols:].reshape(per_group, NNB, BLK, per_dev, E)
        usable = jnp.arange(NNB)[None, :] < used_now[:, None]
        allowed = usable[:, None, None, :, None]
        scores = (
            jnp.einsum("rihe,rjthe->rhijt", queries, keys_sel, preferred_element_type=jnp.float32)
            * scale_factor
        )
        masked = jnp.where(allowed, scores, -1e30)
        highest = jnp.max(masked, axis=(3, 4), keepdims=True)
        raised = jnp.where(allowed, jnp.exp(masked - highest), 0.0)
        total = jnp.sum(raised, axis=(3, 4), keepdims=True)
        probability = raised / total
        weights = probability.astype(jnp.bfloat16)
        out_rows = jnp.einsum(
            "rhijt,rjthe->rihe", weights, values_sel, preferred_element_type=jnp.float32
        ).astype(jnp.bfloat16)
        dprob = jnp.einsum(
            "rihe,rjthe->rhijt", cotangent, values_sel, preferred_element_type=jnp.float32
        )
        row_delta = jnp.sum(probability * dprob, axis=(3, 4), keepdims=True)
        dscore = (probability * (dprob - row_delta) * scale_factor).astype(jnp.bfloat16)
        dquery = jnp.einsum(
            "rhijt,rjthe->rihe", dscore, keys_sel, preferred_element_type=jnp.float32
        ).astype(jnp.bfloat16)
        dkey_part = jnp.einsum(
            "rhijt,rihe->rjthe", dscore, queries, preferred_element_type=jnp.float32
        )
        dvalue_part = jnp.einsum(
            "rhijt,rihe->rjthe", weights, cotangent, preferred_element_type=jnp.float32
        )
        joined = jnp.concatenate(
            [
                dkey_part.reshape(per_group * NNB, BLK, head_cols),
                dvalue_part.reshape(per_group * NNB, BLK, head_cols),
            ],
            axis=-1,
        )
        totals = totals.at[chosen.reshape(-1)].add(joined)
        return (totals, (out_rows, dquery))

    start_grads = jnp.zeros((span_shards * blocks_shard, BLK, 2 * head_cols), jnp.float32)
    grads_window, results = lax.scan(one_group, start_grads, (query_g, grad_g, index_g, used_g))
    grads_window = grads_window.reshape(span_shards, shard_rows, 2 * head_cols)
    combined = grads_window[REACH]
    offsets_back = list(range(1, REACH + 1)) + [-offset for offset in range(1, REACH + 1)]
    for offset in offsets_back:
        combined = combined + passed_along(
            grads_window[REACH - offset].astype(jnp.bfloat16), "ctx", -offset
        ).astype(jnp.float32)
    combined = combined.astype(jnp.bfloat16)
    dkey_s = combined[:, :head_cols]
    dvalue_s = combined[:, head_cols:]
    out_s = results[0].reshape(shard_rows, head_cols)
    dquery_s = results[1].reshape(shard_rows, head_cols)
    back = (
        lax.all_to_all(
            out_s.reshape(shard_rows, 1, head_cols), "head", split_axis=0, concat_axis=1, tiled=True
        ),
        lax.all_to_all(
            dquery_s.reshape(shard_rows, 1, head_cols),
            "head",
            split_axis=0,
            concat_axis=1,
            tiled=True,
        ),
        lax.all_to_all(
            dkey_s.reshape(shard_rows, 1, head_cols),
            "head",
            split_axis=0,
            concat_axis=1,
            tiled=True,
        ),
        lax.all_to_all(
            dvalue_s.reshape(shard_rows, 1, head_cols),
            "head",
            split_axis=0,
            concat_axis=1,
            tiled=True,
        ),
    )
    width = groups * head_cols
    return (
        back[0].reshape(tok_rows, width),
        back[1].reshape(tok_rows, width),
        back[2].reshape(tok_rows, width),
        back[3].reshape(tok_rows, width),
    )


MESH_ID = pl.DeviceIdType.MESH
F32 = jnp.float32
BF16 = jnp.bfloat16
GROUP = 2
VMEM_BYTES = 20 * 1024 * 1024


def left_in_hbm(array):
    return pltpu.with_memory_space_constraint(array, pltpu.HBM)


def place_of():
    index = lax.axis_index("ctx") * lax.axis_size("head") + lax.axis_index("head")
    return lax.div(index, 2), lax.rem(index, 2)


def device_of(owner, side):
    n_head = lax.axis_size("head")
    index = 2 * owner + side
    return (lax.div(index, n_head), lax.rem(index, n_head))


def partners(pairs, owner, step):
    half = pairs // 2
    far = 1 - lax.div(step, half)
    base = lax.rem(lax.div(owner, half) + far, 2) * half
    low, turn = lax.rem(owner, half), lax.rem(step, half)
    return base + lax.rem(low + turn, half), base + lax.rem(low - turn + half, half)


def run_steps(start, stop, body):
    def one(step, carry):
        body(step)
        return carry

    lax.fori_loop(start, stop, one, 0)


def far_steps(pairs, body):
    run_steps(0, pairs // 2, body)


def near_steps(pairs, body):
    run_steps(pairs // 2 + 1, pairs, body)


def each_step(pairs, body):
    far_steps(pairs, body)
    near_steps(pairs, body)


def greet(pairs):
    owner, side = place_of()
    barrier = pltpu.get_barrier_semaphore()
    pl.semaphore_signal(barrier, inc=1, device_id=device_of(owner, 1 - side), device_id_type=MESH_ID)

    def one(step):
        to, _ = partners(pairs, owner, step)
        pl.semaphore_signal(barrier, inc=1, device_id=device_of(to, side), device_id_type=MESH_ID)

    each_step(pairs, one)
    return barrier


def spread_kernel(
    pairs, query, key, value, grad_out, neighbour_hbm, counts_hbm, qd, kv, kvt, x_near, od_near,
    own_rows, send_qd, send_kv, neighbour, counts, pair_scr,
    load, qd_out, qd_in, kv_out, kv_in, share_out, share_in,
):
    owner, side = place_of()
    half = pairs // 2
    near = lax.div(owner, half) * half
    loads = [
        pltpu.make_async_copy(array, own_rows.at[place], load.at[place])
        for place, array in enumerate((key, value, query, grad_out))
    ]
    names_copy = pltpu.make_async_copy(neighbour_hbm, neighbour, load.at[4])
    counts_copy = pltpu.make_async_copy(counts_hbm, counts, load.at[5])
    for copy in loads + [names_copy, counts_copy]:
        copy.start()
    barrier = greet(pairs)

    def pack(first, pieces):
        loads[first].wait()
        loads[first + 1].wait()
        for pair in range(pairs // 2):
            cols = slice(2 * E * pair, 2 * E * (pair + 1))
            a = own_rows[first, :, cols]
            b = own_rows[first + 1, :, cols]
            pieces[2 * pair] = jnp.concatenate([a[:, :E], b[:, :E]], axis=1)
            pieces[2 * pair + 1] = jnp.concatenate([a[:, E:], b[:, E:]], axis=1)

    def kv_copy(step, to, source):
        return pltpu.make_async_remote_copy(
            src_ref=send_kv.at[to],
            dst_ref=kv.at[2 * source + side],
            send_sem=kv_out.at[step],
            recv_sem=kv_in.at[step],
            device_id=device_of(to, side),
            device_id_type=MESH_ID,
        )

    def qd_copy(step, to, source):
        return pltpu.make_async_remote_copy(
            src_ref=send_qd.at[to],
            dst_ref=qd.at[source],
            send_sem=qd_out.at[step],
            recv_sem=qd_in.at[step],
            device_id=device_of(to, side),
            device_id_type=MESH_ID,
        )

    def share_copy(step, source, whose):
        return pltpu.make_async_remote_copy(
            src_ref=kv.at[2 * source + side],
            dst_ref=kv.at[2 * source + whose],
            send_sem=share_out.at[step],
            recv_sem=share_in.at[step],
            device_id=device_of(owner, 1 - side),
            device_id_type=MESH_ID,
        )

    def send_keys(step):
        to, _ = partners(pairs, owner, step)
        kv_copy(step, to, owner).start()

    def send_queries(step):
        to, _ = partners(pairs, owner, step)
        qd_copy(step, to, owner).start()

    pack(0, send_kv)
    pl.semaphore_wait(barrier, pairs)
    each_step(pairs, send_keys)
    pack(2, send_qd)
    near_steps(pairs, send_queries)
    mine = 2 * owner + side
    kv[mine] = send_kv[owner]
    qd[owner] = send_qd[owner]
    share_copy(half, owner, side).start()
    kvt[mine] = kv[mine].T

    def pass_on(step):
        _, source = partners(pairs, owner, step)
        kv_copy(step, owner, source).wait_recv()
        share_copy(step, source, side).start()
        kvt[2 * source + side] = kv[2 * source + side].T

    def pass_on_far(step):
        pass_on(step)
        to, _ = partners(pairs, owner, step)
        kv_copy(step, to, owner).wait_send()
        send_queries(step)

    def take_share(step):
        _, source = partners(pairs, owner, step)
        share_copy(step, source, side).wait_send()
        share_copy(step, source, 1 - side).wait_recv()
        kvt[2 * source + 1 - side] = kv[2 * source + 1 - side].T

    def take_near(step):
        to, source = partners(pairs, owner, step)
        qd_copy(step, owner, source).wait_recv()
        qd_copy(step, to, owner).wait_send()
        kv_copy(step, to, owner).wait_send()

    def take_far(step):
        to, source = partners(pairs, owner, step)
        qd_copy(step, owner, source).wait_recv()
        qd_copy(step, to, owner).wait_send()

    def near_group(turn, carry):
        group = range(GROUP)
        places = [GROUP * turn + one for one in group]
        blocks_now = [2 * (near + place) + side for place in places]
        names = [[neighbour[slot, block] for slot in range(NNB)] for block in blocks_now]
        valid = [
            [slot < counts[block] if slot > 0 else None for slot in range(NNB)]
            for block in blocks_now
        ]
        queries = [qd[near + place] for place in places]
        x_out = [x_near.at[place] for place in places]
        _, results = attend(group, NNB, names, valid, queries, kv, kvt, pair_scr, x_out)
        for one in group:
            od_near[places[one]] = results[one]
        return carry

    far_steps(pairs, pass_on_far)
    near_steps(pairs, pass_on)
    take_share(jnp.int32(half))
    each_step(pairs, take_share)
    near_steps(pairs, take_near)
    names_copy.wait()
    counts_copy.wait()
    lax.fori_loop(0, half // GROUP, near_group, 0)
    far_steps(pairs, take_far)


def attend(group, used, names, valid, qd, kv, kvt, pair_scr, x_out):
    scale = 1.0 / math.sqrt(E)
    exp_scale = scale * math.log2(math.e)
    low = lax.broadcasted_iota(jnp.int32, (BLK, 2 * E), 1) < E
    top = lax.broadcasted_iota(jnp.int32, (2 * E, BLK), 0) < E

    def folded(array, op):
        return op(array.reshape(BLK // 8, 8, BLK), axis=0)

    spread, ahead = [], []
    for one in group:
        both = qd[one]
        zero = jnp.zeros_like(both)
        upper = jnp.where(low, both, zero)
        lower = jnp.where(low, zero, both)
        spread.append(jnp.concatenate([upper, lower], axis=0))
        ahead.append(jnp.concatenate([upper, lower * jnp.asarray(scale, BF16)], axis=0))
    highest = [None for _ in group]
    for one in group:
        keys = jnp.concatenate([kv[name] for name in names[one]], axis=0)
        result = lax.dot_general(
            keys, ahead[one], (((1,), (1,)), ((), ())), preferred_element_type=F32
        ).reshape(used, BLK, 2 * BLK)
        for slot in range(used):
            pair_scr[one, slot] = result[slot]
            part = folded(result[slot, :, :BLK], jnp.max)
            if valid[one][slot] is not None:
                part = jnp.where(valid[one][slot], part, -jnp.inf)
            highest[one] = part if slot == 0 else jnp.maximum(highest[one], part)
    highest = [jnp.max(part, axis=0, keepdims=True) for part in highest]
    total = [jnp.zeros((8, BLK), F32) for _ in group]
    delta = [jnp.zeros((8, BLK), F32) for _ in group]
    for slot in range(used):
        for one in group:
            raised = jnp.exp2((pair_scr[one, slot, :, :BLK] - highest[one]) * exp_scale)
            if valid[one][slot] is not None:
                raised = jnp.where(valid[one][slot], raised, 0.0)
            pair_scr[one, slot, :, :BLK] = raised
            total[one] = total[one] + folded(raised, jnp.sum)
            delta[one] = delta[one] + folded(raised * pair_scr[one, slot, :, BLK:], jnp.sum)
    inverse = [1.0 / jnp.sum(part, axis=0, keepdims=True) for part in total]
    delta = [jnp.sum(delta[one], axis=0, keepdims=True) * inverse[one] for one in group]
    for slot in range(used):
        for one in group:
            probability = pair_scr[one, slot, :, :BLK] * inverse[one]
            dscore = probability * (pair_scr[one, slot, :, BLK:] - delta[one])
            x_out[one][slot] = jnp.concatenate(
                [dscore.astype(BF16), probability.astype(BF16)], axis=1
            )
    results = []
    for one in group:
        rows = jnp.zeros((2 * E, 2 * BLK), F32)
        for slot in range(0, used, 2):
            if slot + 1 < used:
                keys_t = jnp.concatenate(
                    [kvt[names[one][slot]], kvt[names[one][slot + 1]]], axis=1
                )
                grads = jnp.concatenate([x_out[one][slot], x_out[one][slot + 1]], axis=0)
            else:
                keys_t = kvt[names[one][slot]]
                grads = x_out[one][slot]
            rows = rows + jnp.dot(keys_t, grads, preferred_element_type=F32)
        results.append(jnp.where(top, rows[:, :BLK], rows[:, BLK:]).T.astype(BF16))
    return spread, results


def attend_kernel(
    blocks, neighbour_hbm, counts_hbm, qd, kv, kvt, x_near, od_far, totals,
    neighbour, counts, starts, order, pair_scr, x_scr, load
):
    owner, side = place_of()
    pairs = blocks // 2
    half = pairs // 2
    near = lax.div(owner, half) * half
    far = half - near
    names_copy = pltpu.make_async_copy(neighbour_hbm, neighbour, load.at[0])
    names_copy.start()
    counts_copy = pltpu.make_async_copy(counts_hbm, counts, load.at[1])
    counts_copy.start()

    def clear(block, carry):
        totals[block] = jnp.zeros((BLK, 2 * E), F32)
        return carry

    lax.fori_loop(0, blocks, clear, 0)
    names_copy.wait()
    counts_copy.wait()

    def used_of(place):
        return counts[2 * (far + place) + side]

    def sort_by_used():
        for used in range(NNB + 1):
            starts[used] = 0
        for place in range(half):
            used = used_of(place)
            starts[used - 1] = starts[used - 1] + 1
        for used in range(NNB - 1, -1, -1):
            starts[used] = starts[used] + starts[used + 1]
        for place in range(half):
            used = used_of(place)
            at = starts[used]
            order[at] = place
            starts[used] = at + 1

    def add_up(names, x_of_block, spread):
        used = len(names)
        grads = x_of_block[:used].reshape(used * BLK, 2 * BLK)
        added = jnp.dot(grads, spread, preferred_element_type=F32)
        for slot in range(used):
            totals[names[slot]] += added[slot * BLK : (slot + 1) * BLK]

    def rows_with(places, used):
        group = range(len(places))
        blocks_now = [2 * (far + place) + side for place in places]
        names = [[neighbour[slot, block] for slot in range(used)] for block in blocks_now]
        valid = [
            [slot < counts[block] if one > 0 and slot > 0 else None for slot in range(used)]
            for one, block in enumerate(blocks_now)
        ]
        x_out = [x_scr.at[one] for one in group]
        queries = [qd[far + place] for place in places]
        spread, results = attend(group, used, names, valid, queries, kv, kvt, pair_scr, x_out)
        for one in group:
            od_far[places[one]] = results[one]
            add_up(names[one], x_out[one], spread[one])

    def one_group(turn, carry):
        places = [order[GROUP * turn + one] for one in range(GROUP)]
        used_now = used_of(places[0])
        for used in range(1, NNB + 1):
            pl.when(used_now == used)(functools.partial(rows_with, places, used))
        return carry

    def near_sums(place, carry):
        low = lax.broadcasted_iota(jnp.int32, (BLK, 2 * E), 1) < E
        both = qd[near + place]
        zero = jnp.zeros_like(both)
        spread = jnp.concatenate([jnp.where(low, both, zero), jnp.where(low, zero, both)], axis=0)
        block = 2 * (near + place) + side
        add_up([neighbour[slot, block] for slot in range(NNB)], x_near.at[place], spread)
        return carry

    sort_by_used()
    lax.fori_loop(0, half // GROUP, one_group, 0)
    lax.fori_loop(0, half, near_sums, 0)


def collect_kernel(
    pairs, od_near, od_far, totals, got_od, got_kv, other, shared, send_kv,
    od_out, od_in, kv_out, kv_in, share_out, share_in,
):
    owner, side = place_of()
    barrier = greet(pairs)

    def share_copy(step, place):
        return pltpu.make_async_remote_copy(
            src_ref=other.at[place],
            dst_ref=shared.at[place],
            send_sem=share_out.at[step],
            recv_sem=share_in.at[step],
            device_id=device_of(owner, 1 - side),
            device_id_type=MESH_ID,
        )

    def od_copy(array, step, to, source):
        return pltpu.make_async_remote_copy(
            src_ref=array.at[lax.rem(to, pairs // 2)],
            dst_ref=got_od.at[source],
            send_sem=od_out.at[step],
            recv_sem=od_in.at[step],
            device_id=device_of(to, side),
            device_id_type=MESH_ID,
        )

    def kv_copy(step, to, source):
        return pltpu.make_async_remote_copy(
            src_ref=send_kv.at[to],
            dst_ref=got_kv.at[source],
            send_sem=kv_out.at[step],
            recv_sem=kv_in.at[step],
            device_id=device_of(to, side),
            device_id_type=MESH_ID,
        )

    def narrow(place, carry):
        other[place] = totals[2 * place + 1 - side].astype(BF16)
        return carry

    lax.fori_loop(0, pairs, narrow, 0)
    pl.semaphore_wait(barrier, pairs)

    def start_all(array, step):
        to, _ = partners(pairs, owner, step)
        od_copy(array, step, to, owner).start()
        share_copy(step, to).start()

    def summed(place):
        return (totals[2 * place + side] + shared[place].astype(F32)).astype(BF16)

    def add_and_send(step):
        to, _ = partners(pairs, owner, step)
        share_copy(step, to).wait_recv()
        send_kv[to] = summed(to)
        kv_copy(step, to, owner).start()

    def finish(array, step):
        to, source = partners(pairs, owner, step)
        od_copy(array, step, owner, source).wait_recv()
        kv_copy(step, owner, source).wait_recv()
        od_copy(array, step, to, owner).wait_send()
        kv_copy(step, to, owner).wait_send()
        share_copy(step, to).wait_send()

    far_steps(pairs, functools.partial(start_all, od_far))
    near_steps(pairs, functools.partial(start_all, od_near))
    share_copy(pairs // 2, owner).start()
    each_step(pairs, add_and_send)
    share_copy(pairs // 2, owner).wait_recv()
    got_kv[owner] = summed(owner)
    got_od[owner] = od_near[lax.rem(owner, pairs // 2)]
    far_steps(pairs, functools.partial(finish, od_far))
    near_steps(pairs, functools.partial(finish, od_near))
    share_copy(pairs // 2, owner).wait_send()


def join_kernel(pairs, got_od, got_kv, out, dquery, dkey, dvalue, rows, store):
    copies = []
    for place, (pieces, part, array) in enumerate(
        ((got_od, 1, out), (got_od, 0, dquery), (got_kv, 0, dkey), (got_kv, 1, dvalue))
    ):
        cut = slice(part * E, (part + 1) * E)
        for pair in range(pairs // 2):
            cols = slice(2 * E * pair, 2 * E * (pair + 1))
            rows[place, :, cols] = jnp.concatenate(
                [pieces[2 * pair][:, cut], pieces[2 * pair + 1][:, cut]], axis=1
            )
        copies.append(pltpu.make_async_copy(rows.at[place], array, store.at[place]))
        copies[-1].start()
    for copy in copies:
        copy.wait()


def on_device_whole(query, key, value, grad_out, neighbour, counts):
    pairs = lax.axis_size("ctx") * lax.axis_size("head") // 2
    blocks = 2 * pairs
    width = query.shape[1]
    in_vmem = pl.BlockSpec(memory_space=pltpu.VMEM)
    in_hbm = pl.BlockSpec(memory_space=pltpu.HBM)
    many = pltpu.SemaphoreType.DMA((pairs,))
    piece = (BLK, 2 * E)
    own_pieces = jax.ShapeDtypeStruct((pairs, *piece), BF16)
    index_arrays = [
        pltpu.SMEM(neighbour.shape[::-1], jnp.int32),
        pltpu.SMEM(counts.shape, jnp.int32),
    ]
    with jax.named_scope("spread_heads"):
        qd, kv, kvt, x_near, od_near = pl.pallas_call(
            functools.partial(spread_kernel, pairs),
            out_shape=(
                pltpu.VMEM((pairs, *piece), BF16),
                pltpu.VMEM((blocks, *piece), BF16),
                pltpu.VMEM((blocks, *piece), BF16),
                pltpu.VMEM((pairs // 2, NNB, BLK, 2 * BLK), BF16),
                pltpu.VMEM((pairs // 2, *piece), BF16),
            ),
            in_specs=[in_hbm] * 6,
            out_specs=(in_vmem,) * 5,
            scratch_shapes=[pltpu.VMEM((4, BLK, width), BF16)]
            + [pltpu.VMEM((pairs, *piece), BF16)] * 2
            + index_arrays
            + [pltpu.VMEM((GROUP, NNB, BLK, 2 * BLK), F32)]
            + [pltpu.SemaphoreType.DMA((6,))]
            + [many] * 6,
            compiler_params=pltpu.CompilerParams(
                collective_id=0, has_side_effects=True, vmem_limit_bytes=VMEM_BYTES
            ),
        )(*map(left_in_hbm, (query, key, value, grad_out, neighbour.T, counts)))
    with jax.named_scope("block_attention"):
        od_far, totals = pl.pallas_call(
            functools.partial(attend_kernel, blocks),
            out_shape=(
                jax.ShapeDtypeStruct((pairs // 2, *piece), BF16),
                jax.ShapeDtypeStruct((blocks, *piece), F32),
            ),
            in_specs=[in_hbm] * 2 + [in_vmem] * 4,
            out_specs=(in_vmem,) * 2,
            scratch_shapes=[
                *index_arrays,
                pltpu.SMEM((NNB + 1,), jnp.int32),
                pltpu.SMEM((pairs // 2,), jnp.int32),
                pltpu.VMEM((GROUP, NNB, BLK, 2 * BLK), F32),
                pltpu.VMEM((GROUP, NNB, BLK, 2 * BLK), BF16),
                pltpu.SemaphoreType.DMA((2,)),
            ],
            compiler_params=pltpu.CompilerParams(vmem_limit_bytes=VMEM_BYTES),
        )(left_in_hbm(neighbour.T), left_in_hbm(counts), qd, kv, kvt, x_near)
    with jax.named_scope("collect_heads"):
        got_od, got_kv = pl.pallas_call(
            functools.partial(collect_kernel, pairs),
            out_shape=(own_pieces,) * 2,
            in_specs=[in_vmem] * 3,
            out_specs=(in_vmem,) * 2,
            scratch_shapes=[pltpu.VMEM((pairs, *piece), BF16)] * 3 + [many] * 6,
            compiler_params=pltpu.CompilerParams(
                collective_id=1, has_side_effects=True, vmem_limit_bytes=VMEM_BYTES
            ),
        )(od_near, od_far, totals)
    with jax.named_scope("join_heads"):
        return pl.pallas_call(
            functools.partial(join_kernel, pairs),
            out_shape=(jax.ShapeDtypeStruct((BLK, width), BF16),) * 4,
            in_specs=[in_vmem] * 2,
            out_specs=(in_hbm,) * 4,
            scratch_shapes=[
                pltpu.VMEM((4, BLK, width), BF16),
                pltpu.SemaphoreType.DMA((4,)),
            ],
            compiler_params=pltpu.CompilerParams(vmem_limit_bytes=VMEM_BYTES),
        )(got_od, got_kv)


def on_device(query, key, value, grad_out, neighbour, counts):
    devices = lax.axis_size("ctx") * lax.axis_size("head")
    if devices == 2 * H and H % (2 * GROUP) == 0 and query.shape == (BLK, H * E) and counts.shape[0] == devices:
        return on_device_whole(query, key, value, grad_out, neighbour, counts)
    return on_device_windowed(query, key, value, grad_out, neighbour, counts)


def solution(mesh):
    return jax.shard_map(
        on_device,
        mesh=mesh,
        in_specs=(
            P(("ctx", "head"), None),
            P(("ctx", "head"), None),
            P(("ctx", "head"), None),
            P(("ctx", "head"), None),
            P(),
            P(),
        ),
        out_specs=(
            P(("ctx", "head"), None),
            P(("ctx", "head"), None),
            P(("ctx", "head"), None),
            P(("ctx", "head"), None),
        ),
        check_vma=False,
    )
```

```python
import functools
import math

import jax
import jax.numpy as jnp
from jax import lax
from jax.experimental import pallas as pl
from jax.experimental.pallas import tpu as pltpu
from jax.sharding import PartitionSpec as P

H = 16
E = 64
BLK = 128
NNB = 8
REACH = 2


def passed_along(value, axis, steps):
    count = lax.axis_size(axis)
    pairs = [(source, (source + steps) % count) for source in range(count)]
    return lax.ppermute(value, axis, pairs)


def group_rows(blocks_shard, block_len):
    limit = max(512 // block_len, 1)
    best = 1
    for candidate in range(1, blocks_shard + 1):
        if blocks_shard % candidate == 0 and candidate <= limit:
            best = candidate
    return best


def on_device_windowed(query, key, value, grad_out, neighbour, counts):
    tok_rows = query.shape[0]
    groups = lax.axis_size("head")
    per_dev = H // groups
    head_cols = per_dev * E
    moved = (
        lax.all_to_all(
            query.reshape(tok_rows, groups, head_cols),
            "head",
            split_axis=1,
            concat_axis=0,
            tiled=True,
        ),
        lax.all_to_all(
            key.reshape(tok_rows, groups, head_cols),
            "head",
            split_axis=1,
            concat_axis=0,
            tiled=True,
        ),
        lax.all_to_all(
            value.reshape(tok_rows, groups, head_cols),
            "head",
            split_axis=1,
            concat_axis=0,
            tiled=True,
        ),
        lax.all_to_all(
            grad_out.reshape(tok_rows, groups, head_cols),
            "head",
            split_axis=1,
            concat_axis=0,
            tiled=True,
        ),
    )
    shard_rows = groups * tok_rows
    query_s = moved[0].reshape(shard_rows, head_cols)
    key_s = moved[1].reshape(shard_rows, head_cols)
    value_s = moved[2].reshape(shard_rows, head_cols)
    grad_s = moved[3].reshape(shard_rows, head_cols)
    paired = jnp.concatenate([key_s, value_s], axis=1)
    cycle_len = lax.axis_size("ctx")
    position = lax.axis_index("ctx")
    blocks_shard = shard_rows // BLK
    all_blocks = blocks_shard * cycle_len
    fetched = {}
    offsets_all = list(range(1, REACH + 1)) + [-offset for offset in range(1, REACH + 1)]
    for offset in offsets_all:
        fetched[offset] = passed_along(paired, "ctx", offset)
    ordered = (
        [fetched[REACH - place] for place in range(REACH)]
        + [paired]
        + [fetched[-(place + 1)] for place in range(REACH)]
    )
    span_shards = 2 * REACH + 1
    window = jnp.concatenate(ordered, axis=0).reshape(
        span_shards * blocks_shard, BLK, 2 * head_cols
    )
    rows_nbr = lax.dynamic_slice_in_dim(neighbour, position * blocks_shard, blocks_shard, 0)
    local_idx = jnp.mod(rows_nbr - (position - REACH) * blocks_shard, all_blocks)
    used = lax.dynamic_slice_in_dim(counts, position * blocks_shard, blocks_shard, 0)
    per_group = group_rows(blocks_shard, BLK)
    turns = blocks_shard // per_group
    scale_factor = 1.0 / math.sqrt(E)
    query_g = query_s.reshape(turns, per_group, BLK, per_dev, E)
    grad_g = grad_s.reshape(turns, per_group, BLK, per_dev, E)
    index_g = local_idx.reshape(turns, per_group, NNB)
    used_g = used.reshape(turns, per_group)

    def one_group(totals, inputs):
        queries, cotangent, chosen, used_now = inputs
        selected = window[chosen]
        keys_sel = selected[..., :head_cols].reshape(per_group, NNB, BLK, per_dev, E)
        values_sel = selected[..., head_cols:].reshape(per_group, NNB, BLK, per_dev, E)
        usable = jnp.arange(NNB)[None, :] < used_now[:, None]
        allowed = usable[:, None, None, :, None]
        scores = (
            jnp.einsum("rihe,rjthe->rhijt", queries, keys_sel, preferred_element_type=jnp.float32)
            * scale_factor
        )
        masked = jnp.where(allowed, scores, -1e30)
        highest = jnp.max(masked, axis=(3, 4), keepdims=True)
        raised = jnp.where(allowed, jnp.exp(masked - highest), 0.0)
        total = jnp.sum(raised, axis=(3, 4), keepdims=True)
        probability = raised / total
        weights = probability.astype(jnp.bfloat16)
        out_rows = jnp.einsum(
            "rhijt,rjthe->rihe", weights, values_sel, preferred_element_type=jnp.float32
        ).astype(jnp.bfloat16)
        dprob = jnp.einsum(
            "rihe,rjthe->rhijt", cotangent, values_sel, preferred_element_type=jnp.float32
        )
        row_delta = jnp.sum(probability * dprob, axis=(3, 4), keepdims=True)
        dscore = (probability * (dprob - row_delta) * scale_factor).astype(jnp.bfloat16)
        dquery = jnp.einsum(
            "rhijt,rjthe->rihe", dscore, keys_sel, preferred_element_type=jnp.float32
        ).astype(jnp.bfloat16)
        dkey_part = jnp.einsum(
            "rhijt,rihe->rjthe", dscore, queries, preferred_element_type=jnp.float32
        )
        dvalue_part = jnp.einsum(
            "rhijt,rihe->rjthe", weights, cotangent, preferred_element_type=jnp.float32
        )
        joined = jnp.concatenate(
            [
                dkey_part.reshape(per_group * NNB, BLK, head_cols),
                dvalue_part.reshape(per_group * NNB, BLK, head_cols),
            ],
            axis=-1,
        )
        totals = totals.at[chosen.reshape(-1)].add(joined)
        return (totals, (out_rows, dquery))

    start_grads = jnp.zeros((span_shards * blocks_shard, BLK, 2 * head_cols), jnp.float32)
    grads_window, results = lax.scan(one_group, start_grads, (query_g, grad_g, index_g, used_g))
    grads_window = grads_window.reshape(span_shards, shard_rows, 2 * head_cols)
    combined = grads_window[REACH]
    offsets_back = list(range(1, REACH + 1)) + [-offset for offset in range(1, REACH + 1)]
    for offset in offsets_back:
        combined = combined + passed_along(
            grads_window[REACH - offset].astype(jnp.bfloat16), "ctx", -offset
        ).astype(jnp.float32)
    combined = combined.astype(jnp.bfloat16)
    dkey_s = combined[:, :head_cols]
    dvalue_s = combined[:, head_cols:]
    out_s = results[0].reshape(shard_rows, head_cols)
    dquery_s = results[1].reshape(shard_rows, head_cols)
    back = (
        lax.all_to_all(
            out_s.reshape(shard_rows, 1, head_cols), "head", split_axis=0, concat_axis=1, tiled=True
        ),
        lax.all_to_all(
            dquery_s.reshape(shard_rows, 1, head_cols),
            "head",
            split_axis=0,
            concat_axis=1,
            tiled=True,
        ),
        lax.all_to_all(
            dkey_s.reshape(shard_rows, 1, head_cols),
            "head",
            split_axis=0,
            concat_axis=1,
            tiled=True,
        ),
        lax.all_to_all(
            dvalue_s.reshape(shard_rows, 1, head_cols),
            "head",
            split_axis=0,
            concat_axis=1,
            tiled=True,
        ),
    )
    width = groups * head_cols
    return (
        back[0].reshape(tok_rows, width),
        back[1].reshape(tok_rows, width),
        back[2].reshape(tok_rows, width),
        back[3].reshape(tok_rows, width),
    )


MESH_ID = pl.DeviceIdType.MESH
F32 = jnp.float32
BF16 = jnp.bfloat16
GROUP = 2
VMEM_BYTES = 20 * 1024 * 1024


def left_in_hbm(array):
    return pltpu.with_memory_space_constraint(array, pltpu.HBM)


def place_of():
    index = lax.axis_index("ctx") * lax.axis_size("head") + lax.axis_index("head")
    return lax.div(index, 2), lax.rem(index, 2)


def device_of(owner, side):
    n_head = lax.axis_size("head")
    index = 2 * owner + side
    return (lax.div(index, n_head), lax.rem(index, n_head))


def partners(pairs, owner, step):
    half = pairs // 2
    far = 1 - lax.div(step, half)
    base = lax.rem(lax.div(owner, half) + far, 2) * half
    low, turn = lax.rem(owner, half), lax.rem(step, half)
    return base + lax.rem(low + turn, half), base + lax.rem(low - turn + half, half)


def run_steps(start, stop, body):
    def one(step, carry):
        body(step)
        return carry

    lax.fori_loop(start, stop, one, 0)


def far_steps(pairs, body):
    run_steps(0, pairs // 2, body)


def near_steps(pairs, body):
    run_steps(pairs // 2 + 1, pairs, body)


def each_step(pairs, body):
    far_steps(pairs, body)
    near_steps(pairs, body)


def greet(pairs):
    owner, side = place_of()
    barrier = pltpu.get_barrier_semaphore()
    pl.semaphore_signal(barrier, inc=1, device_id=device_of(owner, 1 - side), device_id_type=MESH_ID)

    def one(step):
        to, _ = partners(pairs, owner, step)
        pl.semaphore_signal(barrier, inc=1, device_id=device_of(to, side), device_id_type=MESH_ID)

    each_step(pairs, one)
    return barrier


def spread_kernel(
    pairs, query, key, value, grad_out, neighbour_hbm, counts_hbm, qd, kv, kvt, sums_near, od_near,
    own_rows, send_qd, send_kv, neighbour, counts, pair_scr, x_scr,
    load, qd_out, qd_in, kv_out, kv_in, share_out, share_in,
):
    owner, side = place_of()
    half = pairs // 2
    near = lax.div(owner, half) * half
    loads = [
        pltpu.make_async_copy(array, own_rows.at[place], load.at[place])
        for place, array in enumerate((key, value, query, grad_out))
    ]
    names_copy = pltpu.make_async_copy(neighbour_hbm, neighbour, load.at[4])
    counts_copy = pltpu.make_async_copy(counts_hbm, counts, load.at[5])
    for copy in loads + [names_copy, counts_copy]:
        copy.start()
    barrier = greet(pairs)

    def pack(first, pieces):
        loads[first].wait()
        loads[first + 1].wait()
        for pair in range(pairs // 2):
            cols = slice(2 * E * pair, 2 * E * (pair + 1))
            a = own_rows[first, :, cols]
            b = own_rows[first + 1, :, cols]
            pieces[2 * pair] = jnp.concatenate([a[:, :E], b[:, :E]], axis=1)
            pieces[2 * pair + 1] = jnp.concatenate([a[:, E:], b[:, E:]], axis=1)

    def kv_copy(step, to, source):
        return pltpu.make_async_remote_copy(
            src_ref=send_kv.at[to],
            dst_ref=kv.at[2 * source + side],
            send_sem=kv_out.at[step],
            recv_sem=kv_in.at[step],
            device_id=device_of(to, side),
            device_id_type=MESH_ID,
        )

    def qd_copy(step, to, source):
        return pltpu.make_async_remote_copy(
            src_ref=send_qd.at[to],
            dst_ref=qd.at[source],
            send_sem=qd_out.at[step],
            recv_sem=qd_in.at[step],
            device_id=device_of(to, side),
            device_id_type=MESH_ID,
        )

    def share_copy(step, source, whose):
        return pltpu.make_async_remote_copy(
            src_ref=kv.at[2 * source + side],
            dst_ref=kv.at[2 * source + whose],
            send_sem=share_out.at[step],
            recv_sem=share_in.at[step],
            device_id=device_of(owner, 1 - side),
            device_id_type=MESH_ID,
        )

    def send_keys(step):
        to, _ = partners(pairs, owner, step)
        kv_copy(step, to, owner).start()

    def send_queries(step):
        to, _ = partners(pairs, owner, step)
        qd_copy(step, to, owner).start()

    pack(0, send_kv)
    pl.semaphore_wait(barrier, pairs)
    each_step(pairs, send_keys)
    pack(2, send_qd)
    near_steps(pairs, send_queries)
    mine = 2 * owner + side
    kv[mine] = send_kv[owner]
    qd[owner] = send_qd[owner]
    share_copy(half, owner, side).start()
    kvt[mine] = kv[mine].T

    def pass_on(step):
        _, source = partners(pairs, owner, step)
        kv_copy(step, owner, source).wait_recv()
        share_copy(step, source, side).start()
        kvt[2 * source + side] = kv[2 * source + side].T

    def pass_on_far(step):
        pass_on(step)
        to, _ = partners(pairs, owner, step)
        kv_copy(step, to, owner).wait_send()
        send_queries(step)

    def take_share(step):
        _, source = partners(pairs, owner, step)
        share_copy(step, source, side).wait_send()
        share_copy(step, source, 1 - side).wait_recv()
        kvt[2 * source + 1 - side] = kv[2 * source + 1 - side].T

    def take_near(step):
        to, source = partners(pairs, owner, step)
        qd_copy(step, owner, source).wait_recv()
        qd_copy(step, to, owner).wait_send()
        kv_copy(step, to, owner).wait_send()

    def take_far(step):
        to, source = partners(pairs, owner, step)
        qd_copy(step, owner, source).wait_recv()
        qd_copy(step, to, owner).wait_send()

    def near_group(turn, carry):
        group = range(GROUP)
        places = [GROUP * turn + one for one in group]
        blocks_now = [2 * (near + place) + side for place in places]
        names = [[neighbour[slot, block] for slot in range(NNB)] for block in blocks_now]
        valid = [
            [slot < counts[block] if slot > 0 else None for slot in range(NNB)]
            for block in blocks_now
        ]
        queries = [qd[near + place] for place in places]
        x_out = [x_scr.at[one] for one in group]
        spread, results = attend(group, NNB, names, valid, queries, kv, kvt, pair_scr, x_out)
        for one in group:
            od_near[places[one]] = results[one]
            grads = x_scr[one].reshape(NNB * BLK, 2 * BLK)
            added = jnp.dot(grads, spread[one], preferred_element_type=F32)
            sums_near[places[one]] = added.reshape(NNB, BLK, 2 * E)
        return carry

    far_steps(pairs, pass_on_far)
    near_steps(pairs, pass_on)
    take_share(jnp.int32(half))
    each_step(pairs, take_share)
    near_steps(pairs, take_near)
    names_copy.wait()
    counts_copy.wait()
    lax.fori_loop(0, half // GROUP, near_group, 0)
    far_steps(pairs, take_far)


def attend(group, used, names, valid, qd, kv, kvt, pair_scr, x_out):
    scale = 1.0 / math.sqrt(E)
    exp_scale = scale * math.log2(math.e)
    low = lax.broadcasted_iota(jnp.int32, (BLK, 2 * E), 1) < E
    top = lax.broadcasted_iota(jnp.int32, (2 * E, BLK), 0) < E

    def folded(array, op):
        return op(array.reshape(BLK // 8, 8, BLK), axis=0)

    spread, ahead = [], []
    for one in group:
        both = qd[one]
        zero = jnp.zeros_like(both)
        upper = jnp.where(low, both, zero)
        lower = jnp.where(low, zero, both)
        spread.append(jnp.concatenate([upper, lower], axis=0))
        ahead.append(jnp.concatenate([upper, lower * jnp.asarray(scale, BF16)], axis=0))
    highest = [None for _ in group]
    for one in group:
        keys = jnp.concatenate([kv[name] for name in names[one]], axis=0)
        result = lax.dot_general(
            keys, ahead[one], (((1,), (1,)), ((), ())), preferred_element_type=F32
        ).reshape(used, BLK, 2 * BLK)
        for slot in range(used):
            pair_scr[one, slot] = result[slot]
            part = folded(result[slot, :, :BLK], jnp.max)
            if valid[one][slot] is not None:
                part = jnp.where(valid[one][slot], part, -jnp.inf)
            highest[one] = part if slot == 0 else jnp.maximum(highest[one], part)
    highest = [jnp.max(part, axis=0, keepdims=True) for part in highest]
    total = [jnp.zeros((8, BLK), F32) for _ in group]
    delta = [jnp.zeros((8, BLK), F32) for _ in group]
    for slot in range(used):
        for one in group:
            raised = jnp.exp2((pair_scr[one, slot, :, :BLK] - highest[one]) * exp_scale)
            if valid[one][slot] is not None:
                raised = jnp.where(valid[one][slot], raised, 0.0)
            pair_scr[one, slot, :, :BLK] = raised
            total[one] = total[one] + folded(raised, jnp.sum)
            delta[one] = delta[one] + folded(raised * pair_scr[one, slot, :, BLK:], jnp.sum)
    inverse = [1.0 / jnp.sum(part, axis=0, keepdims=True) for part in total]
    delta = [jnp.sum(delta[one], axis=0, keepdims=True) * inverse[one] for one in group]
    for slot in range(used):
        for one in group:
            probability = pair_scr[one, slot, :, :BLK] * inverse[one]
            dscore = probability * (pair_scr[one, slot, :, BLK:] - delta[one])
            x_out[one][slot] = jnp.concatenate(
                [dscore.astype(BF16), probability.astype(BF16)], axis=1
            )
    results = []
    for one in group:
        rows = jnp.zeros((2 * E, 2 * BLK), F32)
        for slot in range(0, used, 2):
            if slot + 1 < used:
                keys_t = jnp.concatenate(
                    [kvt[names[one][slot]], kvt[names[one][slot + 1]]], axis=1
                )
                grads = jnp.concatenate([x_out[one][slot], x_out[one][slot + 1]], axis=0)
            else:
                keys_t = kvt[names[one][slot]]
                grads = x_out[one][slot]
            rows = rows + jnp.dot(keys_t, grads, preferred_element_type=F32)
        results.append(jnp.where(top, rows[:, :BLK], rows[:, BLK:]).T.astype(BF16))
    return spread, results


def attend_kernel(
    blocks, neighbour_hbm, counts_hbm, qd, kv, kvt, sums_near, od_far, totals,
    neighbour, counts, starts, order, pair_scr, x_scr, load
):
    owner, side = place_of()
    pairs = blocks // 2
    half = pairs // 2
    near = lax.div(owner, half) * half
    far = half - near
    names_copy = pltpu.make_async_copy(neighbour_hbm, neighbour, load.at[0])
    names_copy.start()
    counts_copy = pltpu.make_async_copy(counts_hbm, counts, load.at[1])
    counts_copy.start()

    def clear(block, carry):
        totals[block] = jnp.zeros((BLK, 2 * E), F32)
        return carry

    lax.fori_loop(0, blocks, clear, 0)
    names_copy.wait()
    counts_copy.wait()

    def used_of(place):
        return counts[2 * (far + place) + side]

    def sort_by_used():
        for used in range(NNB + 1):
            starts[used] = 0
        for place in range(half):
            used = used_of(place)
            starts[used - 1] = starts[used - 1] + 1
        for used in range(NNB - 1, -1, -1):
            starts[used] = starts[used] + starts[used + 1]
        for place in range(half):
            used = used_of(place)
            at = starts[used]
            order[at] = place
            starts[used] = at + 1

    def add_up(names, x_of_block, spread):
        used = len(names)
        grads = x_of_block[:used].reshape(used * BLK, 2 * BLK)
        added = jnp.dot(grads, spread, preferred_element_type=F32)
        for slot in range(used):
            totals[names[slot]] += added[slot * BLK : (slot + 1) * BLK]

    def rows_with(places, used):
        group = range(len(places))
        blocks_now = [2 * (far + place) + side for place in places]
        names = [[neighbour[slot, block] for slot in range(used)] for block in blocks_now]
        valid = [
            [slot < counts[block] if one > 0 and slot > 0 else None for slot in range(used)]
            for one, block in enumerate(blocks_now)
        ]
        x_out = [x_scr.at[one] for one in group]
        queries = [qd[far + place] for place in places]
        spread, results = attend(group, used, names, valid, queries, kv, kvt, pair_scr, x_out)
        for one in group:
            od_far[places[one]] = results[one]
            add_up(names[one], x_out[one], spread[one])

    def one_group(turn, carry):
        places = [order[GROUP * turn + one] for one in range(GROUP)]
        used_now = used_of(places[0])
        for used in range(1, NNB + 1):
            pl.when(used_now == used)(functools.partial(rows_with, places, used))
        return carry

    def near_sums(place, carry):
        block = 2 * (near + place) + side

        def one_slot(slot, carry):
            totals[neighbour[slot, block]] += sums_near[place, slot]
            return carry

        lax.fori_loop(0, counts[block], one_slot, 0)
        return carry

    sort_by_used()
    lax.fori_loop(0, half // GROUP, one_group, 0)
    lax.fori_loop(0, half, near_sums, 0)


def collect_kernel(
    pairs, od_near, od_far, totals, got_od, got_kv, other, shared, send_kv,
    od_out, od_in, kv_out, kv_in, share_out, share_in,
):
    owner, side = place_of()
    barrier = greet(pairs)

    def share_copy(step, place):
        return pltpu.make_async_remote_copy(
            src_ref=other.at[place],
            dst_ref=shared.at[place],
            send_sem=share_out.at[step],
            recv_sem=share_in.at[step],
            device_id=device_of(owner, 1 - side),
            device_id_type=MESH_ID,
        )

    def od_copy(array, step, to, source):
        return pltpu.make_async_remote_copy(
            src_ref=array.at[lax.rem(to, pairs // 2)],
            dst_ref=got_od.at[source],
            send_sem=od_out.at[step],
            recv_sem=od_in.at[step],
            device_id=device_of(to, side),
            device_id_type=MESH_ID,
        )

    def kv_copy(step, to, source):
        return pltpu.make_async_remote_copy(
            src_ref=send_kv.at[to],
            dst_ref=got_kv.at[source],
            send_sem=kv_out.at[step],
            recv_sem=kv_in.at[step],
            device_id=device_of(to, side),
            device_id_type=MESH_ID,
        )

    def narrow(place, carry):
        other[place] = totals[2 * place + 1 - side].astype(BF16)
        return carry

    lax.fori_loop(0, pairs, narrow, 0)
    pl.semaphore_wait(barrier, pairs)

    def start_all(array, step):
        to, _ = partners(pairs, owner, step)
        od_copy(array, step, to, owner).start()
        share_copy(step, to).start()

    def summed(place):
        return (totals[2 * place + side] + shared[place].astype(F32)).astype(BF16)

    def add_and_send(step):
        to, _ = partners(pairs, owner, step)
        share_copy(step, to).wait_recv()
        send_kv[to] = summed(to)
        kv_copy(step, to, owner).start()

    def finish(array, step):
        to, source = partners(pairs, owner, step)
        od_copy(array, step, owner, source).wait_recv()
        kv_copy(step, owner, source).wait_recv()
        od_copy(array, step, to, owner).wait_send()
        kv_copy(step, to, owner).wait_send()
        share_copy(step, to).wait_send()

    far_steps(pairs, functools.partial(start_all, od_far))
    near_steps(pairs, functools.partial(start_all, od_near))
    share_copy(pairs // 2, owner).start()
    each_step(pairs, add_and_send)
    share_copy(pairs // 2, owner).wait_recv()
    got_kv[owner] = summed(owner)
    got_od[owner] = od_near[lax.rem(owner, pairs // 2)]
    far_steps(pairs, functools.partial(finish, od_far))
    near_steps(pairs, functools.partial(finish, od_near))
    share_copy(pairs // 2, owner).wait_send()


def join_kernel(pairs, got_od, got_kv, out, dquery, dkey, dvalue, rows, store):
    copies = []
    for place, (pieces, part, array) in enumerate(
        ((got_od, 1, out), (got_od, 0, dquery), (got_kv, 0, dkey), (got_kv, 1, dvalue))
    ):
        cut = slice(part * E, (part + 1) * E)
        for pair in range(pairs // 2):
            cols = slice(2 * E * pair, 2 * E * (pair + 1))
            rows[place, :, cols] = jnp.concatenate(
                [pieces[2 * pair][:, cut], pieces[2 * pair + 1][:, cut]], axis=1
            )
        copies.append(pltpu.make_async_copy(rows.at[place], array, store.at[place]))
        copies[-1].start()
    for copy in copies:
        copy.wait()


def on_device_whole(query, key, value, grad_out, neighbour, counts):
    pairs = lax.axis_size("ctx") * lax.axis_size("head") // 2
    blocks = 2 * pairs
    width = query.shape[1]
    in_vmem = pl.BlockSpec(memory_space=pltpu.VMEM)
    in_hbm = pl.BlockSpec(memory_space=pltpu.HBM)
    many = pltpu.SemaphoreType.DMA((pairs,))
    piece = (BLK, 2 * E)
    own_pieces = jax.ShapeDtypeStruct((pairs, *piece), BF16)
    index_arrays = [
        pltpu.SMEM(neighbour.shape[::-1], jnp.int32),
        pltpu.SMEM(counts.shape, jnp.int32),
    ]
    with jax.named_scope("spread_heads"):
        qd, kv, kvt, sums_near, od_near = pl.pallas_call(
            functools.partial(spread_kernel, pairs),
            out_shape=(
                pltpu.VMEM((pairs, *piece), BF16),
                pltpu.VMEM((blocks, *piece), BF16),
                pltpu.VMEM((blocks, *piece), BF16),
                pltpu.VMEM((pairs // 2, NNB, BLK, 2 * E), F32),
                pltpu.VMEM((pairs // 2, *piece), BF16),
            ),
            in_specs=[in_hbm] * 6,
            out_specs=(in_vmem,) * 5,
            scratch_shapes=[pltpu.VMEM((4, BLK, width), BF16)]
            + [pltpu.VMEM((pairs, *piece), BF16)] * 2
            + index_arrays
            + [pltpu.VMEM((GROUP, NNB, BLK, 2 * BLK), kind) for kind in (F32, BF16)]
            + [pltpu.SemaphoreType.DMA((6,))]
            + [many] * 6,
            compiler_params=pltpu.CompilerParams(
                collective_id=0, has_side_effects=True, vmem_limit_bytes=VMEM_BYTES
            ),
        )(*map(left_in_hbm, (query, key, value, grad_out, neighbour.T, counts)))
    with jax.named_scope("block_attention"):
        od_far, totals = pl.pallas_call(
            functools.partial(attend_kernel, blocks),
            out_shape=(
                jax.ShapeDtypeStruct((pairs // 2, *piece), BF16),
                jax.ShapeDtypeStruct((blocks, *piece), F32),
            ),
            in_specs=[in_hbm] * 2 + [in_vmem] * 4,
            out_specs=(in_vmem,) * 2,
            scratch_shapes=[
                *index_arrays,
                pltpu.SMEM((NNB + 1,), jnp.int32),
                pltpu.SMEM((pairs // 2,), jnp.int32),
                pltpu.VMEM((GROUP, NNB, BLK, 2 * BLK), F32),
                pltpu.VMEM((GROUP, NNB, BLK, 2 * BLK), BF16),
                pltpu.SemaphoreType.DMA((2,)),
            ],
            compiler_params=pltpu.CompilerParams(vmem_limit_bytes=VMEM_BYTES),
        )(left_in_hbm(neighbour.T), left_in_hbm(counts), qd, kv, kvt, sums_near)
    with jax.named_scope("collect_heads"):
        got_od, got_kv = pl.pallas_call(
            functools.partial(collect_kernel, pairs),
            out_shape=(own_pieces,) * 2,
            in_specs=[in_vmem] * 3,
            out_specs=(in_vmem,) * 2,
            scratch_shapes=[pltpu.VMEM((pairs, *piece), BF16)] * 3 + [many] * 6,
            compiler_params=pltpu.CompilerParams(
                collective_id=1, has_side_effects=True, vmem_limit_bytes=VMEM_BYTES
            ),
        )(od_near, od_far, totals)
    with jax.named_scope("join_heads"):
        return pl.pallas_call(
            functools.partial(join_kernel, pairs),
            out_shape=(jax.ShapeDtypeStruct((BLK, width), BF16),) * 4,
            in_specs=[in_vmem] * 2,
            out_specs=(in_hbm,) * 4,
            scratch_shapes=[
                pltpu.VMEM((4, BLK, width), BF16),
                pltpu.SemaphoreType.DMA((4,)),
            ],
            compiler_params=pltpu.CompilerParams(vmem_limit_bytes=VMEM_BYTES),
        )(got_od, got_kv)


def on_device(query, key, value, grad_out, neighbour, counts):
    devices = lax.axis_size("ctx") * lax.axis_size("head")
    if devices == 2 * H and H % (2 * GROUP) == 0 and query.shape == (BLK, H * E) and counts.shape[0] == devices:
        return on_device_whole(query, key, value, grad_out, neighbour, counts)
    return on_device_windowed(query, key, value, grad_out, neighbour, counts)


def solution(mesh):
    return jax.shard_map(
        on_device,
        mesh=mesh,
        in_specs=(
            P(("ctx", "head"), None),
            P(("ctx", "head"), None),
            P(("ctx", "head"), None),
            P(("ctx", "head"), None),
            P(),
            P(),
        ),
        out_specs=(
            P(("ctx", "head"), None),
            P(("ctx", "head"), None),
            P(("ctx", "head"), None),
            P(("ctx", "head"), None),
        ),
        check_vma=False,
    )
```

```python
import functools
import math

import jax
import jax.numpy as jnp
from jax import lax
from jax.experimental import pallas as pl
from jax.experimental.pallas import tpu as pltpu
from jax.sharding import PartitionSpec as P

H = 16
E = 64
BLK = 128
NNB = 8
REACH = 2


def passed_along(value, axis, steps):
    count = lax.axis_size(axis)
    pairs = [(source, (source + steps) % count) for source in range(count)]
    return lax.ppermute(value, axis, pairs)


def group_rows(blocks_shard, block_len):
    limit = max(512 // block_len, 1)
    best = 1
    for candidate in range(1, blocks_shard + 1):
        if blocks_shard % candidate == 0 and candidate <= limit:
            best = candidate
    return best


def on_device_windowed(query, key, value, grad_out, neighbour, counts):
    tok_rows = query.shape[0]
    groups = lax.axis_size("head")
    per_dev = H // groups
    head_cols = per_dev * E
    moved = (
        lax.all_to_all(
            query.reshape(tok_rows, groups, head_cols),
            "head",
            split_axis=1,
            concat_axis=0,
            tiled=True,
        ),
        lax.all_to_all(
            key.reshape(tok_rows, groups, head_cols),
            "head",
            split_axis=1,
            concat_axis=0,
            tiled=True,
        ),
        lax.all_to_all(
            value.reshape(tok_rows, groups, head_cols),
            "head",
            split_axis=1,
            concat_axis=0,
            tiled=True,
        ),
        lax.all_to_all(
            grad_out.reshape(tok_rows, groups, head_cols),
            "head",
            split_axis=1,
            concat_axis=0,
            tiled=True,
        ),
    )
    shard_rows = groups * tok_rows
    query_s = moved[0].reshape(shard_rows, head_cols)
    key_s = moved[1].reshape(shard_rows, head_cols)
    value_s = moved[2].reshape(shard_rows, head_cols)
    grad_s = moved[3].reshape(shard_rows, head_cols)
    paired = jnp.concatenate([key_s, value_s], axis=1)
    cycle_len = lax.axis_size("ctx")
    position = lax.axis_index("ctx")
    blocks_shard = shard_rows // BLK
    all_blocks = blocks_shard * cycle_len
    fetched = {}
    offsets_all = list(range(1, REACH + 1)) + [-offset for offset in range(1, REACH + 1)]
    for offset in offsets_all:
        fetched[offset] = passed_along(paired, "ctx", offset)
    ordered = (
        [fetched[REACH - place] for place in range(REACH)]
        + [paired]
        + [fetched[-(place + 1)] for place in range(REACH)]
    )
    span_shards = 2 * REACH + 1
    window = jnp.concatenate(ordered, axis=0).reshape(
        span_shards * blocks_shard, BLK, 2 * head_cols
    )
    rows_nbr = lax.dynamic_slice_in_dim(neighbour, position * blocks_shard, blocks_shard, 0)
    local_idx = jnp.mod(rows_nbr - (position - REACH) * blocks_shard, all_blocks)
    used = lax.dynamic_slice_in_dim(counts, position * blocks_shard, blocks_shard, 0)
    per_group = group_rows(blocks_shard, BLK)
    turns = blocks_shard // per_group
    scale_factor = 1.0 / math.sqrt(E)
    query_g = query_s.reshape(turns, per_group, BLK, per_dev, E)
    grad_g = grad_s.reshape(turns, per_group, BLK, per_dev, E)
    index_g = local_idx.reshape(turns, per_group, NNB)
    used_g = used.reshape(turns, per_group)

    def one_group(totals, inputs):
        queries, cotangent, chosen, used_now = inputs
        selected = window[chosen]
        keys_sel = selected[..., :head_cols].reshape(per_group, NNB, BLK, per_dev, E)
        values_sel = selected[..., head_cols:].reshape(per_group, NNB, BLK, per_dev, E)
        usable = jnp.arange(NNB)[None, :] < used_now[:, None]
        allowed = usable[:, None, None, :, None]
        scores = (
            jnp.einsum("rihe,rjthe->rhijt", queries, keys_sel, preferred_element_type=jnp.float32)
            * scale_factor
        )
        masked = jnp.where(allowed, scores, -1e30)
        highest = jnp.max(masked, axis=(3, 4), keepdims=True)
        raised = jnp.where(allowed, jnp.exp(masked - highest), 0.0)
        total = jnp.sum(raised, axis=(3, 4), keepdims=True)
        probability = raised / total
        weights = probability.astype(jnp.bfloat16)
        out_rows = jnp.einsum(
            "rhijt,rjthe->rihe", weights, values_sel, preferred_element_type=jnp.float32
        ).astype(jnp.bfloat16)
        dprob = jnp.einsum(
            "rihe,rjthe->rhijt", cotangent, values_sel, preferred_element_type=jnp.float32
        )
        row_delta = jnp.sum(probability * dprob, axis=(3, 4), keepdims=True)
        dscore = (probability * (dprob - row_delta) * scale_factor).astype(jnp.bfloat16)
        dquery = jnp.einsum(
            "rhijt,rjthe->rihe", dscore, keys_sel, preferred_element_type=jnp.float32
        ).astype(jnp.bfloat16)
        dkey_part = jnp.einsum(
            "rhijt,rihe->rjthe", dscore, queries, preferred_element_type=jnp.float32
        )
        dvalue_part = jnp.einsum(
            "rhijt,rihe->rjthe", weights, cotangent, preferred_element_type=jnp.float32
        )
        joined = jnp.concatenate(
            [
                dkey_part.reshape(per_group * NNB, BLK, head_cols),
                dvalue_part.reshape(per_group * NNB, BLK, head_cols),
            ],
            axis=-1,
        )
        totals = totals.at[chosen.reshape(-1)].add(joined)
        return (totals, (out_rows, dquery))

    start_grads = jnp.zeros((span_shards * blocks_shard, BLK, 2 * head_cols), jnp.float32)
    grads_window, results = lax.scan(one_group, start_grads, (query_g, grad_g, index_g, used_g))
    grads_window = grads_window.reshape(span_shards, shard_rows, 2 * head_cols)
    combined = grads_window[REACH]
    offsets_back = list(range(1, REACH + 1)) + [-offset for offset in range(1, REACH + 1)]
    for offset in offsets_back:
        combined = combined + passed_along(
            grads_window[REACH - offset].astype(jnp.bfloat16), "ctx", -offset
        ).astype(jnp.float32)
    combined = combined.astype(jnp.bfloat16)
    dkey_s = combined[:, :head_cols]
    dvalue_s = combined[:, head_cols:]
    out_s = results[0].reshape(shard_rows, head_cols)
    dquery_s = results[1].reshape(shard_rows, head_cols)
    back = (
        lax.all_to_all(
            out_s.reshape(shard_rows, 1, head_cols), "head", split_axis=0, concat_axis=1, tiled=True
        ),
        lax.all_to_all(
            dquery_s.reshape(shard_rows, 1, head_cols),
            "head",
            split_axis=0,
            concat_axis=1,
            tiled=True,
        ),
        lax.all_to_all(
            dkey_s.reshape(shard_rows, 1, head_cols),
            "head",
            split_axis=0,
            concat_axis=1,
            tiled=True,
        ),
        lax.all_to_all(
            dvalue_s.reshape(shard_rows, 1, head_cols),
            "head",
            split_axis=0,
            concat_axis=1,
            tiled=True,
        ),
    )
    width = groups * head_cols
    return (
        back[0].reshape(tok_rows, width),
        back[1].reshape(tok_rows, width),
        back[2].reshape(tok_rows, width),
        back[3].reshape(tok_rows, width),
    )


MESH_ID = pl.DeviceIdType.MESH
F32 = jnp.float32
BF16 = jnp.bfloat16
GROUP = 2
VMEM_BYTES = 20 * 1024 * 1024


def left_in_hbm(array):
    return pltpu.with_memory_space_constraint(array, pltpu.HBM)


def place_of():
    index = lax.axis_index("ctx") * lax.axis_size("head") + lax.axis_index("head")
    return lax.div(index, 2), lax.rem(index, 2)


def device_of(owner, side):
    n_head = lax.axis_size("head")
    index = 2 * owner + side
    return (lax.div(index, n_head), lax.rem(index, n_head))


def partners(pairs, owner, step):
    half = pairs // 2
    far = 1 - lax.div(step, half)
    base = lax.rem(lax.div(owner, half) + far, 2) * half
    low, turn = lax.rem(owner, half), lax.rem(step, half)
    return base + lax.rem(low + turn, half), base + lax.rem(low - turn + half, half)


def run_steps(start, stop, body):
    def one(step, carry):
        body(step)
        return carry

    lax.fori_loop(start, stop, one, 0)


def far_steps(pairs, body):
    run_steps(0, pairs // 2, body)


def near_steps(pairs, body):
    run_steps(pairs // 2 + 1, pairs, body)


def each_step(pairs, body):
    far_steps(pairs, body)
    near_steps(pairs, body)


def greet(pairs):
    owner, side = place_of()
    barrier = pltpu.get_barrier_semaphore()
    pl.semaphore_signal(barrier, inc=1, device_id=device_of(owner, 1 - side), device_id_type=MESH_ID)

    def one(step):
        to, _ = partners(pairs, owner, step)
        pl.semaphore_signal(barrier, inc=1, device_id=device_of(to, side), device_id_type=MESH_ID)

    each_step(pairs, one)
    return barrier


def spread_kernel(
    pairs, query, key, value, grad_out, neighbour_hbm, counts_hbm, qd, kv, kvt, sums_near, od_near,
    own_rows, send_qd, send_kv, neighbour, counts, pair_scr, x_scr,
    load, qd_out, qd_in, kv_out, kv_in, share_out, share_in,
):
    owner, side = place_of()
    half = pairs // 2
    near = lax.div(owner, half) * half
    loads = [
        pltpu.make_async_copy(array, own_rows.at[place], load.at[place])
        for place, array in enumerate((key, value, query, grad_out))
    ]
    names_copy = pltpu.make_async_copy(neighbour_hbm, neighbour, load.at[4])
    counts_copy = pltpu.make_async_copy(counts_hbm, counts, load.at[5])
    for copy in loads + [names_copy, counts_copy]:
        copy.start()
    barrier = greet(pairs)

    def pack(first, pieces):
        loads[first].wait()
        loads[first + 1].wait()
        for pair in range(pairs // 2):
            cols = slice(2 * E * pair, 2 * E * (pair + 1))
            a = own_rows[first, :, cols]
            b = own_rows[first + 1, :, cols]
            pieces[2 * pair] = jnp.concatenate([a[:, :E], b[:, :E]], axis=1)
            pieces[2 * pair + 1] = jnp.concatenate([a[:, E:], b[:, E:]], axis=1)

    def kv_copy(step, to, source):
        return pltpu.make_async_remote_copy(
            src_ref=send_kv.at[to],
            dst_ref=kv.at[2 * source + side],
            send_sem=kv_out.at[step],
            recv_sem=kv_in.at[step],
            device_id=device_of(to, side),
            device_id_type=MESH_ID,
        )

    def qd_copy(step, to, source):
        return pltpu.make_async_remote_copy(
            src_ref=send_qd.at[to],
            dst_ref=qd.at[source],
            send_sem=qd_out.at[step],
            recv_sem=qd_in.at[step],
            device_id=device_of(to, side),
            device_id_type=MESH_ID,
        )

    def share_copy(step, source, whose):
        return pltpu.make_async_remote_copy(
            src_ref=kv.at[2 * source + side],
            dst_ref=kv.at[2 * source + whose],
            send_sem=share_out.at[step],
            recv_sem=share_in.at[step],
            device_id=device_of(owner, 1 - side),
            device_id_type=MESH_ID,
        )

    def send_keys(step):
        to, _ = partners(pairs, owner, step)
        kv_copy(step, to, owner).start()

    def send_queries(step):
        to, _ = partners(pairs, owner, step)
        qd_copy(step, to, owner).start()

    pack(0, send_kv)
    pl.semaphore_wait(barrier, pairs)
    each_step(pairs, send_keys)
    pack(2, send_qd)
    near_steps(pairs, send_queries)
    mine = 2 * owner + side
    kv[mine] = send_kv[owner]
    qd[owner] = send_qd[owner]
    share_copy(half, owner, side).start()
    kvt[mine] = kv[mine].T

    def pass_on(step):
        _, source = partners(pairs, owner, step)
        kv_copy(step, owner, source).wait_recv()
        share_copy(step, source, side).start()
        kvt[2 * source + side] = kv[2 * source + side].T

    def pass_on_far(step):
        pass_on(step)
        to, _ = partners(pairs, owner, step)
        kv_copy(step, to, owner).wait_send()
        send_queries(step)

    def take_share(step):
        _, source = partners(pairs, owner, step)
        share_copy(step, source, side).wait_send()
        share_copy(step, source, 1 - side).wait_recv()
        kvt[2 * source + 1 - side] = kv[2 * source + 1 - side].T

    def take_near(step):
        to, source = partners(pairs, owner, step)
        qd_copy(step, owner, source).wait_recv()
        qd_copy(step, to, owner).wait_send()
        kv_copy(step, to, owner).wait_send()

    def take_far(step):
        to, source = partners(pairs, owner, step)
        qd_copy(step, owner, source).wait_recv()
        qd_copy(step, to, owner).wait_send()

    def near_group(turn, carry):
        group = range(GROUP)
        places = [GROUP * turn + one for one in group]
        blocks_now = [2 * (near + place) + side for place in places]
        names = [[neighbour[slot, block] for slot in range(NNB)] for block in blocks_now]
        valid = [
            [slot < counts[block] if slot > 0 else None for slot in range(NNB)]
            for block in blocks_now
        ]
        queries = [qd[near + place] for place in places]
        x_out = [x_scr.at[one] for one in group]
        spread, results = attend(group, NNB, names, valid, queries, kv, kvt, pair_scr, x_out)
        for one in group:
            od_near[places[one]] = results[one]
            grads = x_scr[one].reshape(NNB * BLK, 2 * BLK)
            added = jnp.dot(grads, spread[one], preferred_element_type=F32)
            sums_near[places[one]] = added.reshape(NNB, BLK, 2 * E)
        return carry

    far_steps(pairs, pass_on_far)
    near_steps(pairs, pass_on)
    take_share(jnp.int32(half))
    each_step(pairs, take_share)
    near_steps(pairs, take_near)
    names_copy.wait()
    counts_copy.wait()
    lax.fori_loop(0, half // GROUP, near_group, 0)
    far_steps(pairs, take_far)


def attend(group, used, names, valid, qd, kv, kvt, pair_scr, x_out):
    scale = 1.0 / math.sqrt(E)
    exp_scale = scale * math.log2(math.e)
    low = lax.broadcasted_iota(jnp.int32, (BLK, 2 * E), 1) < E
    top = lax.broadcasted_iota(jnp.int32, (2 * E, BLK), 0) < E

    def folded(array, op):
        return op(array.reshape(BLK // 8, 8, BLK), axis=0)

    spread, ahead = [], []
    for one in group:
        both = qd[one]
        zero = jnp.zeros_like(both)
        upper = jnp.where(low, both, zero)
        lower = jnp.where(low, zero, both)
        spread.append(jnp.concatenate([upper, lower], axis=0))
        ahead.append(jnp.concatenate([upper, lower * jnp.asarray(scale, BF16)], axis=0))
    highest = [None for _ in group]
    for one in group:
        keys = jnp.concatenate([kv[name] for name in names[one]], axis=0)
        result = lax.dot_general(
            keys, ahead[one], (((1,), (1,)), ((), ())), preferred_element_type=F32
        ).reshape(used, BLK, 2 * BLK)
        for slot in range(used):
            pair_scr[one, slot] = result[slot]
            part = folded(result[slot, :, :BLK], jnp.max)
            if valid[one][slot] is not None:
                part = jnp.where(valid[one][slot], part, -jnp.inf)
            highest[one] = part if slot == 0 else jnp.maximum(highest[one], part)
    highest = [jnp.max(part, axis=0, keepdims=True) for part in highest]
    total = [jnp.zeros((8, BLK), F32) for _ in group]
    delta = [jnp.zeros((8, BLK), F32) for _ in group]
    for slot in range(used):
        for one in group:
            raised = jnp.exp2((pair_scr[one, slot, :, :BLK] - highest[one]) * exp_scale)
            if valid[one][slot] is not None:
                raised = jnp.where(valid[one][slot], raised, 0.0)
            pair_scr[one, slot, :, :BLK] = raised
            total[one] = total[one] + folded(raised, jnp.sum)
            delta[one] = delta[one] + folded(raised * pair_scr[one, slot, :, BLK:], jnp.sum)
    inverse = [1.0 / jnp.sum(part, axis=0, keepdims=True) for part in total]
    delta = [jnp.sum(delta[one], axis=0, keepdims=True) * inverse[one] for one in group]
    for slot in range(used):
        for one in group:
            probability = pair_scr[one, slot, :, :BLK] * inverse[one]
            dscore = probability * (pair_scr[one, slot, :, BLK:] - delta[one])
            x_out[one][slot] = jnp.concatenate(
                [dscore.astype(BF16), probability.astype(BF16)], axis=1
            )
    results = []
    for one in group:
        rows = jnp.zeros((2 * E, 2 * BLK), F32)
        for slot in range(0, used, 2):
            if slot + 1 < used:
                keys_t = jnp.concatenate(
                    [kvt[names[one][slot]], kvt[names[one][slot + 1]]], axis=1
                )
                grads = jnp.concatenate([x_out[one][slot], x_out[one][slot + 1]], axis=0)
            else:
                keys_t = kvt[names[one][slot]]
                grads = x_out[one][slot]
            rows = rows + jnp.dot(keys_t, grads, preferred_element_type=F32)
        results.append(jnp.where(top, rows[:, :BLK], rows[:, BLK:]).T.astype(BF16))
    return spread, results


def attend_kernel(
    blocks, neighbour_hbm, counts_hbm, qd, kv, kvt, sums_near, od_far, totals,
    neighbour, counts, starts, order, pair_scr, x_scr, load
):
    owner, side = place_of()
    pairs = blocks // 2
    half = pairs // 2
    near = lax.div(owner, half) * half
    far = half - near
    names_copy = pltpu.make_async_copy(neighbour_hbm, neighbour, load.at[0])
    names_copy.start()
    counts_copy = pltpu.make_async_copy(counts_hbm, counts, load.at[1])
    counts_copy.start()

    def clear(block, carry):
        totals[block] = jnp.zeros((BLK, 2 * E), F32)
        return carry

    lax.fori_loop(0, blocks, clear, 0)
    names_copy.wait()
    counts_copy.wait()

    def used_of(place):
        return counts[2 * (far + place) + side]

    def sort_by_used():
        for used in range(NNB + 1):
            starts[used] = 0
        for place in range(half):
            used = used_of(place)
            starts[used - 1] = starts[used - 1] + 1
        for used in range(NNB - 1, -1, -1):
            starts[used] = starts[used] + starts[used + 1]
        for place in range(half):
            used = used_of(place)
            at = starts[used]
            order[at] = place
            starts[used] = at + 1

    def add_up(names, x_of_block, spread):
        used = len(names)
        grads = x_of_block[:used].reshape(used * BLK, 2 * BLK)
        added = jnp.dot(grads, spread, preferred_element_type=F32)
        for slot in range(used):
            totals[names[slot]] += added[slot * BLK : (slot + 1) * BLK]

    def rows_with(places, used):
        group = range(len(places))
        blocks_now = [2 * (far + place) + side for place in places]
        names = [[neighbour[slot, block] for slot in range(used)] for block in blocks_now]
        valid = [
            [slot < counts[block] if one > 0 and slot > 0 else None for slot in range(used)]
            for one, block in enumerate(blocks_now)
        ]
        x_out = [x_scr.at[one] for one in group]
        queries = [qd[far + place] for place in places]
        spread, results = attend(group, used, names, valid, queries, kv, kvt, pair_scr, x_out)
        for one in group:
            od_far[places[one]] = results[one]
            add_up(names[one], x_out[one], spread[one])

    def one_group(turn, carry):
        places = [order[GROUP * turn + one] for one in range(GROUP)]
        used_now = used_of(places[0])
        for used in range(1, NNB + 1):
            pl.when(used_now == used)(functools.partial(rows_with, places, used))
        return carry

    def near_sums(place, carry):
        block = 2 * (near + place) + side

        def one_slot(slot, carry):
            totals[neighbour[slot, block]] += sums_near[place, slot]
            return carry

        lax.fori_loop(0, counts[block], one_slot, 0)
        return carry

    sort_by_used()
    lax.fori_loop(0, half // GROUP, one_group, 0)
    lax.fori_loop(0, half, near_sums, 0)


def collect_kernel(
    pairs, od_near, od_far, totals, got_od, got_kv, other, shared, send_kv,
    od_out, od_in, kv_out, kv_in, share_out, share_in,
):
    owner, side = place_of()
    barrier = greet(pairs)

    def share_copy(step, place):
        return pltpu.make_async_remote_copy(
            src_ref=other.at[place],
            dst_ref=shared.at[place],
            send_sem=share_out.at[step],
            recv_sem=share_in.at[step],
            device_id=device_of(owner, 1 - side),
            device_id_type=MESH_ID,
        )

    def od_copy(array, step, to, source):
        return pltpu.make_async_remote_copy(
            src_ref=array.at[lax.rem(to, pairs // 2)],
            dst_ref=got_od.at[source],
            send_sem=od_out.at[step],
            recv_sem=od_in.at[step],
            device_id=device_of(to, side),
            device_id_type=MESH_ID,
        )

    def kv_copy(step, to, source):
        return pltpu.make_async_remote_copy(
            src_ref=send_kv.at[to],
            dst_ref=got_kv.at[source],
            send_sem=kv_out.at[step],
            recv_sem=kv_in.at[step],
            device_id=device_of(to, side),
            device_id_type=MESH_ID,
        )

    def narrow(place, carry):
        other[place] = totals[2 * place + 1 - side].astype(BF16)
        return carry

    lax.fori_loop(0, pairs, narrow, 0)
    pl.semaphore_wait(barrier, pairs)

    def start_share(step):
        to, _ = partners(pairs, owner, step)
        share_copy(step, to).start()

    def start_od(array, step):
        to, _ = partners(pairs, owner, step)
        od_copy(array, step, to, owner).start()

    def summed(place):
        return (totals[2 * place + side] + shared[place].astype(F32)).astype(BF16)

    def add_and_send(step):
        to, _ = partners(pairs, owner, step)
        share_copy(step, to).wait_recv()
        send_kv[to] = summed(to)
        kv_copy(step, to, owner).start()

    def finish(array, step):
        to, source = partners(pairs, owner, step)
        od_copy(array, step, owner, source).wait_recv()
        kv_copy(step, owner, source).wait_recv()
        od_copy(array, step, to, owner).wait_send()
        kv_copy(step, to, owner).wait_send()
        share_copy(step, to).wait_send()

    far_steps(pairs, start_share)
    far_steps(pairs, functools.partial(start_od, od_far))
    far_steps(pairs, add_and_send)
    near_steps(pairs, start_share)
    share_copy(pairs // 2, owner).start()
    near_steps(pairs, functools.partial(start_od, od_near))
    near_steps(pairs, add_and_send)
    share_copy(pairs // 2, owner).wait_recv()
    got_kv[owner] = summed(owner)
    got_od[owner] = od_near[lax.rem(owner, pairs // 2)]
    far_steps(pairs, functools.partial(finish, od_far))
    near_steps(pairs, functools.partial(finish, od_near))
    share_copy(pairs // 2, owner).wait_send()


def join_kernel(pairs, got_od, got_kv, out, dquery, dkey, dvalue, rows, store):
    copies = []
    for place, (pieces, part, array) in enumerate(
        ((got_od, 1, out), (got_od, 0, dquery), (got_kv, 0, dkey), (got_kv, 1, dvalue))
    ):
        cut = slice(part * E, (part + 1) * E)
        for pair in range(pairs // 2):
            cols = slice(2 * E * pair, 2 * E * (pair + 1))
            rows[place, :, cols] = jnp.concatenate(
                [pieces[2 * pair][:, cut], pieces[2 * pair + 1][:, cut]], axis=1
            )
        copies.append(pltpu.make_async_copy(rows.at[place], array, store.at[place]))
        copies[-1].start()
    for copy in copies:
        copy.wait()


def on_device_whole(query, key, value, grad_out, neighbour, counts):
    pairs = lax.axis_size("ctx") * lax.axis_size("head") // 2
    blocks = 2 * pairs
    width = query.shape[1]
    in_vmem = pl.BlockSpec(memory_space=pltpu.VMEM)
    in_hbm = pl.BlockSpec(memory_space=pltpu.HBM)
    many = pltpu.SemaphoreType.DMA((pairs,))
    piece = (BLK, 2 * E)
    own_pieces = jax.ShapeDtypeStruct((pairs, *piece), BF16)
    index_arrays = [
        pltpu.SMEM(neighbour.shape[::-1], jnp.int32),
        pltpu.SMEM(counts.shape, jnp.int32),
    ]
    with jax.named_scope("spread_heads"):
        qd, kv, kvt, sums_near, od_near = pl.pallas_call(
            functools.partial(spread_kernel, pairs),
            out_shape=(
                pltpu.VMEM((pairs, *piece), BF16),
                pltpu.VMEM((blocks, *piece), BF16),
                pltpu.VMEM((blocks, *piece), BF16),
                pltpu.VMEM((pairs // 2, NNB, BLK, 2 * E), F32),
                pltpu.VMEM((pairs // 2, *piece), BF16),
            ),
            in_specs=[in_hbm] * 6,
            out_specs=(in_vmem,) * 5,
            scratch_shapes=[pltpu.VMEM((4, BLK, width), BF16)]
            + [pltpu.VMEM((pairs, *piece), BF16)] * 2
            + index_arrays
            + [pltpu.VMEM((GROUP, NNB, BLK, 2 * BLK), kind) for kind in (F32, BF16)]
            + [pltpu.SemaphoreType.DMA((6,))]
            + [many] * 6,
            compiler_params=pltpu.CompilerParams(
                collective_id=0, has_side_effects=True, vmem_limit_bytes=VMEM_BYTES
            ),
        )(*map(left_in_hbm, (query, key, value, grad_out, neighbour.T, counts)))
    with jax.named_scope("block_attention"):
        od_far, totals = pl.pallas_call(
            functools.partial(attend_kernel, blocks),
            out_shape=(
                jax.ShapeDtypeStruct((pairs // 2, *piece), BF16),
                jax.ShapeDtypeStruct((blocks, *piece), F32),
            ),
            in_specs=[in_hbm] * 2 + [in_vmem] * 4,
            out_specs=(in_vmem,) * 2,
            scratch_shapes=[
                *index_arrays,
                pltpu.SMEM((NNB + 1,), jnp.int32),
                pltpu.SMEM((pairs // 2,), jnp.int32),
                pltpu.VMEM((GROUP, NNB, BLK, 2 * BLK), F32),
                pltpu.VMEM((GROUP, NNB, BLK, 2 * BLK), BF16),
                pltpu.SemaphoreType.DMA((2,)),
            ],
            compiler_params=pltpu.CompilerParams(vmem_limit_bytes=VMEM_BYTES),
        )(left_in_hbm(neighbour.T), left_in_hbm(counts), qd, kv, kvt, sums_near)
    with jax.named_scope("collect_heads"):
        got_od, got_kv = pl.pallas_call(
            functools.partial(collect_kernel, pairs),
            out_shape=(own_pieces,) * 2,
            in_specs=[in_vmem] * 3,
            out_specs=(in_vmem,) * 2,
            scratch_shapes=[pltpu.VMEM((pairs, *piece), BF16)] * 3 + [many] * 6,
            compiler_params=pltpu.CompilerParams(
                collective_id=1, has_side_effects=True, vmem_limit_bytes=VMEM_BYTES
            ),
        )(od_near, od_far, totals)
    with jax.named_scope("join_heads"):
        return pl.pallas_call(
            functools.partial(join_kernel, pairs),
            out_shape=(jax.ShapeDtypeStruct((BLK, width), BF16),) * 4,
            in_specs=[in_vmem] * 2,
            out_specs=(in_hbm,) * 4,
            scratch_shapes=[
                pltpu.VMEM((4, BLK, width), BF16),
                pltpu.SemaphoreType.DMA((4,)),
            ],
            compiler_params=pltpu.CompilerParams(vmem_limit_bytes=VMEM_BYTES),
        )(got_od, got_kv)


def on_device(query, key, value, grad_out, neighbour, counts):
    devices = lax.axis_size("ctx") * lax.axis_size("head")
    if devices == 2 * H and H % (2 * GROUP) == 0 and query.shape == (BLK, H * E) and counts.shape[0] == devices:
        return on_device_whole(query, key, value, grad_out, neighbour, counts)
    return on_device_windowed(query, key, value, grad_out, neighbour, counts)


def solution(mesh):
    return jax.shard_map(
        on_device,
        mesh=mesh,
        in_specs=(
            P(("ctx", "head"), None),
            P(("ctx", "head"), None),
            P(("ctx", "head"), None),
            P(("ctx", "head"), None),
            P(),
            P(),
        ),
        out_specs=(
            P(("ctx", "head"), None),
            P(("ctx", "head"), None),
            P(("ctx", "head"), None),
            P(("ctx", "head"), None),
        ),
        check_vma=False,
    )
```
